32 devices in a mesh: dp: 2 (over x), ctx: 16 (over z, y, core).
Axes of the slice: x: 2, y: 2, z: 4, core: 2. Of those that a mesh axis runs over, the one named last changes fastest.
Arguments:
- grad_out: bfloat16 [2, 2048, 2048], P('dp', 'ctx'), may hold values from -6 to 6
- saved_input: bfloat16 [2, 2048, 2048], P('dp', 'ctx'), may hold values from -6 to 6
- gate_value: bfloat16 [2, 2048, 2048], P('dp', 'ctx'), may hold values from -6 to 6
- filter_taps: bfloat16 [2048, 2048], P(None, 'ctx'), may hold values from -0.125 to 0.125
- skip_gain: float32 [2048], replicated, may hold values from 0.1 to 1.9
- lang_ids: int32 [2, 2048], P('dp', 'ctx'), may hold values from 0 to 15
- doc_ids: int32 [2, 2048], P('dp', 'ctx'), may hold values from 0 to 31, never falling along the last dimension, each value on 1 to 512 neighbouring positions
- dro_weight: float32 [16], replicated, may hold values from 0.25 to 4
Outputs:
- d_input: bfloat16 [2, 2048, 2048], P('dp', 'ctx')
- d_gate: bfloat16 [2, 2048, 2048], P('dp', 'ctx')
- d_filter: float32 [2048, 2048], P('ctx', 'dp')
The draws below stay inside these ranges and needn't reach their ends.
Inputs may be any that keep to these rules, and one draw needn't show every extreme that they name: `doc_ids`: in each sequence the document numbers never fall, and every number from 0 to 31 occurs.
All inputs are finite; a program needn't handle non-finite values.
Results may differ from the reference program's by a relative error of at most 0.017.
Values may be sent and summed in bfloat16 or wider, within the bound.
No kernel may reach another device: no remote copies, remote signals or barrier semaphores. Data moves between devices by JAX's collectives and lax.ppermute only.
A program may use at most 128 MiB of HBM per device.

```python
import math
import jax
import jax.numpy as jnp
import numpy as np
from jax import lax

C = 2048
T_DEV = 128
GROUPS = 16
NDOCS = 32
BATCH = 2
SEQ = 2048
N_CTX = 16


def plant(drawn, rng, low, high):
    place = [jax.random.randint(jax.random.fold_in(rng, axis), (), 0, length) for axis, length in enumerate(drawn.shape)]
    widest = drawn.shape.index(max(drawn.shape))
    beside = place[:widest] + [(place[widest] + 1) % drawn.shape[widest]] + place[widest + 1:]
    return drawn.at[tuple(place)].set(low).at[tuple(beside)].set(high)


def steps_of(own_key, shape, split, smallest, largest):
    factor_of = 1.0
    for axis_at, parts in split:
        steps = jax.random.uniform(jax.random.fold_in(jax.random.fold_in(own_key, 6), axis_at), (parts,), jnp.float32, smallest / len(split), largest / len(split))
        factor_of = factor_of * jnp.repeat(jnp.exp(steps), shape[axis_at] // parts).reshape((-1,) + (1,) * (len(shape) - 1 - axis_at))
    return factor_of


def split_up(count, total, limit, lean):
    weights = [(1 << 20) // math.isqrt(grade ** lean) + 1 for grade in range(2, count + 1)]
    rest, given = total - limit - (count - 1), [1] * (count - 1)
    while rest > 0:
        movable = [i for i in range(count - 1) if given[i] < limit]
        mass, budget = sum([weights[i] for i in movable]), rest
        for i in movable:
            addition = min(limit - given[i], max(1, budget * weights[i] // mass), rest)
            given[i] = given[i] + addition
            rest = rest - addition
    return np.array([limit] + given)


def uneven_parts(rng, amount, total, most, slope):
    if amount == 2:
        one = jax.random.randint(rng, (), max(1, total - most), min(most, total - 1) + 1)
        return jnp.stack([one, total - one])
    tallies = jnp.asarray(split_up(amount, total, most, slope), jnp.int32)
    couples = (amount - 1) // 2
    donor, sink = tallies[1:1 + 2 * couples:2], tallies[2:2 + 2 * couples:2]
    slack = jnp.minimum(donor - 1, most - sink)
    shifted = jax.random.randint(jax.random.fold_in(rng, 1), (couples,), 0, 1 << 20) % (slack + 1)
    tallies = tallies.at[1:1 + 2 * couples:2].set(donor - shifted).at[2:2 + 2 * couples:2].set(sink + shifted)
    return tallies[jax.random.permutation(jax.random.fold_in(rng, 2), amount)]


def gaussian(key, extent, deviation, most, shards=(), held_as=jnp.bfloat16):
    array = deviation * jax.random.normal(key, extent, jnp.float32)
    if shards:
        array = array * steps_of(key, extent, shards, -0.22, 0.18)
    return jnp.clip(array, -most, most).astype(held_as)


def setup_inputs(seed: int = 0) -> dict:
    key_of = jax.random.split(jax.random.key(seed), 9)
    return {
        "grad_out": gaussian(key_of[0], (BATCH, SEQ, C), 1.0, 6.0, ((0, 2), (1, 16))),
        "saved_input": gaussian(key_of[1], (BATCH, SEQ, C), 1.0, 6.0, ((0, 2), (1, 16))),
        "gate_value": gaussian(key_of[2], (BATCH, SEQ, C), 1.0, 6.0, ((0, 2), (1, 16))),
        "filter_taps": gaussian(key_of[3], (C, SEQ), (T_DEV * N_CTX) ** -0.5, 0.125, ((1, 16),)),
        "skip_gain": jnp.clip(1.0 + 0.18 * jax.random.normal(key_of[4], (C,), jnp.float32), 0.1, 1.9),
        "lang_ids": plant(jax.random.randint(key_of[5], (BATCH, SEQ), 0, GROUPS), jax.random.fold_in(key_of[5], 1), 0, GROUPS - 1).astype(jnp.int32),
        "doc_ids": jax.vmap(lambda own: jnp.searchsorted(jnp.cumsum(uneven_parts(own, NDOCS, SEQ, T_DEV * N_CTX // 4, 1)), jnp.arange(SEQ), side="right"))(jax.random.split(key_of[6], BATCH)).reshape((BATCH, SEQ)).astype(jnp.int32),
        "dro_weight": jnp.clip(jnp.exp(jax.random.uniform(key_of[7], (GROUPS,), jnp.float32, math.log(0.25), math.log(4.0))), 0.25, 4.0),
    }


def reference(grad_out, saved_input, gate_value, filter_taps, skip_gain, lang_ids, doc_ids, dro_weight):
    length = grad_out.shape[1]
    width = grad_out.shape[2]
    size = 2 * length
    lang_hot = lang_ids[..., None] == jnp.arange(GROUPS, dtype=jnp.int32)
    group_weight = jnp.sum(jnp.where(lang_hot, dro_weight, jnp.zeros_like(dro_weight)), axis=-1)
    doc_hot = (doc_ids[..., None] == jnp.arange(NDOCS, dtype=jnp.int32)).astype(jnp.float32)
    counts = jnp.sum(doc_hot, axis=1)
    doc_len = jnp.sum(doc_hot * counts[:, None, :], axis=-1)
    mean_len = length / NDOCS
    scale = group_weight * (2.0 * mean_len) / (doc_len + mean_len)
    grad_scaled = grad_out.astype(jnp.float32) * scale[..., None]
    grad_conv = (grad_scaled * gate_value.astype(jnp.float32)).astype(jnp.bfloat16)
    filt = jnp.fft.fft(filter_taps.astype(jnp.float32), n=size, axis=1)
    skip = skip_gain[:, None]

    def one(total, items):
        signal, grad = items
        sig = signal.astype(jnp.float32).T
        grd = grad.astype(jnp.float32).T
        sig_s = jnp.fft.fft(sig, n=size, axis=1)
        grd_s = jnp.fft.fft(grd, n=size, axis=1)
        mixed = (jnp.real(jnp.fft.ifft(filt * sig_s, axis=1))[:, :length] + skip * sig).astype(jnp.bfloat16)
        back = (jnp.real(jnp.fft.ifft(jnp.conj(filt) * grd_s, axis=1))[:, :length] + skip * grd).astype(jnp.bfloat16)
        lagged = jnp.real(jnp.fft.ifft(jnp.conj(sig_s) * grd_s, axis=1))[:, :length]
        return total + lagged, (mixed.T, back.T)

    total, outputs = lax.scan(one, jnp.zeros((width, length), jnp.float32), (saved_input, grad_conv))
    mixed_all, back_all = outputs
    d_gate = (grad_scaled * mixed_all.astype(jnp.float32)).astype(jnp.bfloat16)
    return back_all, d_gate, total
```

```python
import functools
import math

import jax
import jax.numpy as jnp
import numpy as np
from jax import lax
from jax.experimental import pallas as pl
from jax.experimental.pallas import tpu as pltpu
from jax.sharding import PartitionSpec as P

NDOCS = 32
ROWS = 16
VMEM = pl.BlockSpec(memory_space=pltpu.VMEM)
SMEM = pl.BlockSpec(memory_space=pltpu.SMEM)
f32 = jnp.float32
bf16 = jnp.bfloat16


def inner_tables(pieces, tokens):
    size = 2 * pieces * tokens
    m = np.arange(pieces)[:, None, None]
    k = np.arange(tokens)[None, :, None]
    q = np.arange(tokens)[None, None, :]
    turn = (q * (4 * m + 1 + 4 * pieces * k)) % (2 * size)
    angle = math.pi / size * turn
    cos, sin = np.cos(angle), np.sin(angle)
    ahead = np.concatenate(
        [np.concatenate([cos, sin], axis=2), np.concatenate([-sin, cos], axis=2)], axis=1
    )
    behind = np.swapaxes(ahead, 1, 2) * (2.0 / size)
    return jnp.asarray(ahead, bf16), jnp.asarray(behind, bf16)


def turned(value, turns):
    re, im = value
    turns = turns % 1.0
    if turns == 0.0:
        return value
    if turns == 0.25:
        return (-im, re)
    if turns == 0.5:
        return (-re, -im)
    if turns == 0.75:
        return (im, -re)
    cos, sin = math.cos(2.0 * math.pi * turns), math.sin(2.0 * math.pi * turns)
    if (turns * 8.0) % 1.0 == 0.0:
        root = math.sqrt(0.5)
        plus, minus = (re + im) * root, (re - im) * root
        if turns == 0.125:
            return (minus, plus)
        if turns == 0.375:
            return (-plus, minus)
        if turns == 0.625:
            return (-minus, -plus)
        return (plus, -minus)
    return (re * cos - im * sin, re * sin + im * cos)


def dft(values, sign):
    count = len(values)
    if count == 1:
        return values
    even, odd = dft(values[0::2], sign), dft(values[1::2], sign)
    first, second = [], []
    for k in range(count // 2):
        a, b = even[k], turned(odd[k], sign * k / count)
        first.append((a[0] + b[0], a[1] + b[1]))
        second.append((a[0] - b[0], a[1] - b[1]))
    return first + second


def outer_forward(reals):
    count = len(reals)
    values = [(reals[0], jnp.zeros_like(reals[0]))]
    for j in range(1, count):
        angle = -math.pi * j / (2 * count)
        values.append((reals[j] * math.cos(angle), reals[j] * math.sin(angle)))
    return dft(values, -1.0)


def outer_inverse(values):
    count = len(values)
    out = []
    for j, (re, im) in enumerate(dft(values, 1.0)):
        angle = math.pi * j / (2 * count)
        out.append(re if j == 0 else re * math.cos(angle) - im * math.sin(angle))
    return out


def chunked(total, body):
    def step(i, carry):
        body(pl.multiple_of(i * ROWS, ROWS))
        return carry

    lax.fori_loop(0, total // ROWS, step, 0)


def each_piece(pieces, body, group=4):
    def step(i, carry):
        for g in range(group):
            body(i * group + g)
        return carry

    lax.fori_loop(0, pieces // group, step, 0)


def dot(a, b):
    return lax.dot_general(a, b, (((1,), (0,)), ((), ())), preferred_element_type=f32)


def prep_kernel(pieces, span, grad_ref, gate_ref, doc_ref, lang_ref, out_ref):
    tokens = grad_ref.shape[0]
    split = tokens // span
    tile = lax.broadcasted_iota(jnp.int32, (ROWS, span), 0)
    rows = jnp.zeros((ROWS, span), f32)
    for a in range(split):
        part = slice(a * span, (a + 1) * span)
        rows = jnp.where(tile == a, doc_ref[:, part].astype(f32), rows)
        rows = jnp.where(tile == split + a, lang_ref[:, part].astype(f32), rows)
    rows = rows.astype(bf16)
    for i in range(pieces):
        part = slice(i * span, (i + 1) * span)
        out_ref[i, :tokens, :] = (
            grad_ref[:, part].astype(f32) * gate_ref[:, part].astype(f32)
        ).astype(bf16)
        out_ref[i, tokens:, :] = rows


def filter_kernel(taps_ref, ahead_ref, spec_ref, mid_ref):
    pieces, span, tokens = taps_ref.shape

    def outer(row):
        rows = pl.ds(row, ROWS)
        out = outer_forward([taps_ref[j, rows, :].astype(f32) for j in range(pieces)])
        for m, (re, im) in enumerate(out):
            mid_ref[m, rows, :tokens] = re.astype(bf16)
            mid_ref[m, rows, tokens:] = im.astype(bf16)

    chunked(span, outer)

    def inner(m):
        spec_ref[m] = lax.dot_general(
            ahead_ref[m], mid_ref[m], (((1,), (1,)), ((), ())), preferred_element_type=f32
        )

    each_piece(pieces, inner)


def to_middle(load, mid_ref, tokens, pieces):
    def outer(row):
        out = outer_forward([load(j, row) for j in range(pieces)])
        for m, (re, im) in enumerate(out):
            mid_ref[m, pl.ds(row, ROWS), :] = re.astype(bf16)
            mid_ref[m, pl.ds(tokens + row, ROWS), :] = im.astype(bf16)

    chunked(tokens, outer)


def from_middle(back_ref, store, tokens, pieces):
    def outer(row):
        out = outer_inverse(
            [
                (back_ref[m, pl.ds(row, ROWS), :], back_ref[m, pl.ds(tokens + row, ROWS), :])
                for m in range(pieces)
            ]
        )
        for j in range(pieces):
            store(j, row, out[j])

    chunked(tokens, outer)


def mixed_kernel(
    in_ref, filt_ref, skip_ref, ahead_ref, behind_ref, out_ref, spec_ref, mid_ref, back_ref
):
    pieces, tokens, _ = in_ref.shape

    def load(j, row):
        return in_ref[j, pl.ds(row, ROWS), :].astype(f32)

    to_middle(load, mid_ref, tokens, pieces)

    def inner(m):
        spec = dot(ahead_ref[m], mid_ref[m])
        spec_ref[m] = spec
        filt = filt_ref[m]
        re, im = spec[:tokens], spec[tokens:]
        fre, fim = filt[:tokens], filt[tokens:]
        prod = jnp.concatenate([fre * re - fim * im, fre * im + fim * re], axis=0).astype(bf16)
        back_ref[m] = dot(behind_ref[m], prod)

    each_piece(pieces, inner)
    skip = skip_ref[...]

    def store(j, row, value):
        out_ref[j, pl.ds(row, ROWS), :] = (value + skip * load(j, row)).astype(bf16)

    from_middle(back_ref, store, tokens, pieces)


def input_kernel(
    mean_len,
    grad_ref,
    filt_ref,
    skip_ref,
    dro_ref,
    ahead_ref,
    behind_ref,
    out_ref,
    spec_ref,
    scale_ref,
    mid_ref,
    back_ref,
    doc_ref,
    lang_ref,
):
    pieces, tall, span = grad_ref.shape
    tokens = tall - ROWS
    split = tokens // span
    for j in range(pieces):
        rows = grad_ref[j, tokens:, :].astype(f32)
        for a in range(split):
            doc_ref[a, j : j + 1, :] = rows[a : a + 1]
            lang_ref[a, j : j + 1, :] = rows[split + a : split + a + 1]
    docs, langs = doc_ref[...], lang_ref[...]
    doc_len = jnp.zeros_like(docs)
    for d in range(NDOCS):
        hot = (docs == float(d)).astype(f32)
        count = jnp.sum(jnp.sum(hot, axis=0), axis=(0, 1), keepdims=True)
        doc_len = doc_len + hot * count[None]
    weight = jnp.zeros_like(langs)
    for g in range(dro_ref.shape[0]):
        weight = jnp.where(langs == float(g), dro_ref[g], weight)
    scale = weight * (2.0 * mean_len) / (doc_len + mean_len)
    for a in range(split):
        scale_ref[a * span : (a + 1) * span, :] = scale[a].T

    def load(j, row):
        rows = pl.ds(row, ROWS)
        return grad_ref[j, rows, :].astype(f32) * scale_ref[rows, j : j + 1]

    to_middle(load, mid_ref, tokens, pieces)

    def inner(m):
        spec = dot(ahead_ref[m], mid_ref[m])
        spec_ref[m] = spec
        filt = filt_ref[m]
        re, im = spec[:tokens], spec[tokens:]
        fre, fim = filt[:tokens], filt[tokens:]
        prod = jnp.concatenate([fre * re + fim * im, fre * im - fim * re], axis=0).astype(bf16)
        back_ref[m] = dot(behind_ref[m], prod)

    each_piece(pieces, inner)
    skip = skip_ref[...]

    def store(j, row, value):
        out_ref[j, pl.ds(row, ROWS), :] = (value + skip * load(j, row)).astype(bf16)

    from_middle(back_ref, store, tokens, pieces)


def lags_kernel(in_ref, grad_ref, behind_ref, out_ref, back_ref, lag_ref):
    pieces, tall, span = in_ref.shape
    tokens = tall // 2
    held = out_ref.shape[2] // tokens

    def inner(m):
        x, g = in_ref[m], grad_ref[m]
        xre, xim, gre, gim = x[:tokens], x[tokens:], g[:tokens], g[tokens:]
        prod = jnp.concatenate([xre * gre + xim * gim, xre * gim - xim * gre], axis=0)
        back_ref[m] = dot(behind_ref[m], prod.astype(bf16))

    each_piece(pieces, inner)

    def store(j, row, value):
        lag_ref[j, pl.ds(row, ROWS), :] = value

    from_middle(back_ref, store, tokens, pieces)
    for j in range(pieces):
        place = (j % held) * tokens
        out_ref[j // held, :, place : place + tokens] = lag_ref[j].T.astype(bf16)


def gate_kernel(own_ref, grad_ref, scale_ref, mixed_ref, out_ref):
    pieces, tokens, span = mixed_ref.shape
    lane = lax.broadcasted_iota(jnp.int32, (tokens, pieces), 1)
    scale = jnp.sum(
        jnp.where(lane == own_ref[0], scale_ref[...], jnp.zeros((tokens, pieces), f32)),
        axis=1,
        keepdims=True,
    )
    for i in range(pieces):
        part = slice(i * span, (i + 1) * span)
        out_ref[:, part] = (
            grad_ref[:, part].astype(f32) * scale * mixed_ref[i].astype(f32)
        ).astype(bf16)


def call(kernel, out, ins, scratch=(), limit=24, cost=(0, 0)):
    return pl.pallas_call(
        kernel,
        out_shape=out,
        in_specs=ins,
        out_specs=jax.tree.map(lambda _: VMEM, out),
        scratch_shapes=scratch,
        compiler_params=pltpu.CompilerParams(vmem_limit_bytes=limit << 20),
        cost_estimate=pl.CostEstimate(flops=cost[0], bytes_accessed=cost[1], transcendentals=0),
    )


def local(grad_out, saved_input, gate_value, filter_taps, skip_gain, lang_ids, doc_ids, dro_weight):
    tokens = grad_out.shape[1]
    channels = grad_out.shape[2]
    pieces = lax.axis_size("ctx")
    members = lax.axis_size("dp")
    length = tokens * pieces
    span = channels // pieces
    mean_len = length / NDOCS
    own = lax.axis_index("ctx")
    ahead, behind = inner_tables(pieces, tokens)
    skip = lax.dynamic_slice_in_dim(skip_gain, own * span, span)[None, :]
    exchange = functools.partial(
        lax.all_to_all, axis_name="ctx", split_axis=0, concat_axis=0, tiled=True
    )
    block = jax.ShapeDtypeStruct((pieces, tokens, span), bf16)
    spectrum = jax.ShapeDtypeStruct((pieces, 2 * tokens, span), f32)
    middle = pltpu.VMEM((pieces, 2 * tokens, span), bf16)
    turned_back = pltpu.VMEM((pieces, 2 * tokens, span), f32)
    macs = pieces * (2 * tokens) ** 2 * span

    taps = exchange(filter_taps.reshape(pieces, span, tokens))
    inputs = exchange(saved_input[0].reshape(tokens, pieces, span).transpose(1, 0, 2))
    grads = call(
        functools.partial(prep_kernel, pieces, span),
        jax.ShapeDtypeStruct((pieces, tokens + ROWS, span), bf16),
        [VMEM] * 4,
        cost=(0, 4 << 20),
    )(grad_out[0], gate_value[0], doc_ids, lang_ids)
    grads = exchange(grads)
    filt = call(
        filter_kernel,
        spectrum,
        [VMEM] * 2,
        [pltpu.VMEM((pieces, span, 2 * tokens), bf16)],
        cost=(2 * macs, 4 << 20),
    )(taps, ahead)
    mixed, input_spec = call(
        mixed_kernel,
        (block, spectrum),
        [VMEM] * 5,
        [middle, turned_back],
        cost=(4 * macs, 8 << 20),
    )(inputs, filt, skip, ahead, behind)
    mixed = exchange(mixed)
    back, grad_spec, scale = call(
        functools.partial(input_kernel, mean_len),
        (block, spectrum, jax.ShapeDtypeStruct((tokens, pieces), f32)),
        [VMEM, VMEM, VMEM, SMEM, VMEM, VMEM],
        [
            middle,
            turned_back,
            pltpu.VMEM((tokens // span, pieces, span), f32),
            pltpu.VMEM((tokens // span, pieces, span), f32),
        ],
        cost=(4 * macs, 8 << 20),
    )(grads, filt, skip, dro_weight, ahead, behind)
    back = exchange(back)
    lagged = call(
        lags_kernel,
        jax.ShapeDtypeStruct((members, span, length // members), bf16),
        [VMEM] * 3,
        [turned_back, pltpu.VMEM((pieces, tokens, span), f32)],
        cost=(2 * macs, 6 << 20),
    )(input_spec, grad_spec, behind)
    lagged = lax.all_to_all(lagged, "dp", split_axis=0, concat_axis=0, tiled=True)
    d_gate = call(
        gate_kernel,
        jax.ShapeDtypeStruct((tokens, channels), bf16),
        [SMEM, VMEM, VMEM, VMEM],
        cost=(0, 4 << 20),
    )(own.reshape(1), grad_out[0], scale, mixed)
    d_input = back.transpose(1, 0, 2).reshape(tokens, channels)
    d_filter = jnp.sum(lagged.astype(f32), axis=0)
    return (d_input[None], d_gate[None], d_filter)


def solution(mesh):
    return jax.shard_map(
        local,
        mesh=mesh,
        in_specs=(
            P("dp", "ctx", None),
            P("dp", "ctx", None),
            P("dp", "ctx", None),
            P(None, "ctx"),
            P(),
            P("dp", "ctx"),
            P("dp", "ctx"),
            P(),
        ),
        out_specs=(P("dp", "ctx", None), P("dp", "ctx", None), P("ctx", "dp")),
        check_vma=False,
    )
```

```python
import functools
import math

import jax
import jax.numpy as jnp
import numpy as np
from jax import lax
from jax.experimental import pallas as pl
from jax.experimental.pallas import tpu as pltpu
from jax.sharding import PartitionSpec as P

NDOCS = 32
ROWS = 16
VMEM = pl.BlockSpec(memory_space=pltpu.VMEM)
SMEM = pl.BlockSpec(memory_space=pltpu.SMEM)
f32 = jnp.float32
bf16 = jnp.bfloat16


def inner_tables(pieces, tokens):
    size = 2 * pieces * tokens
    m = np.arange(pieces)[:, None, None]
    k = np.arange(tokens)[None, :, None]
    q = np.arange(tokens)[None, None, :]
    turn = (q * (4 * m + 1 + 4 * pieces * k)) % (2 * size)
    angle = math.pi / size * turn
    cos, sin = np.cos(angle), np.sin(angle)
    ahead = np.concatenate(
        [np.concatenate([cos, sin], axis=2), np.concatenate([-sin, cos], axis=2)], axis=1
    )
    behind = np.swapaxes(ahead, 1, 2) * (2.0 / size)
    return jnp.asarray(ahead, bf16), jnp.asarray(behind, bf16)


def turned(value, turns):
    re, im = value
    turns = turns % 1.0
    if turns == 0.0:
        return value
    if turns == 0.25:
        return (-im, re)
    if turns == 0.5:
        return (-re, -im)
    if turns == 0.75:
        return (im, -re)
    cos, sin = math.cos(2.0 * math.pi * turns), math.sin(2.0 * math.pi * turns)
    if (turns * 8.0) % 1.0 == 0.0:
        root = math.sqrt(0.5)
        plus, minus = (re + im) * root, (re - im) * root
        if turns == 0.125:
            return (minus, plus)
        if turns == 0.375:
            return (-plus, minus)
        if turns == 0.625:
            return (-minus, -plus)
        return (plus, -minus)
    return (re * cos - im * sin, re * sin + im * cos)


def dft(values, sign):
    count = len(values)
    if count == 1:
        return values
    even, odd = dft(values[0::2], sign), dft(values[1::2], sign)
    first, second = [], []
    for k in range(count // 2):
        a, b = even[k], turned(odd[k], sign * k / count)
        first.append((a[0] + b[0], a[1] + b[1]))
        second.append((a[0] - b[0], a[1] - b[1]))
    return first + second


def outer_forward(reals):
    count = len(reals)
    values = [(reals[0], jnp.zeros_like(reals[0]))]
    for j in range(1, count):
        angle = -math.pi * j / (2 * count)
        values.append((reals[j] * math.cos(angle), reals[j] * math.sin(angle)))
    return dft(values, -1.0)


def outer_inverse(values):
    count = len(values)
    out = []
    for j, (re, im) in enumerate(dft(values, 1.0)):
        angle = math.pi * j / (2 * count)
        out.append(re if j == 0 else re * math.cos(angle) - im * math.sin(angle))
    return out


def chunked(total, body):
    def step(i, carry):
        body(pl.multiple_of(i * ROWS, ROWS))
        return carry

    lax.fori_loop(0, total // ROWS, step, 0)


def each_piece(pieces, body, group=4):
    def step(i, carry):
        for g in range(group):
            body(i * group + g)
        return carry

    lax.fori_loop(0, pieces // group, step, 0)


def dot(a, b):
    return lax.dot_general(a, b, (((1,), (0,)), ((), ())), preferred_element_type=f32)


def places(pieces, tokens, span):
    beside = max(1, tokens // span)

    def place(index, start):
        row = start + (index // beside) * tokens
        column = (index % beside) * span
        return row, slice(column, column + span)

    tall = -(-2 // beside) * tokens
    return place, tall


def prep_kernel(pieces, span, input_ref, grad_ref, gate_ref, taps_ref, doc_ref, lang_ref, out_ref):
    tokens = grad_ref.shape[0]
    place, tall = places(pieces, tokens, span)
    tile = lax.broadcasted_iota(jnp.int32, (ROWS, tokens), 0)
    ids = jnp.where(tile == 0, doc_ref[...], lang_ref[...]).astype(f32).astype(bf16)
    in_row, in_lanes = place(0, span)
    grad_row, grad_lanes = place(1, span)
    for i in range(pieces):
        part = slice(i * span, (i + 1) * span)
        out_ref[i, :span, :] = taps_ref[part, :]
        out_ref[i, in_row : in_row + tokens, in_lanes] = input_ref[:, part]
        out_ref[i, grad_row : grad_row + tokens, grad_lanes] = (
            grad_ref[:, part].astype(f32) * gate_ref[:, part].astype(f32)
        ).astype(bf16)
        out_ref[i, span + tall :, :] = ids


def token_scale(message_ref, scale_ref, dro_ref, ids, mean_len, doc_ref, lang_ref):
    for j in range(message_ref.shape[0]):
        rows = message_ref[j, ids:, :].astype(f32)
        doc_ref[j : j + 1, :] = rows[0:1]
        lang_ref[j : j + 1, :] = rows[1:2]
    docs, langs = doc_ref[...], lang_ref[...]
    doc_len = jnp.zeros_like(docs)
    for d in range(NDOCS):
        hot = (docs == float(d)).astype(f32)
        doc_len = doc_len + hot * jnp.sum(hot, axis=(0, 1), keepdims=True)
    weight = jnp.zeros_like(langs)
    for g in range(dro_ref.shape[0]):
        weight = jnp.where(langs == float(g), dro_ref[g], weight)
    scale_ref[...] = (weight * (2.0 * mean_len) / (doc_len + mean_len)).T


def conv_kernel(
    mean_len,
    message_ref,
    skip_ref,
    dro_ref,
    ahead_ref,
    behind_ref,
    out_ref,
    cross_ref,
    scale_ref,
    taps_mid_ref,
    mid_ref,
    back_ref,
    doc_ref,
    lang_ref,
):
    pieces = message_ref.shape[0]
    tokens = message_ref.shape[2]
    span = skip_ref.shape[1]
    place, tall = places(pieces, tokens, span)
    token_scale(message_ref, scale_ref, dro_ref, span + tall, mean_len, doc_ref, lang_ref)

    def outer_taps(row):
        rows = pl.ds(row, ROWS)
        out = outer_forward([message_ref[j, rows, :].astype(f32) for j in range(pieces)])
        for m, (re, im) in enumerate(out):
            taps_mid_ref[m, rows, :tokens] = re.astype(bf16)
            taps_mid_ref[m, rows, tokens:] = im.astype(bf16)

    chunked(span, outer_taps)

    def load(side, j, row):
        start, lanes = place(side, span)
        value = message_ref[j, pl.ds(start + row, ROWS), lanes].astype(f32)
        return value * scale_ref[pl.ds(row, ROWS), j : j + 1] if side else value

    sides = (slice(0, span), slice(span, 2 * span))

    def outer(side):
        def body(row):
            out = outer_forward([load(side, j, row) for j in range(pieces)])
            for m, (re, im) in enumerate(out):
                mid_ref[m, pl.ds(row, ROWS), sides[side]] = re.astype(bf16)
                mid_ref[m, pl.ds(tokens + row, ROWS), sides[side]] = im.astype(bf16)

        chunked(tokens, body)

    outer(0)
    outer(1)

    def inner(m):
        filt = lax.dot_general(
            ahead_ref[m], taps_mid_ref[m], (((1,), (1,)), ((), ())), preferred_element_type=f32
        )
        spec = dot(ahead_ref[m], mid_ref[m])
        fre, fim = filt[:tokens], filt[tokens:]
        xre, xim = spec[:tokens, sides[0]], spec[tokens:, sides[0]]
        gre, gim = spec[:tokens, sides[1]], spec[tokens:, sides[1]]
        cross_ref[m, :tokens, :] = (xre * gre + xim * gim).astype(bf16)
        cross_ref[m, tokens:, :] = (xre * gim - xim * gre).astype(bf16)
        mixed = jnp.concatenate([fre * xre - fim * xim, fre * xim + fim * xre], axis=0)
        back = jnp.concatenate([fre * gre + fim * gim, fre * gim - fim * gre], axis=0)
        both = jnp.concatenate([mixed.astype(bf16), back.astype(bf16)], axis=1)
        back_ref[m] = dot(behind_ref[m], both)

    each_piece(pieces, inner)
    skip = skip_ref[...]

    def outer_back(side):
        start, lanes = place(side, 0)

        def body(row):
            out = outer_inverse(
                [
                    (
                        back_ref[m, pl.ds(row, ROWS), sides[side]],
                        back_ref[m, pl.ds(tokens + row, ROWS), sides[side]],
                    )
                    for m in range(pieces)
                ]
            )
            for j in range(pieces):
                out_ref[j, pl.ds(start + row, ROWS), lanes] = (
                    out[j] + skip * load(side, j, row)
                ).astype(bf16)

        chunked(tokens, body)

    outer_back(0)
    outer_back(1)


def lags_kernel(own_ref, cross_ref, behind_ref, keep_ref, send_ref, back_ref, lag_ref):
    pieces, tall, span = cross_ref.shape
    tokens = tall // 2
    held = keep_ref.shape[1] // tokens
    members = pieces // held

    def inner(m):
        back_ref[m] = dot(behind_ref[m], cross_ref[m])

    each_piece(pieces, inner)

    def body(row):
        out = outer_inverse(
            [
                (back_ref[m, pl.ds(row, ROWS), :], back_ref[m, pl.ds(tokens + row, ROWS), :])
                for m in range(pieces)
            ]
        )
        for j in range(pieces):
            lag_ref[j, pl.ds(row, ROWS), :] = out[j]

    chunked(tokens, body)
    for j in range(held):
        part = slice(j * tokens, (j + 1) * tokens)
        keep_ref[:, part] = lag_ref[own_ref[0] * held + j].T
        for r in range(1, members):
            other = lax.rem(own_ref[0] + r, members)
            send_ref[r - 1, :, part] = lag_ref[other * held + j].T.astype(bf16)


def final_kernel(own_ref, grad_ref, scale_ref, message_ref, gate_ref, input_ref):
    pieces = message_ref.shape[0]
    tokens, channels = grad_ref.shape
    span = channels // pieces
    place, _ = places(pieces, tokens, span)
    lane = lax.broadcasted_iota(jnp.int32, (tokens, pieces), 1)
    scale = jnp.sum(
        jnp.where(lane == own_ref[0], scale_ref[...], jnp.zeros((tokens, pieces), f32)),
        axis=1,
        keepdims=True,
    )
    mixed_row, mixed_lanes = place(0, 0)
    back_row, back_lanes = place(1, 0)
    for i in range(pieces):
        part = slice(i * span, (i + 1) * span)
        mixed = message_ref[i, mixed_row : mixed_row + tokens, mixed_lanes].astype(f32)
        gate_ref[:, part] = (grad_ref[:, part].astype(f32) * scale * mixed).astype(bf16)
        input_ref[:, part] = message_ref[i, back_row : back_row + tokens, back_lanes]


def call(kernel, out, ins, scratch=(), limit=24, cost=(0, 0)):
    return pl.pallas_call(
        kernel,
        out_shape=out,
        in_specs=ins,
        out_specs=jax.tree.map(lambda _: VMEM, out),
        scratch_shapes=scratch,
        compiler_params=pltpu.CompilerParams(vmem_limit_bytes=limit << 20),
        cost_estimate=pl.CostEstimate(flops=cost[0], bytes_accessed=cost[1], transcendentals=0),
    )


def local(grad_out, saved_input, gate_value, filter_taps, skip_gain, lang_ids, doc_ids, dro_weight):
    tokens = grad_out.shape[1]
    channels = grad_out.shape[2]
    pieces = lax.axis_size("ctx")
    members = lax.axis_size("dp")
    length = tokens * pieces
    span = channels // pieces
    mean_len = length / NDOCS
    own = lax.axis_index("ctx")
    ahead, behind = inner_tables(pieces, tokens)
    skip = lax.dynamic_slice_in_dim(skip_gain, own * span, span)[None, :]
    exchange = functools.partial(
        lax.all_to_all, axis_name="ctx", split_axis=0, concat_axis=0, tiled=True
    )
    tall = places(pieces, tokens, span)[1]
    macs = pieces * (2 * tokens) ** 2 * span

    message = call(
        functools.partial(prep_kernel, pieces, span),
        jax.ShapeDtypeStruct((pieces, span + tall + ROWS, tokens), bf16),
        [VMEM] * 6,
        cost=(0, 4 << 20),
    )(saved_input[0], grad_out[0], gate_value[0], filter_taps, doc_ids, lang_ids)
    message = exchange(message)
    message, cross, scale = call(
        functools.partial(conv_kernel, mean_len),
        (
            jax.ShapeDtypeStruct((pieces, tall, tokens), bf16),
            jax.ShapeDtypeStruct((pieces, 2 * tokens, span), bf16),
            jax.ShapeDtypeStruct((tokens, pieces), f32),
        ),
        [VMEM, VMEM, SMEM, VMEM, VMEM],
        [
            pltpu.VMEM((pieces, span, 2 * tokens), bf16),
            pltpu.VMEM((pieces, 2 * tokens, 2 * span), bf16),
            pltpu.VMEM((pieces, 2 * tokens, 2 * span), f32),
            pltpu.VMEM((pieces, tokens), f32),
            pltpu.VMEM((pieces, tokens), f32),
        ],
        cost=(10 * macs, 8 << 20),
    )(message, skip, dro_weight, ahead, behind)
    message = exchange(message)
    keep, send = call(
        lags_kernel,
        (
            jax.ShapeDtypeStruct((span, length // members), f32),
            jax.ShapeDtypeStruct((members - 1, span, length // members), bf16),
        ),
        [SMEM, VMEM, VMEM],
        [
            pltpu.VMEM((pieces, 2 * tokens, span), f32),
            pltpu.VMEM((pieces, tokens, span), f32),
        ],
        cost=(2 * macs, 6 << 20),
    )(lax.axis_index("dp").reshape(1), cross, behind)
    d_filter = keep
    for r in range(1, members):
        ring = [(d, (d + r) % members) for d in range(members)]
        d_filter = d_filter + lax.ppermute(send[r - 1], "dp", ring).astype(f32)
    token_block = jax.ShapeDtypeStruct((tokens, channels), bf16)
    d_gate, d_input = call(
        final_kernel,
        (token_block, token_block),
        [SMEM, VMEM, VMEM, VMEM],
        cost=(0, 4 << 20),
    )(own.reshape(1), grad_out[0], scale, message)
    return (d_input[None], d_gate[None], d_filter)


def solution(mesh):
    return jax.shard_map(
        local,
        mesh=mesh,
        in_specs=(
            P("dp", "ctx", None),
            P("dp", "ctx", None),
            P("dp", "ctx", None),
            P(None, "ctx"),
            P(),
            P("dp", "ctx"),
            P("dp", "ctx"),
            P(),
        ),
        out_specs=(P("dp", "ctx", None), P("dp", "ctx", None), P("ctx", "dp")),
        check_vma=False,
    )
```

```python
import functools
import math

import jax
import jax.numpy as jnp
import numpy as np
from jax import lax
from jax.experimental import pallas as pl
from jax.experimental.pallas import tpu as pltpu
from jax.sharding import PartitionSpec as P

NDOCS = 32
ROWS = 16
VMEM = pl.BlockSpec(memory_space=pltpu.VMEM)
SMEM = pl.BlockSpec(memory_space=pltpu.SMEM)
f32 = jnp.float32
bf16 = jnp.bfloat16


def inner_tables(pieces, tokens):
    size = 2 * pieces * tokens
    m = np.arange(pieces)[:, None, None]
    k = np.arange(tokens)[None, :, None]
    q = np.arange(tokens)[None, None, :]
    turn = (q * (4 * m + 1 + 4 * pieces * k)) % (2 * size)
    angle = math.pi / size * turn
    cos, sin = np.cos(angle), np.sin(angle)
    ahead = np.concatenate(
        [np.concatenate([cos, sin], axis=2), np.concatenate([-sin, cos], axis=2)], axis=1
    )
    behind = np.swapaxes(ahead, 1, 2) * (2.0 / size)
    return jnp.asarray(ahead, bf16), jnp.asarray(behind, bf16)


def turned(value, turns):
    re, im = value
    turns = turns % 1.0
    if turns == 0.0:
        return value
    if turns == 0.25:
        return (-im, re)
    if turns == 0.5:
        return (-re, -im)
    if turns == 0.75:
        return (im, -re)
    cos, sin = math.cos(2.0 * math.pi * turns), math.sin(2.0 * math.pi * turns)
    if (turns * 8.0) % 1.0 == 0.0:
        root = math.sqrt(0.5)
        plus, minus = (re + im) * root, (re - im) * root
        if turns == 0.125:
            return (minus, plus)
        if turns == 0.375:
            return (-plus, minus)
        if turns == 0.625:
            return (-minus, -plus)
        return (plus, -minus)
    return (re * cos - im * sin, re * sin + im * cos)


def dft(values, sign):
    count = len(values)
    if count == 1:
        return values
    even, odd = dft(values[0::2], sign), dft(values[1::2], sign)
    first, second = [], []
    for k in range(count // 2):
        a, b = even[k], turned(odd[k], sign * k / count)
        first.append((a[0] + b[0], a[1] + b[1]))
        second.append((a[0] - b[0], a[1] - b[1]))
    return first + second


def outer_forward(reals):
    count = len(reals)
    values = [(reals[0], jnp.zeros_like(reals[0]))]
    for j in range(1, count):
        angle = -math.pi * j / (2 * count)
        values.append((reals[j] * math.cos(angle), reals[j] * math.sin(angle)))
    return dft(values, -1.0)


def outer_inverse(values):
    count = len(values)
    out = []
    for j, (re, im) in enumerate(dft(values, 1.0)):
        angle = math.pi * j / (2 * count)
        out.append(re if j == 0 else re * math.cos(angle) - im * math.sin(angle))
    return out


def chunked(total, body):
    def step(i, carry):
        body(pl.multiple_of(i * ROWS, ROWS))
        return carry

    lax.fori_loop(0, total // ROWS, step, 0)


def each_piece(pieces, body, group=4):
    def step(i, carry):
        for g in range(group):
            body(i * group + g)
        return carry

    lax.fori_loop(0, pieces // group, step, 0)


def dot(a, b):
    return lax.dot_general(a, b, (((1,), (0,)), ((), ())), preferred_element_type=f32)


def relative(own_ref, r, count):
    return lax.rem(own_ref[0] + r, count)


def gathered(own_ref, chunk_refs, held_ref):
    count = len(chunk_refs)
    for r, ref in enumerate(chunk_refs):
        held_ref[relative(own_ref, count - r, count)] = ref[...]


def scattered(own_ref, held_ref, chunk_refs):
    count = len(chunk_refs)
    for r, ref in enumerate(chunk_refs):
        ref[...] = held_ref[relative(own_ref, r, count)]


def taps_out_kernel(pieces, span, own_ref, taps_ref, doc_ref, lang_ref, *out_refs):
    tile = lax.broadcasted_iota(jnp.int32, (ROWS, taps_ref.shape[1]), 0)
    ids = jnp.where(tile == 0, doc_ref[...], lang_ref[...]).astype(f32).astype(bf16)
    for r, ref in enumerate(out_refs):
        start = pl.multiple_of(relative(own_ref, r, pieces) * span, ROWS)
        ref[:span, :] = taps_ref[pl.ds(start, span), :]
        ref[span:, :] = ids


def input_out_kernel(pieces, span, own_ref, input_ref, *refs):
    held_ref = refs[pieces]
    for i in range(pieces):
        held_ref[i] = input_ref[:, i * span : (i + 1) * span]
    scattered(own_ref, held_ref, refs[:pieces])


def grad_out_kernel(pieces, span, own_ref, grad_ref, gate_ref, *refs):
    held_ref = refs[pieces]
    for i in range(pieces):
        part = slice(i * span, (i + 1) * span)
        held_ref[i] = (grad_ref[:, part].astype(f32) * gate_ref[:, part].astype(f32)).astype(bf16)
    scattered(own_ref, held_ref, refs[:pieces])


def token_scale(doc_ref, lang_ref, dro_ref, mean_len, scale_ref):
    docs, langs = doc_ref[...], lang_ref[...]
    doc_len = jnp.zeros_like(docs)
    for d in range(NDOCS):
        hot = (docs == float(d)).astype(f32)
        doc_len = doc_len + hot * jnp.sum(hot, axis=(0, 1), keepdims=True)
    weight = jnp.zeros_like(langs)
    for g in range(dro_ref.shape[0]):
        weight = jnp.where(langs == float(g), dro_ref[g], weight)
    scale_ref[...] = (weight * (2.0 * mean_len) / (doc_len + mean_len)).T


def filter_kernel(mean_len, pieces, own_ref, dro_ref, ahead_ref, *refs):
    chunks, (spec_ref, scale_ref, held_ref, mid_ref, doc_ref, lang_ref) = refs[:pieces], refs[pieces:]
    _, span, _ = mid_ref.shape
    tokens = scale_ref.shape[0]
    gathered(own_ref, chunks, held_ref)
    for j in range(pieces):
        rows = held_ref[j, span:, :].astype(f32)
        doc_ref[j : j + 1, :] = rows[0:1]
        lang_ref[j : j + 1, :] = rows[1:2]
    token_scale(doc_ref, lang_ref, dro_ref, mean_len, scale_ref)

    def outer(row):
        rows = pl.ds(row, ROWS)
        out = outer_forward([held_ref[j, rows, :].astype(f32) for j in range(pieces)])
        for m, (re, im) in enumerate(out):
            mid_ref[m, rows, :tokens] = re.astype(bf16)
            mid_ref[m, rows, tokens:] = im.astype(bf16)

    chunked(span, outer)

    def inner(m):
        spec_ref[m] = lax.dot_general(
            ahead_ref[m], mid_ref[m], (((1,), (1,)), ((), ())), preferred_element_type=f32
        ).astype(bf16)

    each_piece(pieces, inner)


def to_middle(load, mid_ref, tokens, pieces):
    def outer(row):
        out = outer_forward([load(j, row) for j in range(pieces)])
        for m, (re, im) in enumerate(out):
            mid_ref[m, pl.ds(row, ROWS), :] = re.astype(bf16)
            mid_ref[m, pl.ds(tokens + row, ROWS), :] = im.astype(bf16)

    chunked(tokens, outer)


def from_middle(back_ref, store, tokens, pieces):
    def outer(row):
        out = outer_inverse(
            [
                (back_ref[m, pl.ds(row, ROWS), :], back_ref[m, pl.ds(tokens + row, ROWS), :])
                for m in range(pieces)
            ]
        )
        for j in range(pieces):
            store(j, row, out[j])

    chunked(tokens, outer)


def halves(value):
    value = value.astype(f32)
    middle = value.shape[0] // 2
    return value[:middle], value[middle:]


def joined(re, im):
    return jnp.concatenate([re.astype(bf16), im.astype(bf16)], axis=0)


def mixed_kernel(pieces, own_ref, filt_ref, skip_ref, ahead_ref, behind_ref, *refs):
    chunks, outs, (spec_ref, held_ref, mid_ref, back_ref) = (
        refs[:pieces],
        refs[pieces : 2 * pieces],
        refs[2 * pieces :],
    )
    tokens = held_ref.shape[1]
    gathered(own_ref, chunks, held_ref)

    def load(j, row):
        return held_ref[j, pl.ds(row, ROWS), :].astype(f32)

    to_middle(load, mid_ref, tokens, pieces)

    def inner(m):
        spec = dot(ahead_ref[m], mid_ref[m])
        spec_ref[m] = spec.astype(bf16)
        (re, im), (fre, fim) = halves(spec), halves(filt_ref[m])
        back_ref[m] = dot(behind_ref[m], joined(fre * re - fim * im, fre * im + fim * re))

    each_piece(pieces, inner)
    skip = skip_ref[...]

    def store(j, row, value):
        held_ref[j, pl.ds(row, ROWS), :] = (value + skip * load(j, row)).astype(bf16)

    from_middle(back_ref, store, tokens, pieces)
    scattered(own_ref, held_ref, outs)


def input_kernel(
    pieces, own_ref, filt_ref, spec_ref, scale_ref, skip_ref, ahead_ref, behind_ref, *refs
):
    chunks, outs, (cross_ref, held_ref, mid_ref, back_ref) = (
        refs[:pieces],
        refs[pieces : 2 * pieces],
        refs[2 * pieces :],
    )
    tokens = held_ref.shape[1]
    gathered(own_ref, chunks, held_ref)

    def load(j, row):
        rows = pl.ds(row, ROWS)
        return held_ref[j, rows, :].astype(f32) * scale_ref[rows, j : j + 1]

    to_middle(load, mid_ref, tokens, pieces)

    def inner(m):
        re, im = halves(dot(ahead_ref[m], mid_ref[m]))
        (fre, fim), (xre, xim) = halves(filt_ref[m]), halves(spec_ref[m])
        cross_ref[m] = joined(xre * re + xim * im, xre * im - xim * re)
        back_ref[m] = dot(behind_ref[m], joined(fre * re + fim * im, fre * im - fim * re))

    each_piece(pieces, inner)
    skip = skip_ref[...]

    def store(j, row, value):
        held_ref[j, pl.ds(row, ROWS), :] = (value + skip * load(j, row)).astype(bf16)

    from_middle(back_ref, store, tokens, pieces)
    scattered(own_ref, held_ref, outs)


def lags_kernel(own_ref, cross_ref, behind_ref, keep_ref, send_ref, back_ref, lag_ref):
    pieces, tall, span = cross_ref.shape
    tokens = tall // 2
    held = keep_ref.shape[1] // tokens
    members = pieces // held

    def inner(m):
        back_ref[m] = dot(behind_ref[m], cross_ref[m])

    each_piece(pieces, inner)

    def store(j, row, value):
        lag_ref[j, pl.ds(row, ROWS), :] = value

    from_middle(back_ref, store, tokens, pieces)
    for j in range(held):
        part = slice(j * tokens, (j + 1) * tokens)
        keep_ref[:, part] = lag_ref[own_ref[0] * held + j].T
        for r in range(1, members):
            send_ref[r - 1, :, part] = lag_ref[relative(own_ref, r, members) * held + j].T.astype(
                bf16
            )


def gate_kernel(pieces, own_ref, grad_ref, scale_ref, *refs):
    chunks, (out_ref, held_ref) = refs[:pieces], refs[pieces:]
    _, tokens, span = held_ref.shape
    gathered(own_ref, chunks, held_ref)
    lane = lax.broadcasted_iota(jnp.int32, (tokens, pieces), 1)
    scale = jnp.sum(
        jnp.where(lane == own_ref[0], scale_ref[...], jnp.zeros((tokens, pieces), f32)),
        axis=1,
        keepdims=True,
    )
    for i in range(pieces):
        part = slice(i * span, (i + 1) * span)
        out_ref[:, part] = (
            grad_ref[:, part].astype(f32) * scale * held_ref[i].astype(f32)
        ).astype(bf16)


def input_in_kernel(pieces, own_ref, *refs):
    chunks, (out_ref, held_ref) = refs[:pieces], refs[pieces:]
    _, _, span = held_ref.shape
    gathered(own_ref, chunks, held_ref)
    for i in range(pieces):
        out_ref[:, i * span : (i + 1) * span] = held_ref[i]


def call(kernel, out, ins, scratch=(), limit=24, cost=(0, 0)):
    return pl.pallas_call(
        kernel,
        out_shape=out,
        in_specs=ins,
        out_specs=jax.tree.map(lambda _: VMEM, out),
        scratch_shapes=scratch,
        compiler_params=pltpu.CompilerParams(vmem_limit_bytes=limit << 20),
        cost_estimate=pl.CostEstimate(flops=cost[0], bytes_accessed=cost[1], transcendentals=0),
    )


def local(grad_out, saved_input, gate_value, filter_taps, skip_gain, lang_ids, doc_ids, dro_weight):
    tokens = grad_out.shape[1]
    channels = grad_out.shape[2]
    pieces = lax.axis_size("ctx")
    members = lax.axis_size("dp")
    length = tokens * pieces
    span = channels // pieces
    mean_len = length / NDOCS
    place = lax.axis_index("ctx")
    own = place.reshape(1)
    ahead, behind = inner_tables(pieces, tokens)
    skip = lax.dynamic_slice_in_dim(skip_gain, place * span, span)[None, :]

    def exchange(chunks):
        rings = [[(i, (i + r) % pieces) for i in range(pieces)] for r in range(pieces)]
        return [chunks[0]] + [lax.ppermute(chunks[r], "ctx", rings[r]) for r in range(1, pieces)]

    shape = jax.ShapeDtypeStruct
    blocks = [shape((tokens, span), bf16)] * pieces
    held = pltpu.VMEM((pieces, tokens, span), bf16)
    middle = pltpu.VMEM((pieces, 2 * tokens, span), bf16)
    back = pltpu.VMEM((pieces, 2 * tokens, span), f32)
    spectrum = shape((pieces, 2 * tokens, span), bf16)
    many = [VMEM] * pieces
    macs = pieces * (2 * tokens) ** 2 * span

    taps = exchange(
        call(
            functools.partial(taps_out_kernel, pieces, span),
            [shape((span + ROWS, tokens), bf16)] * pieces,
            [SMEM, VMEM, VMEM, VMEM],
            cost=(0, 1 << 20),
        )(own, filter_taps, doc_ids, lang_ids)
    )
    inputs = exchange(
        call(
            functools.partial(input_out_kernel, pieces, span),
            blocks,
            [SMEM, VMEM],
            [held],
            cost=(0, 1 << 20),
        )(own, saved_input[0])
    )
    grads = exchange(
        call(
            functools.partial(grad_out_kernel, pieces, span),
            blocks,
            [SMEM, VMEM, VMEM],
            [held],
            cost=(0, 1 << 20),
        )(own, grad_out[0], gate_value[0])
    )
    filt, scale = call(
        functools.partial(filter_kernel, mean_len, pieces),
        (spectrum, shape((tokens, pieces), f32)),
        [SMEM, SMEM, VMEM] + many,
        [
            pltpu.VMEM((pieces, span + ROWS, tokens), bf16),
            pltpu.VMEM((pieces, span, 2 * tokens), bf16),
            pltpu.VMEM((pieces, tokens), f32),
            pltpu.VMEM((pieces, tokens), f32),
        ],
        cost=(2 * macs, 4 << 20),
    )(own, dro_weight, ahead, *taps)
    *mixed, spec = call(
        functools.partial(mixed_kernel, pieces),
        blocks + [spectrum],
        [SMEM] + [VMEM] * 4 + many,
        [held, middle, back],
        cost=(4 * macs, 8 << 20),
    )(own, filt, skip, ahead, behind, *inputs)
    mixed = exchange(mixed)
    *d_input, cross = call(
        functools.partial(input_kernel, pieces),
        blocks + [spectrum],
        [SMEM] + [VMEM] * 6 + many,
        [held, middle, back],
        cost=(4 * macs, 8 << 20),
    )(own, filt, spec, scale, skip, ahead, behind, *grads)
    d_input = exchange(d_input)
    keep, send = call(
        lags_kernel,
        (
            shape((span, length // members), f32),
            shape((members - 1, span, length // members), bf16),
        ),
        [SMEM, VMEM, VMEM],
        [back, pltpu.VMEM((pieces, tokens, span), f32)],
        cost=(2 * macs, 6 << 20),
    )(lax.axis_index("dp").reshape(1), cross, behind)
    d_filter = keep
    for r in range(1, members):
        ring = [(d, (d + r) % members) for d in range(members)]
        d_filter = d_filter + lax.ppermute(send[r - 1], "dp", ring).astype(f32)
    token_block = shape((tokens, channels), bf16)
    d_gate = call(
        functools.partial(gate_kernel, pieces),
        token_block,
        [SMEM, VMEM, VMEM] + many,
        [held],
        cost=(0, 2 << 20),
    )(own, grad_out[0], scale, *mixed)
    d_input = call(
        functools.partial(input_in_kernel, pieces),
        token_block,
        [SMEM] + many,
        [held],
        cost=(0, 1 << 20),
    )(own, *d_input)
    return (d_input[None], d_gate[None], d_filter)


def solution(mesh):
    return jax.shard_map(
        local,
        mesh=mesh,
        in_specs=(
            P("dp", "ctx", None),
            P("dp", "ctx", None),
            P("dp", "ctx", None),
            P(None, "ctx"),
            P(),
            P("dp", "ctx"),
            P("dp", "ctx"),
            P(),
        ),
        out_specs=(P("dp", "ctx", None), P("dp", "ctx", None), P("ctx", "dp")),
        check_vma=False,
    )
```

```python
import functools
import math

import jax
import jax.numpy as jnp
import numpy as np
from jax import lax
from jax.experimental import pallas as pl
from jax.experimental.pallas import tpu as pltpu
from jax.sharding import PartitionSpec as P

NDOCS = 32
ROWS = 16
VMEM = pl.BlockSpec(memory_space=pltpu.VMEM)
HBM = pl.BlockSpec(memory_space=pltpu.HBM)
SMEM = pl.BlockSpec(memory_space=pltpu.SMEM)
f32 = jnp.float32
bf16 = jnp.bfloat16


def inner_tables(pieces, tokens):
    size = 2 * pieces * tokens
    m = np.arange(pieces)[:, None, None]
    k = np.arange(tokens)[None, :, None]
    q = np.arange(tokens)[None, None, :]
    turn = (q * (4 * m + 1 + 4 * pieces * k)) % (2 * size)
    angle = math.pi / size * turn
    cos, sin = np.cos(angle), np.sin(angle)
    ahead = np.concatenate(
        [np.concatenate([cos, sin], axis=2), np.concatenate([-sin, cos], axis=2)], axis=1
    )
    behind = np.swapaxes(ahead, 1, 2) * (2.0 / size)
    return jnp.asarray(ahead, bf16), jnp.asarray(behind, bf16)


def outer_tables(pieces):
    m = np.arange(pieces)[:, None]
    j = np.arange(pieces)[None, :]
    angle = math.pi / (2 * pieces) * (j * (4 * m + 1) % (4 * pieces))
    both = np.stack([np.cos(angle), -np.sin(angle)], axis=1).reshape(2 * pieces, pieces)
    ahead = np.kron(both, np.eye(ROWS))
    return jnp.asarray(ahead, bf16), jnp.asarray(ahead.T, bf16)


def turned(value, turns):
    re, im = value
    turns = turns % 1.0
    if turns == 0.0:
        return value
    if turns == 0.25:
        return (-im, re)
    if turns == 0.5:
        return (-re, -im)
    if turns == 0.75:
        return (im, -re)
    cos, sin = math.cos(2.0 * math.pi * turns), math.sin(2.0 * math.pi * turns)
    if (turns * 8.0) % 1.0 == 0.0:
        root = math.sqrt(0.5)
        plus, minus = (re + im) * root, (re - im) * root
        if turns == 0.125:
            return (minus, plus)
        if turns == 0.375:
            return (-plus, minus)
        if turns == 0.625:
            return (-minus, -plus)
        return (plus, -minus)
    return (re * cos - im * sin, re * sin + im * cos)


def dft(values, sign):
    count = len(values)
    if count == 1:
        return values
    even, odd = dft(values[0::2], sign), dft(values[1::2], sign)
    first, second = [], []
    for k in range(count // 2):
        a, b = even[k], turned(odd[k], sign * k / count)
        first.append((a[0] + b[0], a[1] + b[1]))
        second.append((a[0] - b[0], a[1] - b[1]))
    return first + second


def outer_inverse(values):
    count = len(values)
    out = []
    for j, (re, im) in enumerate(dft(values, 1.0)):
        angle = math.pi * j / (2 * count)
        out.append(re if j == 0 else re * math.cos(angle) - im * math.sin(angle))
    return out


def chunked(total, body):
    def step(i, carry):
        body(pl.multiple_of(i * ROWS, ROWS))
        return carry

    lax.fori_loop(0, total // ROWS, step, 0)


def each_piece(pieces, body, group=4):
    def step(i, carry):
        for g in range(group):
            body(i * group + g)
        return carry

    lax.fori_loop(0, pieces // group, step, 0)


def dot(a, b):
    return lax.dot_general(a, b, (((1,), (0,)), ((), ())), preferred_element_type=f32)


def places(pieces, tokens, span):
    beside = max(1, tokens // span)

    def place(index, start):
        row = start + (index // beside) * tokens
        column = (index % beside) * span
        return row, slice(column, column + span)

    tall = -(-2 // beside) * tokens
    return place, tall


def copies(*pairs):
    started = [pltpu.make_async_copy(*pair) for pair in pairs]
    for copy in started:
        copy.start()
    return started


def finish(*started):
    for copy in started:
        copy.wait()


def id_rows(doc_ref, lang_ref, tokens):
    tile = lax.broadcasted_iota(jnp.int32, (ROWS, tokens), 0)
    return jnp.where(tile == 0, doc_ref[...], lang_ref[...]).astype(f32).astype(bf16)


def gated(grad_ref, gate_ref, part):
    return (grad_ref[:, part].astype(f32) * gate_ref[:, part].astype(f32)).astype(bf16)


def prep_kernel(pieces, span, input_ref, grad_ref, gate_ref, taps_ref, doc_ref, lang_ref, out_ref):
    tokens = grad_ref.shape[0]
    place, tall = places(pieces, tokens, span)
    ids = id_rows(doc_ref, lang_ref, tokens)
    in_row, in_lanes = place(0, span)
    grad_row, grad_lanes = place(1, span)
    for i in range(pieces):
        part = slice(i * span, (i + 1) * span)
        out_ref[i, :span, :] = taps_ref[part, :]
        out_ref[i, in_row : in_row + tokens, in_lanes] = input_ref[:, part]
        out_ref[i, grad_row : grad_row + tokens, grad_lanes] = gated(grad_ref, gate_ref, part)
        out_ref[i, span + tall :, :] = ids


def prep_copy_kernel(
    pieces,
    span,
    input_ref,
    grad_ref,
    gate_ref,
    taps_ref,
    doc_ref,
    lang_ref,
    out_ref,
    factor_ref,
    made_ref,
    ids_ref,
    in_sem,
    out_sem,
    made_sem,
):
    tokens = grad_ref.shape[0]
    place, tall = places(pieces, tokens, span)
    row = [place(side, span)[0] for side in (0, 1)]
    groups = in_sem.shape[1]
    group = pieces // groups
    loads = []
    for g in range(groups):
        wide = pl.ds(g * group * span, group * span)
        loads.append(
            copies(
                (grad_ref.at[:, wide], factor_ref.at[0, :, wide], in_sem.at[0, g]),
                (gate_ref.at[:, wide], factor_ref.at[1, :, wide], in_sem.at[1, g]),
            )
        )
    sent = []
    for i in range(pieces):
        part = pl.ds(i * span, span)
        sent += copies(
            (input_ref.at[:, part], out_ref.at[i, pl.ds(row[0], tokens), :], out_sem.at[i])
        )
    sent += copies((taps_ref, out_ref.at[:, pl.ds(0, span), :], out_sem.at[pieces]))
    ids = id_rows(doc_ref, lang_ref, tokens)
    for i in range(pieces):
        ids_ref[i] = ids
    sent += copies((ids_ref, out_ref.at[:, pl.ds(span + tall, ROWS), :], out_sem.at[pieces + 1]))
    for g in range(groups):
        finish(*loads[g])
        for i in range(g * group, (g + 1) * group):
            part = slice(i * span, (i + 1) * span)
            made_ref[i] = gated(factor_ref.at[0], factor_ref.at[1], part)
        these = pl.ds(g * group, group)
        sent += copies(
            (made_ref.at[these], out_ref.at[these, pl.ds(row[1], tokens), :], made_sem.at[g])
        )
    finish(*sent)


def token_scale(message_ref, scale_ref, dro_ref, ids, mean_len, doc_ref, lang_ref):
    for j in range(message_ref.shape[0]):
        rows = message_ref[j, ids:, :].astype(f32)
        doc_ref[j : j + 1, :] = rows[0:1]
        lang_ref[j : j + 1, :] = rows[1:2]
    docs, langs = doc_ref[...], lang_ref[...]
    doc_len = jnp.zeros_like(docs)
    for d in range(NDOCS):
        hot = (docs == float(d)).astype(f32)
        doc_len = doc_len + hot * jnp.sum(hot, axis=(0, 1), keepdims=True)
    weight = jnp.zeros_like(langs)
    for g in range(dro_ref.shape[0]):
        weight = jnp.where(langs == float(g), dro_ref[g], weight)
    scale_ref[...] = (weight * (2.0 * mean_len) / (doc_len + mean_len)).T


def conv_kernel(
    mean_len,
    message_ref,
    skip_ref,
    dro_ref,
    ahead_hbm,
    behind_hbm,
    outer_hbm,
    inverse_hbm,
    out_hbm,
    cross_hbm,
    scale_ref,
    ahead_ref,
    behind_ref,
    outer_ref,
    inverse_ref,
    out_ref,
    cross_ref,
    scaled_ref,
    taps_mid_ref,
    mid_ref,
    back_ref,
    doc_ref,
    lang_ref,
    in_sem,
    out_sem,
):
    pieces = message_ref.shape[0]
    tokens = message_ref.shape[2]
    span = skip_ref.shape[1]
    place, tall = places(pieces, tokens, span)
    outer_in, ahead_in, behind_in, inverse_in = copies(
        (outer_hbm, outer_ref, in_sem.at[0]),
        (ahead_hbm, ahead_ref, in_sem.at[1]),
        (behind_hbm, behind_ref, in_sem.at[2]),
        (inverse_hbm, inverse_ref, in_sem.at[3]),
    )
    token_scale(message_ref, scale_ref, dro_ref, span + tall, mean_len, doc_ref, lang_ref)
    outer_in.wait()

    def outer_taps(row):
        rows = pl.ds(row, ROWS)
        stack = jnp.concatenate([message_ref[j, rows, :] for j in range(pieces)], axis=0)
        out = dot(outer_ref[...], stack).astype(bf16)
        for m in range(pieces):
            at = 2 * m * ROWS
            taps_mid_ref[m, rows, :tokens] = out[at : at + ROWS]
            taps_mid_ref[m, rows, tokens:] = out[at + ROWS : at + 2 * ROWS]

    chunked(span, outer_taps)
    sides = (slice(0, span), slice(span, 2 * span))

    def load(side, j, row):
        start, lanes = place(side, span)
        return message_ref[j, pl.ds(start + row, ROWS), lanes]

    def outer(row):
        rows = pl.ds(row, ROWS)
        stack = []
        for j in range(pieces):
            scaled = (load(1, j, row).astype(f32) * scale_ref[rows, j : j + 1]).astype(bf16)
            scaled_ref[j, rows, :] = scaled
            stack.append(jnp.concatenate([load(0, j, row), scaled], axis=1))
        out = dot(outer_ref[...], jnp.concatenate(stack, axis=0)).astype(bf16)
        for m in range(pieces):
            at = 2 * m * ROWS
            mid_ref[m, rows, :] = out[at : at + ROWS]
            mid_ref[m, pl.ds(tokens + row, ROWS), :] = out[at + ROWS : at + 2 * ROWS]

    chunked(tokens, outer)
    finish(ahead_in, behind_in)

    def inner(m):
        filt = lax.dot_general(
            ahead_ref[m], taps_mid_ref[m], (((1,), (1,)), ((), ())), preferred_element_type=f32
        )
        spec = dot(ahead_ref[m], mid_ref[m])
        fre, fim = filt[:tokens], filt[tokens:]
        xre, xim = spec[:tokens, sides[0]], spec[tokens:, sides[0]]
        gre, gim = spec[:tokens, sides[1]], spec[tokens:, sides[1]]
        cross_ref[m, :tokens, :] = (xre * gre + xim * gim).astype(bf16)
        cross_ref[m, tokens:, :] = (xre * gim - xim * gre).astype(bf16)
        mixed = jnp.concatenate([fre * xre - fim * xim, fre * xim + fim * xre], axis=0)
        back = jnp.concatenate([fre * gre + fim * gim, fre * gim - fim * gre], axis=0)
        both = jnp.concatenate([mixed.astype(bf16), back.astype(bf16)], axis=1)
        back_ref[m] = dot(behind_ref[m], both).astype(bf16)

    each_piece(pieces, inner)
    (cross_out,) = copies((cross_ref, cross_hbm, out_sem.at[0]))
    inverse_in.wait()
    skip = skip_ref[...]

    def outer_back(row):
        rows = pl.ds(row, ROWS)
        stack = []
        for m in range(pieces):
            stack += [back_ref[m, rows, :], back_ref[m, pl.ds(tokens + row, ROWS), :]]
        out = dot(inverse_ref[...], jnp.concatenate(stack, axis=0))
        for j in range(pieces):
            at = slice(j * ROWS, (j + 1) * ROWS)
            for side in (0, 1):
                start, lanes = place(side, 0)
                own = load(0, j, row) if side == 0 else scaled_ref[j, rows, :]
                out_ref[j, pl.ds(start + row, ROWS), lanes] = (
                    out[at, sides[side]] + skip * own.astype(f32)
                ).astype(bf16)

    chunked(tokens, outer_back)
    (out_out,) = copies((out_ref, out_hbm, out_sem.at[1]))
    finish(cross_out, out_out)


def lags_kernel(own_ref, cross_ref, behind_ref, keep_ref, send_ref, back_ref, lag_ref):
    pieces, tall, span = cross_ref.shape
    tokens = tall // 2
    held = keep_ref.shape[1] // tokens
    members = pieces // held

    def inner(m):
        back_ref[m] = dot(behind_ref[m], cross_ref[m])

    each_piece(pieces, inner)

    def body(row):
        out = outer_inverse(
            [
                (back_ref[m, pl.ds(row, ROWS), :], back_ref[m, pl.ds(tokens + row, ROWS), :])
                for m in range(pieces)
            ]
        )
        for j in range(pieces):
            lag_ref[j, pl.ds(row, ROWS), :] = out[j]

    chunked(tokens, body)
    for j in range(held):
        part = slice(j * tokens, (j + 1) * tokens)
        keep_ref[:, part] = lag_ref[own_ref[0] * held + j].T
        for r in range(1, members):
            other = lax.rem(own_ref[0] + r, members)
            send_ref[r - 1, :, part] = lag_ref[other * held + j].T.astype(bf16)


def own_scale(own_ref, scale_ref):
    lane = lax.broadcasted_iota(jnp.int32, scale_ref.shape, 1)
    scale = jnp.where(lane == own_ref[0], scale_ref[...], jnp.zeros(scale_ref.shape, f32))
    return jnp.sum(scale, axis=1, keepdims=True)


def final_copy_kernel(
    own_ref, grad_hbm, scale_ref, message_ref, gate_hbm, input_hbm, grad_ref, gate_ref, sem, out_sem
):
    pieces = message_ref.shape[0]
    tokens, channels = grad_hbm.shape
    span = channels // pieces
    place, _ = places(pieces, tokens, span)
    mixed_row, back_row = place(0, 0)[0], place(1, 0)[0]
    (grad_in,) = copies((grad_hbm, grad_ref, sem.at[0]))
    sent = []
    for i in range(pieces):
        part = pl.ds(i * span, span)
        sent += copies(
            (message_ref.at[i, pl.ds(back_row, tokens), :], input_hbm.at[:, part], out_sem.at[i])
        )
    scale = own_scale(own_ref, scale_ref)
    grad_in.wait()
    for i in range(pieces):
        part = slice(i * span, (i + 1) * span)
        mixed = message_ref[i, mixed_row : mixed_row + tokens, :].astype(f32)
        gate_ref[:, part] = (grad_ref[:, part].astype(f32) * scale * mixed).astype(bf16)
        if (2 * (i + 1)) % pieces == 0:
            half = (2 * (i + 1)) // pieces - 1
            wide = pl.ds(half * (channels // 2), channels // 2)
            sent += copies((gate_ref.at[:, wide], gate_hbm.at[:, wide], sem.at[1 + half]))
    finish(*sent)


def final_kernel(own_ref, grad_ref, scale_ref, message_ref, gate_ref, input_ref):
    pieces = message_ref.shape[0]
    tokens, channels = grad_ref.shape
    span = channels // pieces
    place, _ = places(pieces, tokens, span)
    scale = own_scale(own_ref, scale_ref)
    mixed_row, mixed_lanes = place(0, 0)
    back_row, back_lanes = place(1, 0)
    for i in range(pieces):
        part = slice(i * span, (i + 1) * span)
        mixed = message_ref[i, mixed_row : mixed_row + tokens, mixed_lanes].astype(f32)
        gate_ref[:, part] = (grad_ref[:, part].astype(f32) * scale * mixed).astype(bf16)
        input_ref[:, part] = message_ref[i, back_row : back_row + tokens, back_lanes]


def call(kernel, out, ins, scratch=(), outs=None, limit=24, cost=(0, 0)):
    return pl.pallas_call(
        kernel,
        out_shape=out,
        in_specs=ins,
        out_specs=jax.tree.map(lambda _: VMEM, out) if outs is None else outs,
        scratch_shapes=scratch,
        compiler_params=pltpu.CompilerParams(vmem_limit_bytes=limit << 20),
        cost_estimate=pl.CostEstimate(flops=cost[0], bytes_accessed=cost[1], transcendentals=0),
    )


def local(grad_out, saved_input, gate_value, filter_taps, skip_gain, lang_ids, doc_ids, dro_weight):
    tokens = grad_out.shape[1]
    channels = grad_out.shape[2]
    pieces = lax.axis_size("ctx")
    members = lax.axis_size("dp")
    length = tokens * pieces
    span = channels // pieces
    mean_len = length / NDOCS
    own = lax.axis_index("ctx")
    ahead, behind = inner_tables(pieces, tokens)
    outer, inverse = outer_tables(pieces)
    skip = lax.dynamic_slice_in_dim(skip_gain, own * span, span)[None, :]
    exchange = functools.partial(
        lax.all_to_all, axis_name="ctx", split_axis=0, concat_axis=0, tiled=True
    )
    tall = places(pieces, tokens, span)[1]
    macs = pieces * (2 * tokens) ** 2 * span

    aligned = span % 128 == 0
    dma = pltpu.SemaphoreType.DMA
    groups = 4
    message = call(
        functools.partial(prep_copy_kernel if aligned else prep_kernel, pieces, span),
        jax.ShapeDtypeStruct((pieces, span + tall + ROWS, tokens), bf16),
        [HBM] * 4 + [VMEM] * 2 if aligned else [VMEM] * 6,
        [
            pltpu.VMEM((2, tokens, channels), bf16),
            pltpu.VMEM((pieces, tokens, span), bf16),
            pltpu.VMEM((pieces, ROWS, tokens), bf16),
            dma((2, groups)),
            dma((pieces + 2,)),
            dma((groups,)),
        ]
        if aligned
        else (),
        outs=HBM if aligned else VMEM,
        cost=(0, 4 << 20),
    )(
        saved_input[0],
        grad_out[0],
        gate_value[0],
        filter_taps.reshape(pieces, span, tokens) if aligned else filter_taps,
        doc_ids,
        lang_ids,
    )
    message = exchange(message)
    message, cross, scale = call(
        functools.partial(conv_kernel, mean_len),
        (
            jax.ShapeDtypeStruct((pieces, tall, tokens), bf16),
            jax.ShapeDtypeStruct((pieces, 2 * tokens, span), bf16),
            jax.ShapeDtypeStruct((tokens, pieces), f32),
        ),
        [VMEM, VMEM, SMEM, HBM, HBM, HBM, HBM],
        [
            pltpu.VMEM(ahead.shape, bf16),
            pltpu.VMEM(behind.shape, bf16),
            pltpu.VMEM(outer.shape, bf16),
            pltpu.VMEM(inverse.shape, bf16),
            pltpu.VMEM((pieces, tall, tokens), bf16),
            pltpu.VMEM((pieces, 2 * tokens, span), bf16),
            pltpu.VMEM((pieces, tokens, span), bf16),
            pltpu.VMEM((pieces, span, 2 * tokens), bf16),
            pltpu.VMEM((pieces, 2 * tokens, 2 * span), bf16),
            pltpu.VMEM((pieces, 2 * tokens, 2 * span), bf16),
            pltpu.VMEM((pieces, tokens), f32),
            pltpu.VMEM((pieces, tokens), f32),
            dma((4,)),
            dma((2,)),
        ],
        outs=(HBM, HBM, VMEM),
        limit=32,
        cost=(10 * macs, 8 << 20),
    )(message, skip, dro_weight, ahead, behind, outer, inverse)
    message = exchange(message)
    keep, send = call(
        lags_kernel,
        (
            jax.ShapeDtypeStruct((span, length // members), f32),
            jax.ShapeDtypeStruct((members - 1, span, length // members), bf16),
        ),
        [SMEM, VMEM, VMEM],
        [
            pltpu.VMEM((pieces, 2 * tokens, span), f32),
            pltpu.VMEM((pieces, tokens, span), f32),
        ],
        cost=(2 * macs, 6 << 20),
    )(lax.axis_index("dp").reshape(1), cross, behind)
    d_filter = keep
    for r in range(1, members):
        ring = [(d, (d + r) % members) for d in range(members)]
        d_filter = d_filter + lax.ppermute(send[r - 1], "dp", ring).astype(f32)
    token_block = jax.ShapeDtypeStruct((tokens, channels), bf16)
    d_gate, d_input = call(
        final_copy_kernel if aligned else final_kernel,
        (token_block, token_block),
        [SMEM, HBM if aligned else VMEM, VMEM, VMEM],
        [
            pltpu.VMEM((tokens, channels), bf16),
            pltpu.VMEM((tokens, channels), bf16),
            dma((3,)),
            dma((pieces,)),
        ]
        if aligned
        else (),
        outs=(HBM, HBM) if aligned else (VMEM, VMEM),
        cost=(0, 4 << 20),
    )(own.reshape(1), grad_out[0], scale, message)
    return (d_input[None], d_gate[None], d_filter)


def solution(mesh):
    return jax.shard_map(
        local,
        mesh=mesh,
        in_specs=(
            P("dp", "ctx", None),
            P("dp", "ctx", None),
            P("dp", "ctx", None),
            P(None, "ctx"),
            P(),
            P("dp", "ctx"),
            P("dp", "ctx"),
            P(),
        ),
        out_specs=(P("dp", "ctx", None), P("dp", "ctx", None), P("ctx", "dp")),
        check_vma=False,
    )
```

```python
import functools
import math

import jax
import jax.numpy as jnp
import numpy as np
from jax import lax
from jax.experimental import pallas as pl
from jax.experimental.pallas import tpu as pltpu
from jax.sharding import PartitionSpec as P

NDOCS = 32
ROWS = 16
VMEM = pl.BlockSpec(memory_space=pltpu.VMEM)
HBM = pl.BlockSpec(memory_space=pltpu.HBM)
SMEM = pl.BlockSpec(memory_space=pltpu.SMEM)
f32 = jnp.float32
bf16 = jnp.bfloat16


def inner_tables(pieces, tokens):
    size = 2 * pieces * tokens
    m = np.arange(pieces)[:, None, None]
    k = np.arange(tokens)[None, :, None]
    q = np.arange(tokens)[None, None, :]
    turn = (q * (4 * m + 1 + 4 * pieces * k)) % (2 * size)
    angle = math.pi / size * turn
    cos, sin = np.cos(angle), np.sin(angle)
    ahead = np.concatenate(
        [np.concatenate([cos, sin], axis=2), np.concatenate([-sin, cos], axis=2)], axis=1
    )
    behind = np.swapaxes(ahead, 1, 2) * (2.0 / size)
    return jnp.asarray(ahead, bf16), jnp.asarray(behind, bf16)


def outer_tables(pieces):
    m = np.arange(pieces)[:, None]
    j = np.arange(pieces)[None, :]
    angle = math.pi / (2 * pieces) * (j * (4 * m + 1) % (4 * pieces))
    both = np.stack([np.cos(angle), -np.sin(angle)], axis=1).reshape(2 * pieces, pieces)
    ahead = np.kron(both, np.eye(ROWS))
    return jnp.asarray(ahead, bf16), jnp.asarray(ahead.T, bf16)


def turned(value, turns):
    re, im = value
    turns = turns % 1.0
    if turns == 0.0:
        return value
    if turns == 0.25:
        return (-im, re)
    if turns == 0.5:
        return (-re, -im)
    if turns == 0.75:
        return (im, -re)
    cos, sin = math.cos(2.0 * math.pi * turns), math.sin(2.0 * math.pi * turns)
    if (turns * 8.0) % 1.0 == 0.0:
        root = math.sqrt(0.5)
        plus, minus = (re + im) * root, (re - im) * root
        if turns == 0.125:
            return (minus, plus)
        if turns == 0.375:
            return (-plus, minus)
        if turns == 0.625:
            return (-minus, -plus)
        return (plus, -minus)
    return (re * cos - im * sin, re * sin + im * cos)


def dft(values, sign):
    count = len(values)
    if count == 1:
        return values
    even, odd = dft(values[0::2], sign), dft(values[1::2], sign)
    first, second = [], []
    for k in range(count // 2):
        a, b = even[k], turned(odd[k], sign * k / count)
        first.append((a[0] + b[0], a[1] + b[1]))
        second.append((a[0] - b[0], a[1] - b[1]))
    return first + second


def outer_inverse(values):
    count = len(values)
    out = []
    for j, (re, im) in enumerate(dft(values, 1.0)):
        angle = math.pi * j / (2 * count)
        out.append(re if j == 0 else re * math.cos(angle) - im * math.sin(angle))
    return out


def chunked(total, body, unrolled=False):
    if unrolled:
        for i in range(total // ROWS):
            body(i * ROWS)
        return

    def step(i, carry):
        body(pl.multiple_of(i * ROWS, ROWS))
        return carry

    lax.fori_loop(0, total // ROWS, step, 0)


def each_piece(pieces, body, group=4):
    def step(i, carry):
        for g in range(group):
            body(i * group + g)
        return carry

    lax.fori_loop(0, pieces // group, step, 0)


def dot(a, b):
    return lax.dot_general(a, b, (((1,), (0,)), ((), ())), preferred_element_type=f32)


def places(pieces, tokens, span):
    beside = max(1, tokens // span)

    def place(index, start):
        row = start + (index // beside) * tokens
        column = (index % beside) * span
        return row, slice(column, column + span)

    tall = -(-2 // beside) * tokens
    return place, tall


def copies(*pairs):
    started = [pltpu.make_async_copy(*pair) for pair in pairs]
    for copy in started:
        copy.start()
    return started


def finish(*started):
    for copy in started:
        copy.wait()


def id_rows(doc_ref, lang_ref, tokens):
    tile = lax.broadcasted_iota(jnp.int32, (ROWS, tokens), 0)
    return jnp.where(tile == 0, doc_ref[...], lang_ref[...]).astype(f32).astype(bf16)


def gated(grad_ref, gate_ref, part):
    return (grad_ref[:, part].astype(f32) * gate_ref[:, part].astype(f32)).astype(bf16)


def prep_kernel(pieces, span, input_ref, grad_ref, gate_ref, taps_ref, doc_ref, lang_ref, out_ref):
    tokens = grad_ref.shape[0]
    place, tall = places(pieces, tokens, span)
    ids = id_rows(doc_ref, lang_ref, tokens)
    in_row, in_lanes = place(0, span)
    grad_row, grad_lanes = place(1, span)
    for i in range(pieces):
        part = slice(i * span, (i + 1) * span)
        out_ref[i, :span, :] = taps_ref[part, :]
        out_ref[i, in_row : in_row + tokens, in_lanes] = input_ref[:, part]
        out_ref[i, grad_row : grad_row + tokens, grad_lanes] = gated(grad_ref, gate_ref, part)
        out_ref[i, span + tall :, :] = ids


def prep_copy_kernel(
    pieces,
    span,
    input_ref,
    grad_ref,
    gate_ref,
    taps_ref,
    doc_ref,
    lang_ref,
    out_ref,
    factor_ref,
    made_ref,
    ids_ref,
    in_sem,
    out_sem,
    made_sem,
):
    tokens = grad_ref.shape[0]
    place, tall = places(pieces, tokens, span)
    row = [place(side, span)[0] for side in (0, 1)]
    groups = in_sem.shape[1]
    group = pieces // groups
    loads = []
    for g in range(groups):
        wide = pl.ds(g * group * span, group * span)
        loads.append(
            copies(
                (grad_ref.at[:, wide], factor_ref.at[0, :, wide], in_sem.at[0, g]),
                (gate_ref.at[:, wide], factor_ref.at[1, :, wide], in_sem.at[1, g]),
            )
        )
    sent = []
    for i in range(pieces):
        part = pl.ds(i * span, span)
        sent += copies(
            (input_ref.at[:, part], out_ref.at[i, pl.ds(row[0], tokens), :], out_sem.at[i])
        )
    sent += copies((taps_ref, out_ref.at[:, pl.ds(0, span), :], out_sem.at[pieces]))
    ids = id_rows(doc_ref, lang_ref, tokens)
    for i in range(pieces):
        ids_ref[i] = ids
    sent += copies((ids_ref, out_ref.at[:, pl.ds(span + tall, ROWS), :], out_sem.at[pieces + 1]))
    for g in range(groups):
        finish(*loads[g])
        for i in range(g * group, (g + 1) * group):
            part = slice(i * span, (i + 1) * span)
            made_ref[i] = gated(factor_ref.at[0], factor_ref.at[1], part)
        these = pl.ds(g * group, group)
        sent += copies(
            (made_ref.at[these], out_ref.at[these, pl.ds(row[1], tokens), :], made_sem.at[g])
        )
    finish(*sent)


def token_scale(message_ref, scale_ref, dro_ref, ids, mean_len, doc_ref, lang_ref):
    for j in range(message_ref.shape[0]):
        rows = message_ref[j, ids:, :].astype(f32)
        doc_ref[j : j + 1, :] = rows[0:1]
        lang_ref[j : j + 1, :] = rows[1:2]
    docs, langs = doc_ref[...], lang_ref[...]
    doc_len = jnp.zeros_like(docs)
    for d in range(NDOCS):
        hot = (docs == float(d)).astype(f32)
        doc_len = doc_len + hot * jnp.sum(hot, axis=(0, 1), keepdims=True)
    weight = jnp.zeros_like(langs)
    for g in range(dro_ref.shape[0]):
        weight = jnp.where(langs == float(g), dro_ref[g], weight)
    scale_ref[...] = (weight * (2.0 * mean_len) / (doc_len + mean_len)).T


def conv_kernel(
    mean_len,
    message_ref,
    skip_ref,
    dro_ref,
    ahead_hbm,
    behind_hbm,
    outer_hbm,
    inverse_hbm,
    out_hbm,
    cross_hbm,
    scale_ref,
    ahead_ref,
    behind_ref,
    outer_ref,
    inverse_ref,
    out_ref,
    cross_ref,
    scaled_ref,
    taps_mid_ref,
    mid_ref,
    back_ref,
    doc_ref,
    lang_ref,
    in_sem,
    out_sem,
):
    pieces = message_ref.shape[0]
    tokens = message_ref.shape[2]
    span = skip_ref.shape[1]
    place, tall = places(pieces, tokens, span)
    outer_in, ahead_in, behind_in, inverse_in = copies(
        (outer_hbm, outer_ref, in_sem.at[0]),
        (ahead_hbm, ahead_ref, in_sem.at[1]),
        (behind_hbm, behind_ref, in_sem.at[2]),
        (inverse_hbm, inverse_ref, in_sem.at[3]),
    )
    token_scale(message_ref, scale_ref, dro_ref, span + tall, mean_len, doc_ref, lang_ref)
    outer_in.wait()

    def outer_taps(row):
        rows = pl.ds(row, ROWS)
        stack = jnp.concatenate([message_ref[j, rows, :] for j in range(pieces)], axis=0)
        out = dot(outer_ref[...], stack).astype(bf16)
        for m in range(pieces):
            at = 2 * m * ROWS
            taps_mid_ref[m, rows, :tokens] = out[at : at + ROWS]
            taps_mid_ref[m, rows, tokens:] = out[at + ROWS : at + 2 * ROWS]

    chunked(span, outer_taps, True)
    sides = (slice(0, span), slice(span, 2 * span))

    def load(side, j, row):
        start, lanes = place(side, span)
        return message_ref[j, pl.ds(start + row, ROWS), lanes]

    def outer(row):
        rows = pl.ds(row, ROWS)
        stack = []
        for j in range(pieces):
            scaled = (load(1, j, row).astype(f32) * scale_ref[rows, j : j + 1]).astype(bf16)
            scaled_ref[j, rows, :] = scaled
            stack.append(jnp.concatenate([load(0, j, row), scaled], axis=1))
        out = dot(outer_ref[...], jnp.concatenate(stack, axis=0)).astype(bf16)
        for m in range(pieces):
            at = 2 * m * ROWS
            mid_ref[m, rows, :] = out[at : at + ROWS]
            mid_ref[m, pl.ds(tokens + row, ROWS), :] = out[at + ROWS : at + 2 * ROWS]

    chunked(tokens, outer, True)
    finish(ahead_in, behind_in)

    def inner(m):
        filt = lax.dot_general(
            ahead_ref[m], taps_mid_ref[m], (((1,), (1,)), ((), ())), preferred_element_type=f32
        )
        spec = dot(ahead_ref[m], mid_ref[m])
        fre, fim = filt[:tokens], filt[tokens:]
        xre, xim = spec[:tokens, sides[0]], spec[tokens:, sides[0]]
        gre, gim = spec[:tokens, sides[1]], spec[tokens:, sides[1]]
        cross_ref[m, :tokens, :] = (xre * gre + xim * gim).astype(bf16)
        cross_ref[m, tokens:, :] = (xre * gim - xim * gre).astype(bf16)
        mixed = jnp.concatenate([fre * xre - fim * xim, fre * xim + fim * xre], axis=0)
        back = jnp.concatenate([fre * gre + fim * gim, fre * gim - fim * gre], axis=0)
        both = jnp.concatenate([mixed.astype(bf16), back.astype(bf16)], axis=1)
        back_ref[m] = dot(behind_ref[m], both).astype(bf16)

    each_piece(pieces, inner, 8)
    (cross_out,) = copies((cross_ref, cross_hbm, out_sem.at[0]))
    inverse_in.wait()
    skip = skip_ref[...]

    def outer_back(row):
        rows = pl.ds(row, ROWS)
        stack = []
        for m in range(pieces):
            stack += [back_ref[m, rows, :], back_ref[m, pl.ds(tokens + row, ROWS), :]]
        out = dot(inverse_ref[...], jnp.concatenate(stack, axis=0))
        for j in range(pieces):
            at = slice(j * ROWS, (j + 1) * ROWS)
            for side in (0, 1):
                start, lanes = place(side, 0)
                own = load(0, j, row) if side == 0 else scaled_ref[j, rows, :]
                out_ref[j, pl.ds(start + row, ROWS), lanes] = (
                    out[at, sides[side]] + skip * own.astype(f32)
                ).astype(bf16)

    chunked(tokens, outer_back, True)
    (out_out,) = copies((out_ref, out_hbm, out_sem.at[1]))
    finish(cross_out, out_out)


def lags_kernel(own_ref, cross_ref, behind_ref, keep_ref, send_ref, back_ref, lag_ref):
    pieces, tall, span = cross_ref.shape
    tokens = tall // 2
    held = keep_ref.shape[1] // tokens
    members = pieces // held

    def inner(m):
        back_ref[m] = dot(behind_ref[m], cross_ref[m])

    each_piece(pieces, inner)

    def body(row):
        out = outer_inverse(
            [
                (back_ref[m, pl.ds(row, ROWS), :], back_ref[m, pl.ds(tokens + row, ROWS), :])
                for m in range(pieces)
            ]
        )
        for j in range(pieces):
            lag_ref[j, pl.ds(row, ROWS), :] = out[j]

    chunked(tokens, body)
    for j in range(held):
        part = slice(j * tokens, (j + 1) * tokens)
        keep_ref[:, part] = lag_ref[own_ref[0] * held + j].T
        for r in range(1, members):
            other = lax.rem(own_ref[0] + r, members)
            send_ref[r - 1, :, part] = lag_ref[other * held + j].T.astype(bf16)


def own_scale(own_ref, scale_ref):
    lane = lax.broadcasted_iota(jnp.int32, scale_ref.shape, 1)
    scale = jnp.where(lane == own_ref[0], scale_ref[...], jnp.zeros(scale_ref.shape, f32))
    return jnp.sum(scale, axis=1, keepdims=True)


def final_copy_kernel(
    own_ref, grad_hbm, scale_ref, message_ref, gate_hbm, input_hbm, grad_ref, gate_ref, sem, out_sem
):
    pieces = message_ref.shape[0]
    tokens, channels = grad_hbm.shape
    span = channels // pieces
    place, _ = places(pieces, tokens, span)
    mixed_row, back_row = place(0, 0)[0], place(1, 0)[0]
    (grad_in,) = copies((grad_hbm, grad_ref, sem.at[0]))
    sent = []
    for i in range(pieces):
        part = pl.ds(i * span, span)
        sent += copies(
            (message_ref.at[i, pl.ds(back_row, tokens), :], input_hbm.at[:, part], out_sem.at[i])
        )
    scale = own_scale(own_ref, scale_ref)
    grad_in.wait()
    for i in range(pieces):
        part = slice(i * span, (i + 1) * span)
        mixed = message_ref[i, mixed_row : mixed_row + tokens, :].astype(f32)
        gate_ref[:, part] = (grad_ref[:, part].astype(f32) * scale * mixed).astype(bf16)
        if (2 * (i + 1)) % pieces == 0:
            half = (2 * (i + 1)) // pieces - 1
            wide = pl.ds(half * (channels // 2), channels // 2)
            sent += copies((gate_ref.at[:, wide], gate_hbm.at[:, wide], sem.at[1 + half]))
    finish(*sent)


def final_kernel(own_ref, grad_ref, scale_ref, message_ref, gate_ref, input_ref):
    pieces = message_ref.shape[0]
    tokens, channels = grad_ref.shape
    span = channels // pieces
    place, _ = places(pieces, tokens, span)
    scale = own_scale(own_ref, scale_ref)
    mixed_row, mixed_lanes = place(0, 0)
    back_row, back_lanes = place(1, 0)
    for i in range(pieces):
        part = slice(i * span, (i + 1) * span)
        mixed = message_ref[i, mixed_row : mixed_row + tokens, mixed_lanes].astype(f32)
        gate_ref[:, part] = (grad_ref[:, part].astype(f32) * scale * mixed).astype(bf16)
        input_ref[:, part] = message_ref[i, back_row : back_row + tokens, back_lanes]


def call(kernel, out, ins, scratch=(), outs=None, room=40 << 20, cost=(0, 0)):
    return pl.pallas_call(
        kernel,
        out_shape=out,
        in_specs=ins,
        out_specs=jax.tree.map(lambda _: VMEM, out) if outs is None else outs,
        scratch_shapes=scratch,
        compiler_params=pltpu.CompilerParams(vmem_limit_bytes=(64 << 20) - room),
        cost_estimate=pl.CostEstimate(flops=cost[0], bytes_accessed=cost[1], transcendentals=0),
    )


def local(grad_out, saved_input, gate_value, filter_taps, skip_gain, lang_ids, doc_ids, dro_weight):
    tokens = grad_out.shape[1]
    channels = grad_out.shape[2]
    pieces = lax.axis_size("ctx")
    members = lax.axis_size("dp")
    length = tokens * pieces
    span = channels // pieces
    mean_len = length / NDOCS
    own = lax.axis_index("ctx")
    ahead, behind = inner_tables(pieces, tokens)
    outer, inverse = outer_tables(pieces)
    skip = lax.dynamic_slice_in_dim(skip_gain, own * span, span)[None, :]
    exchange = functools.partial(
        lax.all_to_all, axis_name="ctx", split_axis=0, concat_axis=0, tiled=True
    )
    tall = places(pieces, tokens, span)[1]
    macs = pieces * (2 * tokens) ** 2 * span

    aligned = span % 128 == 0
    dma = pltpu.SemaphoreType.DMA
    groups = 4
    message = call(
        functools.partial(prep_copy_kernel if aligned else prep_kernel, pieces, span),
        jax.ShapeDtypeStruct((pieces, span + tall + ROWS, tokens), bf16),
        [HBM] * 4 + [VMEM] * 2 if aligned else [VMEM] * 6,
        [
            pltpu.VMEM((2, tokens, channels), bf16),
            pltpu.VMEM((pieces, tokens, span), bf16),
            pltpu.VMEM((pieces, ROWS, tokens), bf16),
            dma((2, groups)),
            dma((pieces + 2,)),
            dma((groups,)),
        ]
        if aligned
        else (),
        outs=HBM if aligned else VMEM,
        room=(256 << 10) if aligned else (40 << 20),
        cost=(0, 4 << 20),
    )(
        saved_input[0],
        grad_out[0],
        gate_value[0],
        filter_taps.reshape(pieces, span, tokens) if aligned else filter_taps,
        doc_ids,
        lang_ids,
    )
    message = exchange(message)
    message, cross, scale = call(
        functools.partial(conv_kernel, mean_len),
        (
            jax.ShapeDtypeStruct((pieces, tall, tokens), bf16),
            jax.ShapeDtypeStruct((pieces, 2 * tokens, span), bf16),
            jax.ShapeDtypeStruct((tokens, pieces), f32),
        ),
        [VMEM, VMEM, SMEM, HBM, HBM, HBM, HBM],
        [
            pltpu.VMEM(ahead.shape, bf16),
            pltpu.VMEM(behind.shape, bf16),
            pltpu.VMEM(outer.shape, bf16),
            pltpu.VMEM(inverse.shape, bf16),
            pltpu.VMEM((pieces, tall, tokens), bf16),
            pltpu.VMEM((pieces, 2 * tokens, span), bf16),
            pltpu.VMEM((pieces, tokens, span), bf16),
            pltpu.VMEM((pieces, span, 2 * tokens), bf16),
            pltpu.VMEM((pieces, 2 * tokens, 2 * span), bf16),
            pltpu.VMEM((pieces, 2 * tokens, 2 * span), bf16),
            pltpu.VMEM((pieces, tokens), f32),
            pltpu.VMEM((pieces, tokens), f32),
            dma((4,)),
            dma((2,)),
        ],
        outs=(HBM, HBM, VMEM),
        room=(2 << 20) if aligned else (16 << 20),
        cost=(10 * macs, 8 << 20),
    )(message, skip, dro_weight, ahead, behind, outer, inverse)
    message = exchange(message)
    keep, send = call(
        lags_kernel,
        (
            jax.ShapeDtypeStruct((span, length // members), f32),
            jax.ShapeDtypeStruct((members - 1, span, length // members), bf16),
        ),
        [SMEM, VMEM, VMEM],
        [
            pltpu.VMEM((pieces, 2 * tokens, span), f32),
            pltpu.VMEM((pieces, tokens, span), f32),
        ],
        cost=(2 * macs, 6 << 20),
    )(lax.axis_index("dp").reshape(1), cross, behind)
    d_filter = keep
    for r in range(1, members):
        ring = [(d, (d + r) % members) for d in range(members)]
        d_filter = d_filter + lax.ppermute(send[r - 1], "dp", ring).astype(f32)
    token_block = jax.ShapeDtypeStruct((tokens, channels), bf16)
    d_gate, d_input = call(
        final_copy_kernel if aligned else final_kernel,
        (token_block, token_block),
        [SMEM, HBM if aligned else VMEM, VMEM, VMEM],
        [
            pltpu.VMEM((tokens, channels), bf16),
            pltpu.VMEM((tokens, channels), bf16),
            dma((3,)),
            dma((pieces,)),
        ]
        if aligned
        else (),
        outs=(HBM, HBM) if aligned else (VMEM, VMEM),
        room=(5 << 18) if aligned else (40 << 20),
        cost=(0, 4 << 20),
    )(own.reshape(1), grad_out[0], scale, message)
    return (d_input[None], d_gate[None], d_filter)


def solution(mesh):
    return jax.shard_map(
        local,
        mesh=mesh,
        in_specs=(
            P("dp", "ctx", None),
            P("dp", "ctx", None),
            P("dp", "ctx", None),
            P(None, "ctx"),
            P(),
            P("dp", "ctx"),
            P("dp", "ctx"),
            P(),
        ),
        out_specs=(P("dp", "ctx", None), P("dp", "ctx", None), P("ctx", "dp")),
        check_vma=False,
    )
```

```python
import functools
import math

import jax
import jax.numpy as jnp
import numpy as np
from jax import lax
from jax.experimental import pallas as pl
from jax.experimental.pallas import tpu as pltpu
from jax.sharding import PartitionSpec as P

NDOCS = 32
ROWS = 16
VMEM = pl.BlockSpec(memory_space=pltpu.VMEM)
HBM = pl.BlockSpec(memory_space=pltpu.HBM)
SMEM = pl.BlockSpec(memory_space=pltpu.SMEM)
f32 = jnp.float32
bf16 = jnp.bfloat16


def inner_tables(pieces, tokens):
    size = 2 * pieces * tokens
    m = np.arange(pieces)[:, None, None]
    k = np.arange(tokens)[None, :, None]
    q = np.arange(tokens)[None, None, :]
    turn = (q * (4 * m + 1 + 4 * pieces * k)) % (2 * size)
    angle = math.pi / size * turn
    cos, sin = np.cos(angle), np.sin(angle)
    ahead = np.concatenate(
        [np.concatenate([cos, sin], axis=2), np.concatenate([-sin, cos], axis=2)], axis=1
    )
    behind = np.swapaxes(ahead, 1, 2) * (2.0 / size)
    return jnp.asarray(ahead, bf16), jnp.asarray(behind, bf16)


def outer_tables(pieces):
    m = np.arange(pieces)[:, None]
    j = np.arange(pieces)[None, :]
    angle = math.pi / (2 * pieces) * (j * (4 * m + 1) % (4 * pieces))
    both = np.stack([np.cos(angle), -np.sin(angle)], axis=1).reshape(2 * pieces, pieces)
    ahead = np.kron(both, np.eye(ROWS))
    return jnp.asarray(ahead, bf16), jnp.asarray(ahead.T, bf16)


def turned(value, turns):
    re, im = value
    turns = turns % 1.0
    if turns == 0.0:
        return value
    if turns == 0.25:
        return (-im, re)
    if turns == 0.5:
        return (-re, -im)
    if turns == 0.75:
        return (im, -re)
    cos, sin = math.cos(2.0 * math.pi * turns), math.sin(2.0 * math.pi * turns)
    if (turns * 8.0) % 1.0 == 0.0:
        root = math.sqrt(0.5)
        plus, minus = (re + im) * root, (re - im) * root
        if turns == 0.125:
            return (minus, plus)
        if turns == 0.375:
            return (-plus, minus)
        if turns == 0.625:
            return (-minus, -plus)
        return (plus, -minus)
    return (re * cos - im * sin, re * sin + im * cos)


def dft(values, sign):
    count = len(values)
    if count == 1:
        return values
    even, odd = dft(values[0::2], sign), dft(values[1::2], sign)
    first, second = [], []
    for k in range(count // 2):
        a, b = even[k], turned(odd[k], sign * k / count)
        first.append((a[0] + b[0], a[1] + b[1]))
        second.append((a[0] - b[0], a[1] - b[1]))
    return first + second


def outer_inverse(values):
    count = len(values)
    out = []
    for j, (re, im) in enumerate(dft(values, 1.0)):
        angle = math.pi * j / (2 * count)
        out.append(re if j == 0 else re * math.cos(angle) - im * math.sin(angle))
    return out


def chunked(total, body, unrolled=False):
    if unrolled:
        for i in range(total // ROWS):
            body(i * ROWS)
        return

    def step(i, carry):
        body(pl.multiple_of(i * ROWS, ROWS))
        return carry

    lax.fori_loop(0, total // ROWS, step, 0)


def each_piece(pieces, body, group=4):
    def step(i, carry):
        for g in range(group):
            body(i * group + g)
        return carry

    lax.fori_loop(0, pieces // group, step, 0)


def dot(a, b):
    return lax.dot_general(a, b, (((1,), (0,)), ((), ())), preferred_element_type=f32)


def places(pieces, tokens, span):
    beside = max(1, tokens // span)

    def place(index, start):
        row = start + (index // beside) * tokens
        column = (index % beside) * span
        return row, slice(column, column + span)

    tall = -(-2 // beside) * tokens
    return place, tall


def copies(*pairs):
    started = [pltpu.make_async_copy(*pair) for pair in pairs]
    for copy in started:
        copy.start()
    return started


def finish(*started):
    for copy in started:
        copy.wait()


def row_copies(source, target, sems):
    count = sems.shape[0]
    group = source.shape[0] // count
    rows = [pl.ds(g * group, group) for g in range(count)]
    return copies(*[(source.at[r], target.at[r], sems.at[g]) for g, r in enumerate(rows)])


def partner(own_ref, r):
    return jnp.bitwise_xor(own_ref[0], r)


def collect(own_ref, chunk_refs, held_ref, sems):
    return copies(
        *[(c, held_ref.at[partner(own_ref, r)], sems.at[r]) for r, c in enumerate(chunk_refs)]
    )


def hand_out(own_ref, held_ref, chunk_refs, sems):
    return copies(
        *[(held_ref.at[partner(own_ref, r)], c, sems.at[r]) for r, c in enumerate(chunk_refs)]
    )


def prep_kernel(
    pieces, span, own_ref, input_hbm, grad_hbm, gate_hbm, taps_hbm, doc_ref, lang_ref, *refs
):
    outs, (input_ref, grad_ref, gate_ref, made_ref, in_sem, taps_sem, out_sem) = (
        refs[:pieces],
        refs[pieces:],
    )
    tokens = grad_ref.shape[0]
    groups = in_sem.shape[1]
    place, tall = places(pieces, tokens, span)
    taps_in = copies((taps_hbm, made_ref.at[:, pl.ds(0, span), :], taps_sem.at[0]))
    grad_in = row_copies(grad_hbm, grad_ref, in_sem.at[0])
    gate_in = row_copies(gate_hbm, gate_ref, in_sem.at[1])
    input_in = row_copies(input_hbm, input_ref, in_sem.at[2])
    tile = lax.broadcasted_iota(jnp.int32, (ROWS, tokens), 0)
    ids = jnp.where(tile == 0, doc_ref[...], lang_ref[...]).astype(f32).astype(bf16)
    for i in range(pieces):
        made_ref[i, span + tall :, :] = ids
    in_row, in_lanes = place(0, span)
    grad_row, grad_lanes = place(1, span)
    group = tokens // groups
    for g in range(groups):
        finish(grad_in[g], gate_in[g])
        rows = slice(g * group, (g + 1) * group)
        at = slice(grad_row + g * group, grad_row + (g + 1) * group)
        for i in range(pieces):
            part = slice(i * span, (i + 1) * span)
            made_ref[i, at, grad_lanes] = (
                grad_ref[rows, part].astype(f32) * gate_ref[rows, part].astype(f32)
            ).astype(bf16)
    for g in range(groups):
        finish(input_in[g])
        rows = slice(g * group, (g + 1) * group)
        at = slice(in_row + g * group, in_row + (g + 1) * group)
        for i in range(pieces):
            made_ref[i, at, in_lanes] = input_ref[rows, i * span : (i + 1) * span]
    finish(*taps_in)
    finish(*hand_out(own_ref, made_ref, outs, out_sem))


def token_scale(message_ref, scale_ref, dro_ref, ids, mean_len, doc_ref, lang_ref):
    for j in range(message_ref.shape[0]):
        rows = message_ref[j, ids:, :].astype(f32)
        doc_ref[j : j + 1, :] = rows[0:1]
        lang_ref[j : j + 1, :] = rows[1:2]
    docs, langs = doc_ref[...], lang_ref[...]
    doc_len = jnp.zeros_like(docs)
    for d in range(NDOCS):
        hot = (docs == float(d)).astype(f32)
        doc_len = doc_len + hot * jnp.sum(hot, axis=(0, 1), keepdims=True)
    weight = jnp.zeros_like(langs)
    for g in range(dro_ref.shape[0]):
        weight = jnp.where(langs == float(g), dro_ref[g], weight)
    scale_ref[...] = (weight * (2.0 * mean_len) / (doc_len + mean_len)).T


def conv_kernel(
    mean_len,
    pieces,
    own_ref,
    dro_ref,
    skip_ref,
    ahead_hbm,
    behind_hbm,
    outer_hbm,
    inverse_hbm,
    *refs,
):
    chunks, outs = refs[:pieces], refs[pieces : 2 * pieces]
    (
        cross_hbm,
        scale_ref,
        message_ref,
        ahead_ref,
        behind_ref,
        outer_ref,
        inverse_ref,
        out_ref,
        cross_ref,
        scaled_ref,
        taps_mid_ref,
        mid_ref,
        back_ref,
        doc_ref,
        lang_ref,
        table_sem,
        outer_sem,
        cross_sem,
        chunk_sem,
        out_sem,
    ) = refs[2 * pieces :]
    tokens = message_ref.shape[2]
    span = skip_ref.shape[1]
    place, tall = places(pieces, tokens, span)
    chunks_in = collect(own_ref, chunks, message_ref, chunk_sem)
    outer_in = copies((outer_hbm, outer_ref, outer_sem.at[0]))
    ahead_in = row_copies(ahead_hbm, ahead_ref, table_sem.at[0])
    behind_in = row_copies(behind_hbm, behind_ref, table_sem.at[1])
    inverse_in = copies((inverse_hbm, inverse_ref, outer_sem.at[1]))
    finish(*chunks_in)
    token_scale(message_ref, scale_ref, dro_ref, span + tall, mean_len, doc_ref, lang_ref)
    finish(*outer_in)

    def outer_taps(row):
        rows = pl.ds(row, ROWS)
        stack = jnp.concatenate([message_ref[j, rows, :] for j in range(pieces)], axis=0)
        out = dot(outer_ref[...], stack).astype(bf16)
        for m in range(pieces):
            at = 2 * m * ROWS
            taps_mid_ref[m, rows, :tokens] = out[at : at + ROWS]
            taps_mid_ref[m, rows, tokens:] = out[at + ROWS : at + 2 * ROWS]

    chunked(span, outer_taps, True)
    sides = (slice(0, span), slice(span, 2 * span))

    def load(side, j, row):
        start, lanes = place(side, span)
        return message_ref[j, pl.ds(start + row, ROWS), lanes]

    def outer(row):
        rows = pl.ds(row, ROWS)
        stack = []
        for j in range(pieces):
            scaled = (load(1, j, row).astype(f32) * scale_ref[rows, j : j + 1]).astype(bf16)
            scaled_ref[j, rows, :] = scaled
            stack.append(jnp.concatenate([load(0, j, row), scaled], axis=1))
        out = dot(outer_ref[...], jnp.concatenate(stack, axis=0)).astype(bf16)
        for m in range(pieces):
            at = 2 * m * ROWS
            mid_ref[m, rows, :] = out[at : at + ROWS]
            mid_ref[m, pl.ds(tokens + row, ROWS), :] = out[at + ROWS : at + 2 * ROWS]

    chunked(tokens, outer, True)
    finish(*ahead_in, *behind_in)

    def inner(m):
        filt = lax.dot_general(
            ahead_ref[m], taps_mid_ref[m], (((1,), (1,)), ((), ())), preferred_element_type=f32
        )
        spec = dot(ahead_ref[m], mid_ref[m])
        fre, fim = filt[:tokens], filt[tokens:]
        xre, xim = spec[:tokens, sides[0]], spec[tokens:, sides[0]]
        gre, gim = spec[:tokens, sides[1]], spec[tokens:, sides[1]]
        cross_ref[m, :tokens, :] = (xre * gre + xim * gim).astype(bf16)
        cross_ref[m, tokens:, :] = (xre * gim - xim * gre).astype(bf16)
        mixed = jnp.concatenate([fre * xre - fim * xim, fre * xim + fim * xre], axis=0)
        back = jnp.concatenate([fre * gre + fim * gim, fre * gim - fim * gre], axis=0)
        both = jnp.concatenate([mixed.astype(bf16), back.astype(bf16)], axis=1)
        back_ref[m] = dot(behind_ref[m], both).astype(bf16)

    each_piece(pieces, inner, 8)
    cross_out = copies((cross_ref, cross_hbm, cross_sem.at[0]))
    finish(*inverse_in)
    skip = skip_ref[...]

    def outer_back(row):
        rows = pl.ds(row, ROWS)
        stack = []
        for m in range(pieces):
            stack += [back_ref[m, rows, :], back_ref[m, pl.ds(tokens + row, ROWS), :]]
        out = dot(inverse_ref[...], jnp.concatenate(stack, axis=0))
        for j in range(pieces):
            at = slice(j * ROWS, (j + 1) * ROWS)
            for side in (0, 1):
                start, lanes = place(side, 0)
                own = load(0, j, row) if side == 0 else scaled_ref[j, rows, :]
                out_ref[j, pl.ds(start + row, ROWS), lanes] = (
                    out[at, sides[side]] + skip * own.astype(f32)
                ).astype(bf16)

    chunked(tokens, outer_back, True)
    finish(*cross_out, *hand_out(own_ref, out_ref, outs, out_sem))


def lags_kernel(own_ref, cross_ref, behind_ref, keep_ref, send_ref, back_ref, lag_ref):
    pieces, tall, span = cross_ref.shape
    tokens = tall // 2
    held = keep_ref.shape[1] // tokens
    members = pieces // held

    def inner(m):
        back_ref[m] = dot(behind_ref[m], cross_ref[m])

    each_piece(pieces, inner)

    def body(row):
        out = outer_inverse(
            [
                (back_ref[m, pl.ds(row, ROWS), :], back_ref[m, pl.ds(tokens + row, ROWS), :])
                for m in range(pieces)
            ]
        )
        for j in range(pieces):
            lag_ref[j, pl.ds(row, ROWS), :] = out[j]

    chunked(tokens, body)
    for j in range(held):
        part = slice(j * tokens, (j + 1) * tokens)
        keep_ref[:, part] = lag_ref[own_ref[0] * held + j].T
        for r in range(1, members):
            other = lax.rem(own_ref[0] + r, members)
            send_ref[r - 1, :, part] = lag_ref[other * held + j].T.astype(bf16)


def own_scale(own_ref, scale_ref):
    lane = lax.broadcasted_iota(jnp.int32, scale_ref.shape, 1)
    scale = jnp.where(lane == own_ref[0], scale_ref[...], jnp.zeros(scale_ref.shape, f32))
    return jnp.sum(scale, axis=1, keepdims=True)


def final_kernel(pieces, own_ref, grad_hbm, scale_ref, *refs):
    chunks = refs[:pieces]
    (
        gate_hbm,
        input_hbm,
        message_ref,
        grad_ref,
        gate_ref,
        input_ref,
        chunk_sem,
        grad_sem,
        out_sem,
    ) = refs[pieces:]
    tokens, channels = grad_ref.shape
    span = channels // pieces
    groups = grad_sem.shape[0]
    group = tokens // groups
    place, _ = places(pieces, tokens, span)
    chunks_in = collect(own_ref, chunks, message_ref, chunk_sem)
    grad_in = row_copies(grad_hbm, grad_ref, grad_sem)
    scale = own_scale(own_ref, scale_ref)
    mixed_row, mixed_lanes = place(0, 0)
    back_row, back_lanes = place(1, 0)
    finish(*chunks_in)
    sent = []
    for g in range(groups):
        finish(grad_in[g])
        rows = slice(g * group, (g + 1) * group)
        for i in range(pieces):
            part = slice(i * span, (i + 1) * span)
            start = mixed_row + g * group
            mixed = message_ref[i, start : start + group, mixed_lanes].astype(f32)
            gate_ref[rows, part] = (
                grad_ref[rows, part].astype(f32) * scale[rows] * mixed
            ).astype(bf16)
            start = back_row + g * group
            input_ref[rows, part] = message_ref[i, start : start + group, back_lanes]
        rows = pl.ds(g * group, group)
        sent += copies(
            (gate_ref.at[rows], gate_hbm.at[rows], out_sem.at[0, g]),
            (input_ref.at[rows], input_hbm.at[rows], out_sem.at[1, g]),
        )
    finish(*sent)


def call(kernel, out, ins, scratch=(), outs=None, room=40 << 20, cost=(0, 0)):
    return pl.pallas_call(
        kernel,
        out_shape=out,
        in_specs=ins,
        out_specs=jax.tree.map(lambda _: VMEM, out) if outs is None else outs,
        scratch_shapes=scratch,
        compiler_params=pltpu.CompilerParams(vmem_limit_bytes=(64 << 20) - room),
        cost_estimate=pl.CostEstimate(flops=cost[0], bytes_accessed=cost[1], transcendentals=0),
    )


def local(grad_out, saved_input, gate_value, filter_taps, skip_gain, lang_ids, doc_ids, dro_weight):
    tokens = grad_out.shape[1]
    channels = grad_out.shape[2]
    pieces = lax.axis_size("ctx")
    members = lax.axis_size("dp")
    length = tokens * pieces
    span = channels // pieces
    mean_len = length / NDOCS
    place = lax.axis_index("ctx")
    own = place.reshape(1)
    ahead, behind = inner_tables(pieces, tokens)
    outer, inverse = outer_tables(pieces)
    skip = lax.dynamic_slice_in_dim(skip_gain, place * span, span)[None, :]
    def exchange(chunks):
        half = pieces // 2
        far = [half + (r >> 1) + (r & 1) * (half // 2) for r in range(half)]
        near = list(range(1, half)) + [0]
        order = [r for pair in zip(far, near) for r in pair]
        got = {0: chunks[0]}
        for r in order:
            if r:
                pairs = [(i, i ^ r) for i in range(pieces)]
                got[r] = lax.ppermute(chunks[r], "ctx", pairs)
        return [got[r] for r in range(pieces)]

    shape = jax.ShapeDtypeStruct
    dma = pltpu.SemaphoreType.DMA
    tall = places(pieces, tokens, span)[1]
    macs = pieces * (2 * tokens) ** 2 * span
    message = shape((span + tall + ROWS, tokens), bf16)
    answer = shape((tall, tokens), bf16)
    many = [HBM] * pieces
    groups = 4

    chunks = call(
        functools.partial(prep_kernel, pieces, span),
        [message] * pieces,
        [SMEM] + [HBM] * 4 + [VMEM] * 2,
        [
            pltpu.VMEM((tokens, channels), bf16),
            pltpu.VMEM((tokens, channels), bf16),
            pltpu.VMEM((tokens, channels), bf16),
            pltpu.VMEM((pieces,) + message.shape, bf16),
            dma((3, groups)),
            dma((1,)),
            dma((pieces,)),
        ],
        outs=many,
        room=256 << 10,
        cost=(0, 4 << 20),
    )(
        own,
        saved_input[0],
        grad_out[0],
        gate_value[0],
        filter_taps.reshape(pieces, span, tokens),
        doc_ids,
        lang_ids,
    )
    *chunks, cross, scale = call(
        functools.partial(conv_kernel, mean_len, pieces),
        [answer] * pieces
        + [shape((pieces, 2 * tokens, span), bf16), shape((tokens, pieces), f32)],
        [SMEM, SMEM, VMEM] + [HBM] * 4 + many,
        [
            pltpu.VMEM((pieces,) + message.shape, bf16),
            pltpu.VMEM(ahead.shape, bf16),
            pltpu.VMEM(behind.shape, bf16),
            pltpu.VMEM(outer.shape, bf16),
            pltpu.VMEM(inverse.shape, bf16),
            pltpu.VMEM((pieces,) + answer.shape, bf16),
            pltpu.VMEM((pieces, 2 * tokens, span), bf16),
            pltpu.VMEM((pieces, tokens, span), bf16),
            pltpu.VMEM((pieces, span, 2 * tokens), bf16),
            pltpu.VMEM((pieces, 2 * tokens, 2 * span), bf16),
            pltpu.VMEM((pieces, 2 * tokens, 2 * span), bf16),
            pltpu.VMEM((pieces, tokens), f32),
            pltpu.VMEM((pieces, tokens), f32),
            dma((2, groups)),
            dma((2,)),
            dma((1,)),
            dma((pieces,)),
            dma((pieces,)),
        ],
        outs=many + [HBM, VMEM],
        room=2 << 20,
        cost=(10 * macs, 8 << 20),
    )(own, dro_weight, skip, ahead, behind, outer, inverse, *exchange(chunks))
    chunks = exchange(chunks)
    keep, send = call(
        lags_kernel,
        (
            jax.ShapeDtypeStruct((span, length // members), f32),
            jax.ShapeDtypeStruct((members - 1, span, length // members), bf16),
        ),
        [SMEM, VMEM, VMEM],
        [
            pltpu.VMEM((pieces, 2 * tokens, span), f32),
            pltpu.VMEM((pieces, tokens, span), f32),
        ],
        cost=(2 * macs, 6 << 20),
    )(lax.axis_index("dp").reshape(1), cross, behind)
    d_filter = keep
    for r in range(1, members):
        ring = [(d, (d + r) % members) for d in range(members)]
        d_filter = d_filter + lax.ppermute(send[r - 1], "dp", ring).astype(f32)
    token_block = jax.ShapeDtypeStruct((tokens, channels), bf16)
    d_gate, d_input = call(
        functools.partial(final_kernel, pieces),
        (token_block, token_block),
        [SMEM, HBM, VMEM] + many,
        [
            pltpu.VMEM((pieces,) + answer.shape, bf16),
            pltpu.VMEM((tokens, channels), bf16),
            pltpu.VMEM((tokens, channels), bf16),
            pltpu.VMEM((tokens, channels), bf16),
            dma((pieces,)),
            dma((groups,)),
            dma((2, groups)),
        ],
        outs=(HBM, HBM),
        room=5 << 18,
        cost=(0, 4 << 20),
    )(own, grad_out[0], scale, *chunks)
    return (d_input[None], d_gate[None], d_filter)


def solution(mesh):
    return jax.shard_map(
        local,
        mesh=mesh,
        in_specs=(
            P("dp", "ctx", None),
            P("dp", "ctx", None),
            P("dp", "ctx", None),
            P(None, "ctx"),
            P(),
            P("dp", "ctx"),
            P("dp", "ctx"),
            P(),
        ),
        out_specs=(P("dp", "ctx", None), P("dp", "ctx", None), P("ctx", "dp")),
        check_vma=False,
    )
```

```python
import functools
import math

import jax
import jax.numpy as jnp
import numpy as np
from jax import lax
from jax.experimental import pallas as pl
from jax.experimental.pallas import tpu as pltpu
from jax.sharding import PartitionSpec as P

NDOCS = 32
ROWS = 16
VMEM = pl.BlockSpec(memory_space=pltpu.VMEM)
HBM = pl.BlockSpec(memory_space=pltpu.HBM)
SMEM = pl.BlockSpec(memory_space=pltpu.SMEM)
f32 = jnp.float32
bf16 = jnp.bfloat16


def inner_tables(pieces, tokens):
    size = 2 * pieces * tokens
    m = np.arange(pieces)[:, None, None]
    k = np.arange(tokens)[None, :, None]
    q = np.arange(tokens)[None, None, :]
    turn = (q * (4 * m + 1 + 4 * pieces * k)) % (2 * size)
    angle = math.pi / size * turn
    cos, sin = np.cos(angle), np.sin(angle)
    ahead = np.concatenate(
        [np.concatenate([cos, sin], axis=2), np.concatenate([-sin, cos], axis=2)], axis=1
    )
    behind = np.swapaxes(ahead, 1, 2) * (2.0 / size)
    return jnp.asarray(ahead, bf16), jnp.asarray(behind, bf16)


def outer_tables(pieces):
    m = np.arange(pieces)[:, None]
    j = np.arange(pieces)[None, :]
    angle = math.pi / (2 * pieces) * (j * (4 * m + 1) % (4 * pieces))
    both = np.stack([np.cos(angle), -np.sin(angle)], axis=1).reshape(2 * pieces, pieces)
    ahead = np.kron(both, np.eye(ROWS))
    return jnp.asarray(ahead, bf16), jnp.asarray(ahead.T, bf16)


def turned(value, turns):
    re, im = value
    turns = turns % 1.0
    if turns == 0.0:
        return value
    if turns == 0.25:
        return (-im, re)
    if turns == 0.5:
        return (-re, -im)
    if turns == 0.75:
        return (im, -re)
    cos, sin = math.cos(2.0 * math.pi * turns), math.sin(2.0 * math.pi * turns)
    if (turns * 8.0) % 1.0 == 0.0:
        root = math.sqrt(0.5)
        plus, minus = (re + im) * root, (re - im) * root
        if turns == 0.125:
            return (minus, plus)
        if turns == 0.375:
            return (-plus, minus)
        if turns == 0.625:
            return (-minus, -plus)
        return (plus, -minus)
    return (re * cos - im * sin, re * sin + im * cos)


def dft(values, sign):
    count = len(values)
    if count == 1:
        return values
    even, odd = dft(values[0::2], sign), dft(values[1::2], sign)
    first, second = [], []
    for k in range(count // 2):
        a, b = even[k], turned(odd[k], sign * k / count)
        first.append((a[0] + b[0], a[1] + b[1]))
        second.append((a[0] - b[0], a[1] - b[1]))
    return first + second


def outer_inverse(values):
    count = len(values)
    out = []
    for j, (re, im) in enumerate(dft(values, 1.0)):
        angle = math.pi * j / (2 * count)
        out.append(re if j == 0 else re * math.cos(angle) - im * math.sin(angle))
    return out


def chunked(total, body, unrolled=False):
    if unrolled:
        for i in range(total // ROWS):
            body(i * ROWS)
        return

    def step(i, carry):
        body(pl.multiple_of(i * ROWS, ROWS))
        return carry

    lax.fori_loop(0, total // ROWS, step, 0)


def each_piece(pieces, body, group=4):
    if group == pieces:
        for m in range(pieces):
            body(m)
        return

    def step(i, carry):
        for g in range(group):
            body(i * group + g)
        return carry

    lax.fori_loop(0, pieces // group, step, 0)


def dot(a, b):
    return lax.dot_general(a, b, (((1,), (0,)), ((), ())), preferred_element_type=f32)


def places(pieces, tokens, span):
    beside = max(1, tokens // span)

    def place(index, start):
        row = start + (index // beside) * tokens
        column = (index % beside) * span
        return row, slice(column, column + span)

    tall = -(-2 // beside) * tokens
    return place, tall


def copies(*pairs):
    started = [pltpu.make_async_copy(*pair) for pair in pairs]
    for copy in started:
        copy.start()
    return started


def finish(*started):
    for copy in started:
        copy.wait()


def row_copies(source, target, sems):
    count = sems.shape[0]
    group = source.shape[0] // count
    rows = [pl.ds(g * group, group) for g in range(count)]
    return copies(*[(source.at[r], target.at[r], sems.at[g]) for g, r in enumerate(rows)])


def prep_kernel(
    pieces,
    span,
    input_hbm,
    grad_hbm,
    gate_hbm,
    taps_hbm,
    doc_ref,
    lang_ref,
    out_hbm,
    input_ref,
    grad_ref,
    gate_ref,
    made_ref,
    in_sem,
    taps_sem,
    out_sem,
):
    tokens = grad_ref.shape[0]
    groups = in_sem.shape[1]
    place, tall = places(pieces, tokens, span)
    in_row, in_lanes = place(0, span)
    grad_row, grad_lanes = place(1, span)

    def send(part, start, size):
        rows = pl.ds(start, size)
        return copies((made_ref.at[:, rows, :], out_hbm.at[:, rows, :], out_sem.at[part]))

    input_in = row_copies(input_hbm, input_ref, in_sem.at[2])
    grad_in = row_copies(grad_hbm, grad_ref, in_sem.at[0])
    gate_in = row_copies(gate_hbm, gate_ref, in_sem.at[1])
    taps_in = copies((taps_hbm, made_ref.at[:, pl.ds(0, span), :], taps_sem.at[0]))
    tile = lax.broadcasted_iota(jnp.int32, (ROWS, tokens), 0)
    ids = jnp.where(tile == 0, doc_ref[...], lang_ref[...]).astype(f32).astype(bf16)
    for i in range(pieces):
        made_ref[i, span + tall :, :] = ids
    group = tokens // groups
    sent = []
    for g in range(groups):
        finish(input_in[g])
        rows = slice(g * group, (g + 1) * group)
        at = slice(in_row + g * group, in_row + (g + 1) * group)
        for i in range(pieces):
            made_ref[i, at, in_lanes] = input_ref[rows, i * span : (i + 1) * span]
    finish(*taps_in)
    sent += send(0, 0, span if grad_row == in_row else grad_row)
    for g in range(groups):
        finish(grad_in[g], gate_in[g])
        rows = slice(g * group, (g + 1) * group)
        at = slice(grad_row + g * group, grad_row + (g + 1) * group)
        for i in range(pieces):
            part = slice(i * span, (i + 1) * span)
            made_ref[i, at, grad_lanes] = (
                grad_ref[rows, part].astype(f32) * gate_ref[rows, part].astype(f32)
            ).astype(bf16)
        if g == groups // 2 - 1:
            sent += send(1, grad_row, (g + 1) * group)
    start = grad_row + tokens // 2
    sent += send(2, start, span + tall + ROWS - start)
    finish(*sent)


def token_scale(message_ref, scale_ref, dro_ref, ids, mean_len, doc_ref, lang_ref):
    for j in range(message_ref.shape[0]):
        rows = message_ref[j, ids:, :].astype(f32)
        doc_ref[j : j + 1, :] = rows[0:1]
        lang_ref[j : j + 1, :] = rows[1:2]
    docs, langs = doc_ref[...], lang_ref[...]
    doc_len = jnp.zeros_like(docs)
    for d in range(NDOCS):
        hot = (docs == float(d)).astype(f32)
        doc_len = doc_len + hot * jnp.sum(hot, axis=(0, 1), keepdims=True)
    weight = jnp.zeros_like(langs)
    for g in range(dro_ref.shape[0]):
        weight = jnp.where(langs == float(g), dro_ref[g], weight)
    scale_ref[...] = (weight * (2.0 * mean_len) / (doc_len + mean_len)).T


def conv_kernel(
    mean_len,
    message_ref,
    dro_ref,
    skip_ref,
    ahead_hbm,
    behind_hbm,
    outer_hbm,
    inverse_hbm,
    out_hbm,
    cross_hbm,
    scale_ref,
    ahead_ref,
    behind_ref,
    outer_ref,
    inverse_ref,
    out_ref,
    cross_ref,
    scaled_ref,
    taps_mid_ref,
    mid_ref,
    back_ref,
    doc_ref,
    lang_ref,
    table_sem,
    outer_sem,
    cross_sem,
    out_sem,
):
    pieces = message_ref.shape[0]
    tokens = message_ref.shape[2]
    span = skip_ref.shape[1]
    place, tall = places(pieces, tokens, span)
    outer_in = copies((outer_hbm, outer_ref, outer_sem.at[0]))
    ahead_in = row_copies(ahead_hbm, ahead_ref, table_sem.at[0])
    behind_in = row_copies(behind_hbm, behind_ref, table_sem.at[1])
    inverse_in = copies((inverse_hbm, inverse_ref, outer_sem.at[1]))
    token_scale(message_ref, scale_ref, dro_ref, span + tall, mean_len, doc_ref, lang_ref)
    finish(*outer_in)

    def outer_taps(row):
        rows = pl.ds(row, ROWS)
        stack = jnp.concatenate([message_ref[j, rows, :] for j in range(pieces)], axis=0)
        out = dot(outer_ref[...], stack).astype(bf16)
        for m in range(pieces):
            at = 2 * m * ROWS
            taps_mid_ref[m, rows, :tokens] = out[at : at + ROWS]
            taps_mid_ref[m, rows, tokens:] = out[at + ROWS : at + 2 * ROWS]

    chunked(span, outer_taps, True)
    sides = (slice(0, span), slice(span, 2 * span))

    def load(side, j, row):
        start, lanes = place(side, span)
        return message_ref[j, pl.ds(start + row, ROWS), lanes]

    def outer(row):
        rows = pl.ds(row, ROWS)
        stack = []
        for j in range(pieces):
            scaled = (load(1, j, row).astype(f32) * scale_ref[rows, j : j + 1]).astype(bf16)
            scaled_ref[j, rows, :] = scaled
            stack.append(jnp.concatenate([load(0, j, row), scaled], axis=1))
        out = dot(outer_ref[...], jnp.concatenate(stack, axis=0)).astype(bf16)
        for m in range(pieces):
            at = 2 * m * ROWS
            mid_ref[m, rows, :] = out[at : at + ROWS]
            mid_ref[m, pl.ds(tokens + row, ROWS), :] = out[at + ROWS : at + 2 * ROWS]

    chunked(tokens, outer, True)
    finish(*ahead_in, *behind_in)

    def inner(m):
        filt = lax.dot_general(
            ahead_ref[m], taps_mid_ref[m], (((1,), (1,)), ((), ())), preferred_element_type=f32
        )
        spec = dot(ahead_ref[m], mid_ref[m])
        fre, fim = filt[:tokens], filt[tokens:]
        xre, xim = spec[:tokens, sides[0]], spec[tokens:, sides[0]]
        gre, gim = spec[:tokens, sides[1]], spec[tokens:, sides[1]]
        cross_ref[m, :tokens, :] = (xre * gre + xim * gim).astype(bf16)
        cross_ref[m, tokens:, :] = (xre * gim - xim * gre).astype(bf16)
        mixed = jnp.concatenate([fre * xre - fim * xim, fre * xim + fim * xre], axis=0)
        back = jnp.concatenate([fre * gre + fim * gim, fre * gim - fim * gre], axis=0)
        both = jnp.concatenate([mixed.astype(bf16), back.astype(bf16)], axis=1)
        back_ref[m] = dot(behind_ref[m], both).astype(bf16)

    each_piece(pieces, inner, pieces)
    cross_out = copies((cross_ref, cross_hbm, cross_sem.at[0]))
    finish(*inverse_in)
    skip = skip_ref[...]

    def outer_back(row):
        rows = pl.ds(row, ROWS)
        stack = []
        for m in range(pieces):
            stack += [back_ref[m, rows, :], back_ref[m, pl.ds(tokens + row, ROWS), :]]
        out = dot(inverse_ref[...], jnp.concatenate(stack, axis=0))
        for j in range(pieces):
            at = slice(j * ROWS, (j + 1) * ROWS)
            for side in (0, 1):
                start, lanes = place(side, 0)
                own = load(0, j, row) if side == 0 else scaled_ref[j, rows, :]
                out_ref[j, pl.ds(start + row, ROWS), lanes] = (
                    out[at, sides[side]] + skip * own.astype(f32)
                ).astype(bf16)

    chunked(tokens, outer_back, True)
    finish(*cross_out, *row_copies(out_ref, out_hbm, out_sem))


def lags_kernel(own_ref, cross_ref, behind_ref, keep_ref, send_ref, back_ref, lag_ref):
    pieces, tall, span = cross_ref.shape
    tokens = tall // 2
    held = keep_ref.shape[1] // tokens
    members = pieces // held

    def inner(m):
        back_ref[m] = dot(behind_ref[m], cross_ref[m])

    each_piece(pieces, inner)

    def body(row):
        out = outer_inverse(
            [
                (back_ref[m, pl.ds(row, ROWS), :], back_ref[m, pl.ds(tokens + row, ROWS), :])
                for m in range(pieces)
            ]
        )
        for j in range(pieces):
            lag_ref[j, pl.ds(row, ROWS), :] = out[j]

    chunked(tokens, body)
    for j in range(held):
        part = slice(j * tokens, (j + 1) * tokens)
        keep_ref[:, part] = lag_ref[own_ref[0] * held + j].T
        for r in range(1, members):
            other = lax.rem(own_ref[0] + r, members)
            send_ref[r - 1, :, part] = lag_ref[other * held + j].T.astype(bf16)


def own_scale(own_ref, scale_ref):
    lane = lax.broadcasted_iota(jnp.int32, scale_ref.shape, 1)
    scale = jnp.where(lane == own_ref[0], scale_ref[...], jnp.zeros(scale_ref.shape, f32))
    return jnp.sum(scale, axis=1, keepdims=True)


def final_kernel(
    own_ref,
    grad_hbm,
    scale_ref,
    message_ref,
    gate_hbm,
    input_hbm,
    grad_ref,
    gate_ref,
    input_ref,
    grad_sem,
    out_sem,
):
    pieces = message_ref.shape[0]
    tokens, channels = grad_ref.shape
    span = channels // pieces
    groups = grad_sem.shape[0]
    group = tokens // groups
    place, _ = places(pieces, tokens, span)
    grad_in = row_copies(grad_hbm, grad_ref, grad_sem)
    mixed_row, mixed_lanes = place(0, 0)
    back_row, back_lanes = place(1, 0)
    sent = []
    for g in range(groups):
        rows = slice(g * group, (g + 1) * group)
        for i in range(pieces):
            start = back_row + g * group
            input_ref[rows, i * span : (i + 1) * span] = message_ref[
                i, start : start + group, back_lanes
            ]
        rows = pl.ds(g * group, group)
        sent += copies((input_ref.at[rows], input_hbm.at[rows], out_sem.at[1, g]))
    scale = own_scale(own_ref, scale_ref)
    for g in range(groups):
        finish(grad_in[g])
        rows = slice(g * group, (g + 1) * group)
        for i in range(pieces):
            part = slice(i * span, (i + 1) * span)
            start = mixed_row + g * group
            mixed = message_ref[i, start : start + group, mixed_lanes].astype(f32)
            gate_ref[rows, part] = (
                grad_ref[rows, part].astype(f32) * scale[rows] * mixed
            ).astype(bf16)
        rows = pl.ds(g * group, group)
        sent += copies((gate_ref.at[rows], gate_hbm.at[rows], out_sem.at[0, g]))
    finish(*sent)


def call(kernel, out, ins, scratch=(), outs=None, room=40 << 20, cost=(0, 0)):
    return pl.pallas_call(
        kernel,
        out_shape=out,
        in_specs=ins,
        out_specs=jax.tree.map(lambda _: VMEM, out) if outs is None else outs,
        scratch_shapes=scratch,
        compiler_params=pltpu.CompilerParams(vmem_limit_bytes=(64 << 20) - room),
        cost_estimate=pl.CostEstimate(flops=cost[0], bytes_accessed=cost[1], transcendentals=0),
    )


def local(grad_out, saved_input, gate_value, filter_taps, skip_gain, lang_ids, doc_ids, dro_weight):
    tokens = grad_out.shape[1]
    channels = grad_out.shape[2]
    pieces = lax.axis_size("ctx")
    members = lax.axis_size("dp")
    length = tokens * pieces
    span = channels // pieces
    mean_len = length / NDOCS
    place = lax.axis_index("ctx")
    own = place.reshape(1)
    ahead, behind = inner_tables(pieces, tokens)
    outer, inverse = outer_tables(pieces)
    skip = lax.dynamic_slice_in_dim(skip_gain, place * span, span)[None, :]
    exchange = functools.partial(
        lax.all_to_all, axis_name="ctx", split_axis=0, concat_axis=0, tiled=True
    )
    shape = jax.ShapeDtypeStruct
    dma = pltpu.SemaphoreType.DMA
    tall = places(pieces, tokens, span)[1]
    macs = pieces * (2 * tokens) ** 2 * span
    message = shape((pieces, span + tall + ROWS, tokens), bf16)
    answer = shape((pieces, tall, tokens), bf16)
    groups = 4

    sent = call(
        functools.partial(prep_kernel, pieces, span),
        message,
        [HBM] * 4 + [VMEM] * 2,
        [
            pltpu.VMEM((tokens, channels), bf16),
            pltpu.VMEM((tokens, channels), bf16),
            pltpu.VMEM((tokens, channels), bf16),
            pltpu.VMEM(message.shape, bf16),
            dma((3, groups)),
            dma((1,)),
            dma((3,)),
        ],
        outs=HBM,
        room=256 << 10,
        cost=(0, 4 << 20),
    )(
        saved_input[0],
        grad_out[0],
        gate_value[0],
        filter_taps.reshape(pieces, span, tokens),
        doc_ids,
        lang_ids,
    )
    sent, cross, scale = call(
        functools.partial(conv_kernel, mean_len),
        [answer, shape((pieces, 2 * tokens, span), bf16), shape((tokens, pieces), f32)],
        [VMEM, SMEM, VMEM] + [HBM] * 4,
        [
            pltpu.VMEM(ahead.shape, bf16),
            pltpu.VMEM(behind.shape, bf16),
            pltpu.VMEM(outer.shape, bf16),
            pltpu.VMEM(inverse.shape, bf16),
            pltpu.VMEM(answer.shape, bf16),
            pltpu.VMEM((pieces, 2 * tokens, span), bf16),
            pltpu.VMEM((pieces, tokens, span), bf16),
            pltpu.VMEM((pieces, span, 2 * tokens), bf16),
            pltpu.VMEM((pieces, 2 * tokens, 2 * span), bf16),
            pltpu.VMEM((pieces, 2 * tokens, 2 * span), bf16),
            pltpu.VMEM((pieces, tokens), f32),
            pltpu.VMEM((pieces, tokens), f32),
            dma((2, groups)),
            dma((2,)),
            dma((1,)),
            dma((groups,)),
        ],
        outs=[HBM, HBM, VMEM],
        room=3 << 20,
        cost=(10 * macs, 8 << 20),
    )(exchange(sent), dro_weight, skip, ahead, behind, outer, inverse)
    got = exchange(sent)
    keep, send = call(
        lags_kernel,
        (
            jax.ShapeDtypeStruct((span, length // members), f32),
            jax.ShapeDtypeStruct((members - 1, span, length // members), bf16),
        ),
        [SMEM, VMEM, VMEM],
        [
            pltpu.VMEM((pieces, 2 * tokens, span), f32),
            pltpu.VMEM((pieces, tokens, span), f32),
        ],
        cost=(2 * macs, 6 << 20),
    )(lax.axis_index("dp").reshape(1), cross, behind)
    d_filter = keep
    for r in range(1, members):
        ring = [(d, (d + r) % members) for d in range(members)]
        d_filter = d_filter + lax.ppermute(send[r - 1], "dp", ring).astype(f32)
    token_block = jax.ShapeDtypeStruct((tokens, channels), bf16)
    d_gate, d_input = call(
        final_kernel,
        (token_block, token_block),
        [SMEM, HBM, VMEM, VMEM],
        [
            pltpu.VMEM((tokens, channels), bf16),
            pltpu.VMEM((tokens, channels), bf16),
            pltpu.VMEM((tokens, channels), bf16),
            dma((groups,)),
            dma((2, groups)),
        ],
        outs=(HBM, HBM),
        room=1450 << 10,
        cost=(0, 4 << 20),
    )(own, grad_out[0], scale, got)
    return (d_input[None], d_gate[None], d_filter)


def solution(mesh):
    return jax.shard_map(
        local,
        mesh=mesh,
        in_specs=(
            P("dp", "ctx", None),
            P("dp", "ctx", None),
            P("dp", "ctx", None),
            P(None, "ctx"),
            P(),
            P("dp", "ctx"),
            P("dp", "ctx"),
            P(),
        ),
        out_specs=(P("dp", "ctx", None), P("dp", "ctx", None), P("ctx", "dp")),
        check_vma=False,
    )
```

```python
import functools
import math

import jax
import jax.numpy as jnp
import numpy as np
from jax import lax
from jax.experimental import pallas as pl
from jax.experimental.pallas import tpu as pltpu
from jax.sharding import PartitionSpec as P

NDOCS = 32
ROWS = 16
VMEM = pl.BlockSpec(memory_space=pltpu.VMEM)
HBM = pl.BlockSpec(memory_space=pltpu.HBM)
SMEM = pl.BlockSpec(memory_space=pltpu.SMEM)
f32 = jnp.float32
bf16 = jnp.bfloat16


def inner_tables(pieces, tokens):
    size = 2 * pieces * tokens
    m = np.arange(pieces)[:, None, None]
    k = np.arange(tokens)[None, :, None]
    q = np.arange(tokens)[None, None, :]
    turn = (q * (4 * m + 1 + 4 * pieces * k)) % (2 * size)
    angle = math.pi / size * turn
    cos, sin = np.cos(angle), np.sin(angle)
    ahead = np.concatenate(
        [np.concatenate([cos, sin], axis=2), np.concatenate([-sin, cos], axis=2)], axis=1
    )
    behind = np.swapaxes(ahead, 1, 2) * (2.0 / size)
    return ahead, behind


def outer_tables(pieces):
    m = np.arange(pieces)[:, None]
    j = np.arange(pieces)[None, :]
    angle = math.pi / (2 * pieces) * (j * (4 * m + 1) % (4 * pieces))
    both = np.stack([np.cos(angle), -np.sin(angle)], axis=1).reshape(2 * pieces, pieces)
    ahead = np.kron(both, np.eye(ROWS))
    return ahead, ahead.T


def side_by_side(table, width):
    return np.concatenate(np.split(table, table.shape[1] // width, axis=1), axis=0)


def all_tables(pieces, tokens):
    width = 2 * tokens
    ahead, behind = inner_tables(pieces, tokens)
    outer, inverse = outer_tables(pieces)
    parts = [
        ahead.reshape(-1, width),
        behind.reshape(-1, width),
        side_by_side(outer, width),
        side_by_side(inverse, width),
    ]
    return jnp.asarray(np.concatenate(parts, axis=0), bf16), jnp.asarray(behind, bf16)


def turned(value, turns):
    re, im = value
    turns = turns % 1.0
    if turns == 0.0:
        return value
    if turns == 0.25:
        return (-im, re)
    if turns == 0.5:
        return (-re, -im)
    if turns == 0.75:
        return (im, -re)
    cos, sin = math.cos(2.0 * math.pi * turns), math.sin(2.0 * math.pi * turns)
    if (turns * 8.0) % 1.0 == 0.0:
        root = math.sqrt(0.5)
        plus, minus = (re + im) * root, (re - im) * root
        if turns == 0.125:
            return (minus, plus)
        if turns == 0.375:
            return (-plus, minus)
        if turns == 0.625:
            return (-minus, -plus)
        return (plus, -minus)
    return (re * cos - im * sin, re * sin + im * cos)


def dft(values, sign):
    count = len(values)
    if count == 1:
        return values
    even, odd = dft(values[0::2], sign), dft(values[1::2], sign)
    first, second = [], []
    for k in range(count // 2):
        a, b = even[k], turned(odd[k], sign * k / count)
        first.append((a[0] + b[0], a[1] + b[1]))
        second.append((a[0] - b[0], a[1] - b[1]))
    return first + second


def outer_inverse(values):
    count = len(values)
    out = []
    for j, (re, im) in enumerate(dft(values, 1.0)):
        angle = math.pi * j / (2 * count)
        out.append(re if j == 0 else re * math.cos(angle) - im * math.sin(angle))
    return out


def chunked(total, body, unrolled=False):
    if unrolled:
        for i in range(total // ROWS):
            body(i * ROWS)
        return

    def step(i, carry):
        body(pl.multiple_of(i * ROWS, ROWS))
        return carry

    lax.fori_loop(0, total // ROWS, step, 0)


def each_piece(pieces, body, group=4):
    if group == pieces:
        for m in range(pieces):
            body(m)
        return

    def step(i, carry):
        for g in range(group):
            body(i * group + g)
        return carry

    lax.fori_loop(0, pieces // group, step, 0)


def dot(a, b):
    return lax.dot_general(a, b, (((1,), (0,)), ((), ())), preferred_element_type=f32)


def places(pieces, tokens, span):
    beside = max(1, tokens // span)

    def place(index, start):
        row = start + (index // beside) * tokens
        column = (index % beside) * span
        return row, slice(column, column + span)

    tall = -(-2 // beside) * tokens
    return place, tall


def copies(*pairs):
    started = [pltpu.make_async_copy(*pair) for pair in pairs]
    for copy in started:
        copy.start()
    return started


def finish(*started):
    for copy in started:
        copy.wait()


def row_copies(source, target, sems):
    count = sems.shape[0]
    group = source.shape[0] // count
    rows = [pl.ds(g * group, group) for g in range(count)]
    return copies(*[(source.at[r], target.at[r], sems.at[g]) for g, r in enumerate(rows)])


def prep_kernel(
    pieces,
    span,
    input_hbm,
    grad_hbm,
    gate_hbm,
    taps_hbm,
    doc_ref,
    lang_ref,
    out_hbm,
    input_ref,
    grad_ref,
    gate_ref,
    made_ref,
    in_sem,
    taps_sem,
    out_sem,
):
    tokens = grad_ref.shape[0]
    groups = in_sem.shape[1]
    place, tall = places(pieces, tokens, span)
    in_row, in_lanes = place(0, span)
    grad_row, grad_lanes = place(1, span)

    def send(part, start, size):
        rows = pl.ds(start, size)
        return copies((made_ref.at[:, rows, :], out_hbm.at[:, rows, :], out_sem.at[part]))

    input_in = row_copies(input_hbm, input_ref, in_sem.at[2])
    grad_in = row_copies(grad_hbm, grad_ref, in_sem.at[0])
    gate_in = row_copies(gate_hbm, gate_ref, in_sem.at[1])
    taps_in = copies((taps_hbm, made_ref.at[:, pl.ds(0, span), :], taps_sem.at[0]))
    tile = lax.broadcasted_iota(jnp.int32, (ROWS, tokens), 0)
    ids = jnp.where(tile == 0, doc_ref[...], lang_ref[...]).astype(f32).astype(bf16)
    for i in range(pieces):
        made_ref[i, span + tall :, :] = ids
    group = tokens // groups
    sent = []
    for g in range(groups):
        finish(input_in[g])
        rows = slice(g * group, (g + 1) * group)
        at = slice(in_row + g * group, in_row + (g + 1) * group)
        for i in range(pieces):
            made_ref[i, at, in_lanes] = input_ref[rows, i * span : (i + 1) * span]
    finish(*taps_in)
    sent += send(0, 0, span if grad_row == in_row else grad_row)
    for g in range(groups):
        finish(grad_in[g], gate_in[g])
        rows = slice(g * group, (g + 1) * group)
        at = slice(grad_row + g * group, grad_row + (g + 1) * group)
        for i in range(pieces):
            part = slice(i * span, (i + 1) * span)
            made_ref[i, at, grad_lanes] = (
                grad_ref[rows, part].astype(f32) * gate_ref[rows, part].astype(f32)
            ).astype(bf16)
        if g == groups // 2 - 1:
            sent += send(1, grad_row, (g + 1) * group)
    start = grad_row + tokens // 2
    sent += send(2, start, span + tall + ROWS - start)
    finish(*sent)


def token_scale(message_ref, scale_ref, dro_ref, ids, mean_len, doc_ref, lang_ref):
    for j in range(message_ref.shape[0]):
        rows = message_ref[j, ids:, :].astype(f32)
        doc_ref[j : j + 1, :] = rows[0:1]
        lang_ref[j : j + 1, :] = rows[1:2]
    docs, langs = doc_ref[...], lang_ref[...]
    doc_len = jnp.zeros_like(docs)
    for d in range(NDOCS):
        hot = (docs == float(d)).astype(f32)
        doc_len = doc_len + hot * jnp.sum(hot, axis=(0, 1), keepdims=True)
    weight = jnp.zeros_like(langs)
    for g in range(dro_ref.shape[0]):
        weight = jnp.where(langs == float(g), dro_ref[g], weight)
    scale_ref[...] = (weight * (2.0 * mean_len) / (doc_len + mean_len)).T


def conv_kernel(
    mean_len,
    message_ref,
    dro_ref,
    skip_ref,
    table_ref,
    out_hbm,
    cross_hbm,
    scale_ref,
    out_ref,
    cross_ref,
    scaled_ref,
    taps_mid_ref,
    mid_ref,
    back_ref,
    doc_ref,
    lang_ref,
    cross_sem,
    out_sem,
):
    pieces = message_ref.shape[0]
    tokens = message_ref.shape[2]
    span = skip_ref.shape[1]
    place, tall = places(pieces, tokens, span)
    width = 2 * tokens
    slab = pieces * ROWS

    def ahead(m):
        return table_ref[m * width : (m + 1) * width, :]

    def behind(m):
        return ahead(pieces + m)

    def joint(start, rows, blocks):
        parts = [slice(start + b * rows, start + (b + 1) * rows) for b in range(blocks)]
        return jnp.concatenate([table_ref[part, :] for part in parts], axis=1)

    start = 2 * pieces * width
    outer_blocks = slab // width
    outer_table = joint(start, 2 * slab, outer_blocks)
    inverse_table = joint(start + 2 * slab * outer_blocks, slab, 2 * outer_blocks)
    token_scale(message_ref, scale_ref, dro_ref, span + tall, mean_len, doc_ref, lang_ref)

    def outer_taps(row):
        rows = pl.ds(row, ROWS)
        stack = jnp.concatenate([message_ref[j, rows, :] for j in range(pieces)], axis=0)
        out = dot(outer_table, stack).astype(bf16)
        for m in range(pieces):
            at = 2 * m * ROWS
            taps_mid_ref[m, rows, :tokens] = out[at : at + ROWS]
            taps_mid_ref[m, rows, tokens:] = out[at + ROWS : at + 2 * ROWS]

    chunked(span, outer_taps, True)
    sides = (slice(0, span), slice(span, 2 * span))

    def load(side, j, row):
        start, lanes = place(side, span)
        return message_ref[j, pl.ds(start + row, ROWS), lanes]

    def outer(row):
        rows = pl.ds(row, ROWS)
        stack = []
        for j in range(pieces):
            scaled = (load(1, j, row).astype(f32) * scale_ref[rows, j : j + 1]).astype(bf16)
            scaled_ref[j, rows, :] = scaled
            stack.append(jnp.concatenate([load(0, j, row), scaled], axis=1))
        out = dot(outer_table, jnp.concatenate(stack, axis=0)).astype(bf16)
        for m in range(pieces):
            at = 2 * m * ROWS
            mid_ref[m, rows, :] = out[at : at + ROWS]
            mid_ref[m, pl.ds(tokens + row, ROWS), :] = out[at + ROWS : at + 2 * ROWS]

    chunked(tokens, outer, True)

    def inner(m):
        filt = lax.dot_general(
            ahead(m), taps_mid_ref[m], (((1,), (1,)), ((), ())), preferred_element_type=f32
        )
        spec = dot(ahead(m), mid_ref[m])
        fre, fim = filt[:tokens], filt[tokens:]
        xre, xim = spec[:tokens, sides[0]], spec[tokens:, sides[0]]
        gre, gim = spec[:tokens, sides[1]], spec[tokens:, sides[1]]
        cross_ref[m, :tokens, :] = (xre * gre + xim * gim).astype(bf16)
        cross_ref[m, tokens:, :] = (xre * gim - xim * gre).astype(bf16)
        mixed = jnp.concatenate([fre * xre - fim * xim, fre * xim + fim * xre], axis=0)
        back = jnp.concatenate([fre * gre + fim * gim, fre * gim - fim * gre], axis=0)
        both = jnp.concatenate([mixed.astype(bf16), back.astype(bf16)], axis=1)
        back_ref[m] = dot(behind(m), both).astype(bf16)

    each_piece(pieces, inner, pieces)
    cross_out = copies((cross_ref, cross_hbm, cross_sem.at[0]))
    skip = skip_ref[...]

    def outer_back(row):
        rows = pl.ds(row, ROWS)
        stack = []
        for m in range(pieces):
            stack += [back_ref[m, rows, :], back_ref[m, pl.ds(tokens + row, ROWS), :]]
        out = dot(inverse_table, jnp.concatenate(stack, axis=0))
        for j in range(pieces):
            at = slice(j * ROWS, (j + 1) * ROWS)
            for side in (0, 1):
                start, lanes = place(side, 0)
                own = load(0, j, row) if side == 0 else scaled_ref[j, rows, :]
                out_ref[j, pl.ds(start + row, ROWS), lanes] = (
                    out[at, sides[side]] + skip * own.astype(f32)
                ).astype(bf16)

    sent = cross_out
    halves = out_sem.shape[0]
    starts = sorted({place(side, 0)[0] for side in (0, 1)})
    for half in range(halves):
        size = tokens // halves
        for row in range(half * size, (half + 1) * size, ROWS):
            outer_back(row)
        for side, first in enumerate(starts):
            rows = pl.ds(first + half * size, size)
            sent += copies((out_ref.at[:, rows, :], out_hbm.at[:, rows, :], out_sem.at[half, side]))
    finish(*sent)


def lags_kernel(own_ref, cross_ref, behind_ref, keep_ref, send_ref, back_ref, lag_ref):
    pieces, tall, span = cross_ref.shape
    tokens = tall // 2
    held = keep_ref.shape[1] // tokens
    members = pieces // held

    def inner(m):
        back_ref[m] = dot(behind_ref[m], cross_ref[m])

    each_piece(pieces, inner)

    def body(row):
        out = outer_inverse(
            [
                (back_ref[m, pl.ds(row, ROWS), :], back_ref[m, pl.ds(tokens + row, ROWS), :])
                for m in range(pieces)
            ]
        )
        for j in range(pieces):
            lag_ref[j, pl.ds(row, ROWS), :] = out[j]

    chunked(tokens, body)
    for j in range(held):
        part = slice(j * tokens, (j + 1) * tokens)
        keep_ref[:, part] = lag_ref[own_ref[0] * held + j].T
        for r in range(1, members):
            other = lax.rem(own_ref[0] + r, members)
            send_ref[r - 1, :, part] = lag_ref[other * held + j].T.astype(bf16)


def scaled_kernel(own_ref, grad_ref, scale_ref, out_ref):
    lane = lax.broadcasted_iota(jnp.int32, scale_ref.shape, 1)
    scale = jnp.where(lane == own_ref[0], scale_ref[...], jnp.zeros(scale_ref.shape, f32))
    out_ref[...] = grad_ref[...].astype(f32) * jnp.sum(scale, axis=1, keepdims=True)


def final_kernel(scaled_ref, message_ref, gate_ref, input_ref):
    pieces = message_ref.shape[0]
    tokens, channels = scaled_ref.shape
    span = channels // pieces
    place, _ = places(pieces, tokens, span)
    mixed_row, mixed_lanes = place(0, 0)
    back_row, back_lanes = place(1, 0)
    for i in range(pieces):
        part = slice(i * span, (i + 1) * span)
        mixed = message_ref[i, mixed_row : mixed_row + tokens, mixed_lanes].astype(f32)
        gate_ref[:, part] = (scaled_ref[:, part] * mixed).astype(bf16)
        input_ref[:, part] = message_ref[i, back_row : back_row + tokens, back_lanes]


def call(kernel, out, ins, scratch=(), outs=None, room=40 << 20, cost=(0, 0)):
    return pl.pallas_call(
        kernel,
        out_shape=out,
        in_specs=ins,
        out_specs=jax.tree.map(lambda _: VMEM, out) if outs is None else outs,
        scratch_shapes=scratch,
        compiler_params=pltpu.CompilerParams(vmem_limit_bytes=(64 << 20) - room),
        cost_estimate=pl.CostEstimate(flops=cost[0], bytes_accessed=cost[1], transcendentals=0),
    )


def local(grad_out, saved_input, gate_value, filter_taps, skip_gain, lang_ids, doc_ids, dro_weight):
    tokens = grad_out.shape[1]
    channels = grad_out.shape[2]
    pieces = lax.axis_size("ctx")
    members = lax.axis_size("dp")
    length = tokens * pieces
    span = channels // pieces
    mean_len = length / NDOCS
    place = lax.axis_index("ctx")
    own = place.reshape(1)
    tables, behind = all_tables(pieces, tokens)
    skip = lax.dynamic_slice_in_dim(skip_gain, place * span, span)[None, :]
    exchange = functools.partial(
        lax.all_to_all, axis_name="ctx", split_axis=0, concat_axis=0, tiled=True
    )
    shape = jax.ShapeDtypeStruct
    dma = pltpu.SemaphoreType.DMA
    tall = places(pieces, tokens, span)[1]
    macs = pieces * (2 * tokens) ** 2 * span
    message = shape((pieces, span + tall + ROWS, tokens), bf16)
    answer = shape((pieces, tall, tokens), bf16)
    groups = 4

    sent = call(
        functools.partial(prep_kernel, pieces, span),
        message,
        [HBM] * 4 + [VMEM] * 2,
        [
            pltpu.VMEM((tokens, channels), bf16),
            pltpu.VMEM((tokens, channels), bf16),
            pltpu.VMEM((tokens, channels), bf16),
            pltpu.VMEM(message.shape, bf16),
            dma((3, groups)),
            dma((1,)),
            dma((3,)),
        ],
        outs=HBM,
        room=256 << 10,
        cost=(0, 4 << 20),
    )(
        saved_input[0],
        grad_out[0],
        gate_value[0],
        filter_taps.reshape(pieces, span, tokens),
        doc_ids,
        lang_ids,
    )
    sent, cross, scale = call(
        functools.partial(conv_kernel, mean_len),
        [answer, shape((pieces, 2 * tokens, span), bf16), shape((tokens, pieces), f32)],
        [VMEM, SMEM, VMEM, VMEM],
        [
            pltpu.VMEM(answer.shape, bf16),
            pltpu.VMEM((pieces, 2 * tokens, span), bf16),
            pltpu.VMEM((pieces, tokens, span), bf16),
            pltpu.VMEM((pieces, span, 2 * tokens), bf16),
            pltpu.VMEM((pieces, 2 * tokens, 2 * span), bf16),
            pltpu.VMEM((pieces, 2 * tokens, 2 * span), bf16),
            pltpu.VMEM((pieces, tokens), f32),
            pltpu.VMEM((pieces, tokens), f32),
            dma((1,)),
            dma((2, 2)),
        ],
        outs=[HBM, HBM, VMEM],
        room=(8 << 20) if span % 128 == 0 else (20 << 20),
        cost=(10 * macs, 8 << 20),
    )(exchange(sent), dro_weight, skip, tables)
    got = exchange(sent)
    keep, send = call(
        lags_kernel,
        (
            jax.ShapeDtypeStruct((span, length // members), f32),
            jax.ShapeDtypeStruct((members - 1, span, length // members), bf16),
        ),
        [SMEM, VMEM, VMEM],
        [
            pltpu.VMEM((pieces, 2 * tokens, span), f32),
            pltpu.VMEM((pieces, tokens, span), f32),
        ],
        cost=(2 * macs, 6 << 20),
    )(lax.axis_index("dp").reshape(1), cross, behind)
    d_filter = keep
    for r in range(1, members):
        ring = [(d, (d + r) % members) for d in range(members)]
        d_filter = d_filter + lax.ppermute(send[r - 1], "dp", ring).astype(f32)
    token_block = jax.ShapeDtypeStruct((tokens, channels), bf16)
    scaled = call(
        scaled_kernel,
        shape((tokens, channels), f32),
        [SMEM, VMEM, VMEM],
        cost=(0, 2 << 20),
    )(own, grad_out[0], scale)
    d_gate, d_input = call(
        final_kernel,
        (token_block, token_block),
        [VMEM, VMEM],
        cost=(0, 4 << 20),
    )(scaled, got)
    return (d_input[None], d_gate[None], d_filter)


def solution(mesh):
    return jax.shard_map(
        local,
        mesh=mesh,
        in_specs=(
            P("dp", "ctx", None),
            P("dp", "ctx", None),
            P("dp", "ctx", None),
            P(None, "ctx"),
            P(),
            P("dp", "ctx"),
            P("dp", "ctx"),
            P(),
        ),
        out_specs=(P("dp", "ctx", None), P("dp", "ctx", None), P("ctx", "dp")),
        check_vma=False,
    )
```

```python
import functools
import math

import jax
import jax.numpy as jnp
import numpy as np
from jax import lax
from jax.experimental import pallas as pl
from jax.experimental.pallas import tpu as pltpu
from jax.sharding import PartitionSpec as P

NDOCS = 32
ROWS = 16
VMEM = pl.BlockSpec(memory_space=pltpu.VMEM)
HBM = pl.BlockSpec(memory_space=pltpu.HBM)
SMEM = pl.BlockSpec(memory_space=pltpu.SMEM)
f32 = jnp.float32
bf16 = jnp.bfloat16


def inner_tables(pieces, tokens):
    size = 2 * pieces * tokens
    m = np.arange(pieces)[:, None, None]
    k = np.arange(tokens)[None, :, None]
    q = np.arange(tokens)[None, None, :]
    turn = (q * (4 * m + 1 + 4 * pieces * k)) % (2 * size)
    angle = math.pi / size * turn
    cos, sin = np.cos(angle), np.sin(angle)
    ahead = np.concatenate(
        [np.concatenate([cos, sin], axis=2), np.concatenate([-sin, cos], axis=2)], axis=1
    )
    behind = np.swapaxes(ahead, 1, 2) * (2.0 / size)
    return ahead, behind


def outer_tables(pieces):
    m = np.arange(pieces)[:, None]
    j = np.arange(pieces)[None, :]
    angle = math.pi / (2 * pieces) * (j * (4 * m + 1) % (4 * pieces))
    both = np.stack([np.cos(angle), -np.sin(angle)], axis=1).reshape(2 * pieces, pieces)
    ahead = np.kron(both, np.eye(ROWS))
    return ahead, ahead.T


def side_by_side(table, width):
    return np.concatenate(np.split(table, table.shape[1] // width, axis=1), axis=0)


def all_tables(pieces, tokens):
    width = 2 * tokens
    ahead, behind = inner_tables(pieces, tokens)
    outer, inverse = outer_tables(pieces)
    parts = [
        ahead.reshape(-1, width),
        behind.reshape(-1, width),
        side_by_side(outer, width),
        side_by_side(inverse, width),
    ]
    return jnp.asarray(np.concatenate(parts, axis=0), bf16), jnp.asarray(behind, bf16)


def turned(value, turns):
    re, im = value
    turns = turns % 1.0
    if turns == 0.0:
        return value
    if turns == 0.25:
        return (-im, re)
    if turns == 0.5:
        return (-re, -im)
    if turns == 0.75:
        return (im, -re)
    cos, sin = math.cos(2.0 * math.pi * turns), math.sin(2.0 * math.pi * turns)
    if (turns * 8.0) % 1.0 == 0.0:
        root = math.sqrt(0.5)
        plus, minus = (re + im) * root, (re - im) * root
        if turns == 0.125:
            return (minus, plus)
        if turns == 0.375:
            return (-plus, minus)
        if turns == 0.625:
            return (-minus, -plus)
        return (plus, -minus)
    return (re * cos - im * sin, re * sin + im * cos)


def dft(values, sign):
    count = len(values)
    if count == 1:
        return values
    even, odd = dft(values[0::2], sign), dft(values[1::2], sign)
    first, second = [], []
    for k in range(count // 2):
        a, b = even[k], turned(odd[k], sign * k / count)
        first.append((a[0] + b[0], a[1] + b[1]))
        second.append((a[0] - b[0], a[1] - b[1]))
    return first + second


def outer_inverse(values):
    count = len(values)
    out = []
    for j, (re, im) in enumerate(dft(values, 1.0)):
        angle = math.pi * j / (2 * count)
        out.append(re if j == 0 else re * math.cos(angle) - im * math.sin(angle))
    return out


def chunked(total, body, unrolled=False):
    if unrolled:
        for i in range(total // ROWS):
            body(i * ROWS)
        return

    def step(i, carry):
        body(pl.multiple_of(i * ROWS, ROWS))
        return carry

    lax.fori_loop(0, total // ROWS, step, 0)


def each_piece(pieces, body, group=4):
    if group == pieces:
        for m in range(pieces):
            body(m)
        return

    def step(i, carry):
        for g in range(group):
            body(i * group + g)
        return carry

    lax.fori_loop(0, pieces // group, step, 0)


def dot(a, b):
    return lax.dot_general(a, b, (((1,), (0,)), ((), ())), preferred_element_type=f32)


def places(pieces, tokens, span):
    beside = max(1, tokens // span)

    def place(index, start):
        row = start + (index // beside) * tokens
        column = (index % beside) * span
        return row, slice(column, column + span)

    tall = -(-2 // beside) * tokens
    return place, tall


def copies(*pairs):
    started = [pltpu.make_async_copy(*pair) for pair in pairs]
    for copy in started:
        copy.start()
    return started


def finish(*started):
    for copy in started:
        copy.wait()


def row_copies(source, target, sems):
    count = sems.shape[0]
    group = source.shape[0] // count
    rows = [pl.ds(g * group, group) for g in range(count)]
    return copies(*[(source.at[r], target.at[r], sems.at[g]) for g, r in enumerate(rows)])


def prep_kernel(
    pieces,
    span,
    input_hbm,
    grad_hbm,
    gate_hbm,
    taps_hbm,
    doc_ref,
    lang_ref,
    out_hbm,
    input_ref,
    grad_ref,
    gate_ref,
    made_ref,
    in_sem,
    taps_sem,
    out_sem,
):
    tokens = grad_ref.shape[0]
    groups = in_sem.shape[1]
    place, tall = places(pieces, tokens, span)
    in_row, in_lanes = place(0, span)
    grad_row, grad_lanes = place(1, span)

    def send(part, start, size):
        rows = pl.ds(start, size)
        return copies((made_ref.at[:, rows, :], out_hbm.at[:, rows, :], out_sem.at[part]))

    input_in = row_copies(input_hbm, input_ref, in_sem.at[2])
    grad_in = row_copies(grad_hbm, grad_ref, in_sem.at[0])
    gate_in = row_copies(gate_hbm, gate_ref, in_sem.at[1])
    taps_in = copies((taps_hbm, made_ref.at[:, pl.ds(0, span), :], taps_sem.at[0]))
    tile = lax.broadcasted_iota(jnp.int32, (ROWS, tokens), 0)
    ids = jnp.where(tile == 0, doc_ref[...], lang_ref[...]).astype(f32).astype(bf16)
    for i in range(pieces):
        made_ref[i, span + tall :, :] = ids
    group = tokens // groups
    sent = []
    for g in range(groups):
        finish(input_in[g])
        rows = slice(g * group, (g + 1) * group)
        at = slice(in_row + g * group, in_row + (g + 1) * group)
        for i in range(pieces):
            made_ref[i, at, in_lanes] = input_ref[rows, i * span : (i + 1) * span]
    finish(*taps_in)
    sent += send(0, 0, span if grad_row == in_row else grad_row)
    for g in range(groups):
        finish(grad_in[g], gate_in[g])
        rows = slice(g * group, (g + 1) * group)
        at = slice(grad_row + g * group, grad_row + (g + 1) * group)
        for i in range(pieces):
            part = slice(i * span, (i + 1) * span)
            made_ref[i, at, grad_lanes] = (
                grad_ref[rows, part].astype(f32) * gate_ref[rows, part].astype(f32)
            ).astype(bf16)
        if g == groups // 2 - 1:
            sent += send(1, grad_row, (g + 1) * group)
    start = grad_row + tokens // 2
    sent += send(2, start, span + tall + ROWS - start)
    finish(*sent)


def token_scale(message_ref, scale_ref, dro_ref, ids, mean_len, doc_ref, lang_ref):
    for j in range(message_ref.shape[0]):
        rows = message_ref[j, ids:, :].astype(f32)
        doc_ref[j : j + 1, :] = rows[0:1]
        lang_ref[j : j + 1, :] = rows[1:2]
    docs, langs = doc_ref[...], lang_ref[...]
    doc_len = jnp.zeros_like(docs)
    for d in range(NDOCS):
        hot = (docs == float(d)).astype(f32)
        doc_len = doc_len + hot * jnp.sum(hot, axis=(0, 1), keepdims=True)
    weight = jnp.zeros_like(langs)
    for g in range(dro_ref.shape[0]):
        weight = jnp.where(langs == float(g), dro_ref[g], weight)
    scale_ref[...] = (weight * (2.0 * mean_len) / (doc_len + mean_len)).T


def conv_kernel(
    mean_len,
    message_ref,
    dro_ref,
    skip_ref,
    table_ref,
    out_ref,
    cross_ref,
    scale_ref,
    scaled_ref,
    taps_mid_ref,
    mid_ref,
    back_ref,
    doc_ref,
    lang_ref,
):
    pieces = message_ref.shape[0]
    tokens = message_ref.shape[2]
    span = skip_ref.shape[1]
    place, tall = places(pieces, tokens, span)
    width = 2 * tokens
    slab = pieces * ROWS

    def ahead(m):
        return table_ref[m * width : (m + 1) * width, :]

    def behind(m):
        return ahead(pieces + m)

    def joint(start, rows, blocks):
        parts = [slice(start + b * rows, start + (b + 1) * rows) for b in range(blocks)]
        return jnp.concatenate([table_ref[part, :] for part in parts], axis=1)

    start = 2 * pieces * width
    outer_blocks = slab // width
    outer_table = joint(start, 2 * slab, outer_blocks)
    inverse_table = joint(start + 2 * slab * outer_blocks, slab, 2 * outer_blocks)
    token_scale(message_ref, scale_ref, dro_ref, span + tall, mean_len, doc_ref, lang_ref)

    def outer_taps(row):
        rows = pl.ds(row, ROWS)
        stack = jnp.concatenate([message_ref[j, rows, :] for j in range(pieces)], axis=0)
        out = dot(outer_table, stack).astype(bf16)
        for m in range(pieces):
            at = 2 * m * ROWS
            taps_mid_ref[m, rows, :tokens] = out[at : at + ROWS]
            taps_mid_ref[m, rows, tokens:] = out[at + ROWS : at + 2 * ROWS]

    chunked(span, outer_taps, True)
    sides = (slice(0, span), slice(span, 2 * span))

    def load(side, j, row):
        start, lanes = place(side, span)
        return message_ref[j, pl.ds(start + row, ROWS), lanes]

    def outer(row):
        rows = pl.ds(row, ROWS)
        stack = []
        for j in range(pieces):
            scaled = (load(1, j, row).astype(f32) * scale_ref[rows, j : j + 1]).astype(bf16)
            scaled_ref[j, rows, :] = scaled
            stack.append(jnp.concatenate([load(0, j, row), scaled], axis=1))
        out = dot(outer_table, jnp.concatenate(stack, axis=0)).astype(bf16)
        for m in range(pieces):
            at = 2 * m * ROWS
            mid_ref[m, rows, :] = out[at : at + ROWS]
            mid_ref[m, pl.ds(tokens + row, ROWS), :] = out[at + ROWS : at + 2 * ROWS]

    chunked(tokens, outer, True)

    def inner(m):
        filt = lax.dot_general(
            ahead(m), taps_mid_ref[m], (((1,), (1,)), ((), ())), preferred_element_type=f32
        )
        spec = dot(ahead(m), mid_ref[m])
        fre, fim = filt[:tokens], filt[tokens:]
        xre, xim = spec[:tokens, sides[0]], spec[tokens:, sides[0]]
        gre, gim = spec[:tokens, sides[1]], spec[tokens:, sides[1]]
        cross_ref[m, :tokens, :] = (xre * gre + xim * gim).astype(bf16)
        cross_ref[m, tokens:, :] = (xre * gim - xim * gre).astype(bf16)
        mixed = jnp.concatenate([fre * xre - fim * xim, fre * xim + fim * xre], axis=0)
        back = jnp.concatenate([fre * gre + fim * gim, fre * gim - fim * gre], axis=0)
        both = jnp.concatenate([mixed.astype(bf16), back.astype(bf16)], axis=1)
        back_ref[m] = dot(behind(m), both).astype(bf16)

    each_piece(pieces, inner, pieces)
    skip = skip_ref[...]

    def outer_back(row):
        rows = pl.ds(row, ROWS)
        stack = []
        for m in range(pieces):
            stack += [back_ref[m, rows, :], back_ref[m, pl.ds(tokens + row, ROWS), :]]
        out = dot(inverse_table, jnp.concatenate(stack, axis=0))
        for j in range(pieces):
            at = slice(j * ROWS, (j + 1) * ROWS)
            for side in (0, 1):
                start, lanes = place(side, 0)
                own = load(0, j, row) if side == 0 else scaled_ref[j, rows, :]
                out_ref[j, pl.ds(start + row, ROWS), lanes] = (
                    out[at, sides[side]] + skip * own.astype(f32)
                ).astype(bf16)

    chunked(tokens, outer_back, True)


def lags_kernel(own_ref, cross_ref, behind_ref, keep_ref, send_ref, back_ref, lag_ref):
    pieces, tall, span = cross_ref.shape
    tokens = tall // 2
    held = keep_ref.shape[1] // tokens
    members = pieces // held

    def inner(m):
        back_ref[m] = dot(behind_ref[m], cross_ref[m])

    each_piece(pieces, inner)

    def body(row):
        out = outer_inverse(
            [
                (back_ref[m, pl.ds(row, ROWS), :], back_ref[m, pl.ds(tokens + row, ROWS), :])
                for m in range(pieces)
            ]
        )
        for j in range(pieces):
            lag_ref[j, pl.ds(row, ROWS), :] = out[j]

    chunked(tokens, body)
    for j in range(held):
        part = slice(j * tokens, (j + 1) * tokens)
        keep_ref[:, part] = lag_ref[own_ref[0] * held + j].T
        for r in range(1, members):
            other = lax.rem(own_ref[0] + r, members)
            send_ref[r - 1, :, part] = lag_ref[other * held + j].T.astype(bf16)


def scaled_kernel(own_ref, grad_ref, scale_ref, out_ref):
    lane = lax.broadcasted_iota(jnp.int32, scale_ref.shape, 1)
    scale = jnp.where(lane == own_ref[0], scale_ref[...], jnp.zeros(scale_ref.shape, f32))
    out_ref[...] = grad_ref[...].astype(f32) * jnp.sum(scale, axis=1, keepdims=True)


def final_kernel(scaled_ref, message_ref, gate_ref, input_ref):
    pieces = message_ref.shape[0]
    tokens, channels = scaled_ref.shape
    span = channels // pieces
    place, _ = places(pieces, tokens, span)
    mixed_row, mixed_lanes = place(0, 0)
    back_row, back_lanes = place(1, 0)
    for i in range(pieces):
        part = slice(i * span, (i + 1) * span)
        mixed = message_ref[i, mixed_row : mixed_row + tokens, mixed_lanes].astype(f32)
        gate_ref[:, part] = (scaled_ref[:, part] * mixed).astype(bf16)
        input_ref[:, part] = message_ref[i, back_row : back_row + tokens, back_lanes]


def call(kernel, out, ins, scratch=(), outs=None, room=40 << 20, cost=(0, 0)):
    return pl.pallas_call(
        kernel,
        out_shape=out,
        in_specs=ins,
        out_specs=jax.tree.map(lambda _: VMEM, out) if outs is None else outs,
        scratch_shapes=scratch,
        compiler_params=pltpu.CompilerParams(vmem_limit_bytes=(64 << 20) - room),
        cost_estimate=pl.CostEstimate(flops=cost[0], bytes_accessed=cost[1], transcendentals=0),
    )


def local(grad_out, saved_input, gate_value, filter_taps, skip_gain, lang_ids, doc_ids, dro_weight):
    tokens = grad_out.shape[1]
    channels = grad_out.shape[2]
    pieces = lax.axis_size("ctx")
    members = lax.axis_size("dp")
    length = tokens * pieces
    span = channels // pieces
    mean_len = length / NDOCS
    place = lax.axis_index("ctx")
    own = place.reshape(1)
    tables, behind = all_tables(pieces, tokens)
    skip = lax.dynamic_slice_in_dim(skip_gain, place * span, span)[None, :]
    exchange = functools.partial(
        lax.all_to_all, axis_name="ctx", split_axis=0, concat_axis=0, tiled=True
    )
    shape = jax.ShapeDtypeStruct
    dma = pltpu.SemaphoreType.DMA
    tall = places(pieces, tokens, span)[1]
    macs = pieces * (2 * tokens) ** 2 * span
    message = shape((pieces, span + tall + ROWS, tokens), bf16)
    answer = shape((pieces, tall, tokens), bf16)
    groups = 4

    sent = call(
        functools.partial(prep_kernel, pieces, span),
        message,
        [HBM] * 4 + [VMEM] * 2,
        [
            pltpu.VMEM((tokens, channels), bf16),
            pltpu.VMEM((tokens, channels), bf16),
            pltpu.VMEM((tokens, channels), bf16),
            pltpu.VMEM(message.shape, bf16),
            dma((3, groups)),
            dma((1,)),
            dma((3,)),
        ],
        outs=HBM,
        room=256 << 10,
        cost=(0, 4 << 20),
    )(
        saved_input[0],
        grad_out[0],
        gate_value[0],
        filter_taps.reshape(pieces, span, tokens),
        doc_ids,
        lang_ids,
    )
    sent, cross, scale = call(
        functools.partial(conv_kernel, mean_len),
        [answer, shape((pieces, 2 * tokens, span), bf16), shape((tokens, pieces), f32)],
        [VMEM, SMEM, VMEM, VMEM],
        [
            pltpu.VMEM((pieces, tokens, span), bf16),
            pltpu.VMEM((pieces, span, 2 * tokens), bf16),
            pltpu.VMEM((pieces, 2 * tokens, 2 * span), bf16),
            pltpu.VMEM((pieces, 2 * tokens, 2 * span), bf16),
            pltpu.VMEM((pieces, tokens), f32),
            pltpu.VMEM((pieces, tokens), f32),
        ],
        room=(40 << 20) if span % 128 == 0 else (20 << 20),
        cost=(10 * macs, 8 << 20),
    )(exchange(sent), dro_weight, skip, tables)
    got = exchange(sent)
    keep, send = call(
        lags_kernel,
        (
            jax.ShapeDtypeStruct((span, length // members), f32),
            jax.ShapeDtypeStruct((members - 1, span, length // members), bf16),
        ),
        [SMEM, VMEM, VMEM],
        [
            pltpu.VMEM((pieces, 2 * tokens, span), f32),
            pltpu.VMEM((pieces, tokens, span), f32),
        ],
        cost=(2 * macs, 6 << 20),
    )(lax.axis_index("dp").reshape(1), cross, behind)
    d_filter = keep
    for r in range(1, members):
        ring = [(d, (d + r) % members) for d in range(members)]
        d_filter = d_filter + lax.ppermute(send[r - 1], "dp", ring).astype(f32)
    token_block = jax.ShapeDtypeStruct((tokens, channels), bf16)
    scaled = call(
        scaled_kernel,
        shape((tokens, channels), f32),
        [SMEM, VMEM, VMEM],
        cost=(0, 2 << 20),
    )(own, grad_out[0], scale)
    d_gate, d_input = call(
        final_kernel,
        (token_block, token_block),
        [VMEM, VMEM],
        cost=(0, 4 << 20),
    )(scaled, got)
    return (d_input[None], d_gate[None], d_filter)


def solution(mesh):
    return jax.shard_map(
        local,
        mesh=mesh,
        in_specs=(
            P("dp", "ctx", None),
            P("dp", "ctx", None),
            P("dp", "ctx", None),
            P(None, "ctx"),
            P(),
            P("dp", "ctx"),
            P("dp", "ctx"),
            P(),
        ),
        out_specs=(P("dp", "ctx", None), P("dp", "ctx", None), P("ctx", "dp")),
        check_vma=False,
    )
```

```python
import functools
import math

import jax
import jax.numpy as jnp
import numpy as np
from jax import lax
from jax.experimental import pallas as pl
from jax.experimental.pallas import tpu as pltpu
from jax.sharding import PartitionSpec as P

NDOCS = 32
ROWS = 16
VMEM = pl.BlockSpec(memory_space=pltpu.VMEM)
HBM = pl.BlockSpec(memory_space=pltpu.HBM)
SMEM = pl.BlockSpec(memory_space=pltpu.SMEM)
f32 = jnp.float32
bf16 = jnp.bfloat16


def inner_tables(pieces, tokens):
    size = 2 * pieces * tokens
    m = np.arange(pieces)[:, None, None]
    k = np.arange(tokens)[None, :, None]
    q = np.arange(tokens)[None, None, :]
    turn = (q * (4 * m + 1 + 4 * pieces * k)) % (2 * size)
    angle = math.pi / size * turn
    cos, sin = np.cos(angle), np.sin(angle)
    ahead = np.concatenate(
        [np.concatenate([cos, sin], axis=2), np.concatenate([-sin, cos], axis=2)], axis=1
    )
    behind = np.swapaxes(ahead, 1, 2) * (2.0 / size)
    return ahead, behind


def outer_tables(pieces):
    m = np.arange(pieces)[:, None]
    j = np.arange(pieces)[None, :]
    angle = math.pi / (2 * pieces) * (j * (4 * m + 1) % (4 * pieces))
    both = np.stack([np.cos(angle), -np.sin(angle)], axis=1).reshape(2 * pieces, pieces)
    ahead = np.kron(both, np.eye(ROWS))
    return ahead, ahead.T


def side_by_side(table, width):
    return np.concatenate(np.split(table, table.shape[1] // width, axis=1), axis=0)


def all_tables(pieces, tokens):
    width = 2 * tokens
    ahead, behind = inner_tables(pieces, tokens)
    outer, inverse = outer_tables(pieces)
    parts = [
        ahead.reshape(-1, width),
        behind.reshape(-1, width),
        side_by_side(outer, width),
        side_by_side(inverse, width),
    ]
    return jnp.asarray(np.concatenate(parts, axis=0), bf16), jnp.asarray(behind, bf16)


def turned(value, turns):
    re, im = value
    turns = turns % 1.0
    if turns == 0.0:
        return value
    if turns == 0.25:
        return (-im, re)
    if turns == 0.5:
        return (-re, -im)
    if turns == 0.75:
        return (im, -re)
    cos, sin = math.cos(2.0 * math.pi * turns), math.sin(2.0 * math.pi * turns)
    if (turns * 8.0) % 1.0 == 0.0:
        root = math.sqrt(0.5)
        plus, minus = (re + im) * root, (re - im) * root
        if turns == 0.125:
            return (minus, plus)
        if turns == 0.375:
            return (-plus, minus)
        if turns == 0.625:
            return (-minus, -plus)
        return (plus, -minus)
    return (re * cos - im * sin, re * sin + im * cos)


def dft(values, sign):
    count = len(values)
    if count == 1:
        return values
    even, odd = dft(values[0::2], sign), dft(values[1::2], sign)
    first, second = [], []
    for k in range(count // 2):
        a, b = even[k], turned(odd[k], sign * k / count)
        first.append((a[0] + b[0], a[1] + b[1]))
        second.append((a[0] - b[0], a[1] - b[1]))
    return first + second


def outer_inverse(values):
    count = len(values)
    out = []
    for j, (re, im) in enumerate(dft(values, 1.0)):
        angle = math.pi * j / (2 * count)
        out.append(re if j == 0 else re * math.cos(angle) - im * math.sin(angle))
    return out


def chunked(total, body, unrolled=False):
    if unrolled:
        for i in range(total // ROWS):
            body(i * ROWS)
        return

    def step(i, carry):
        body(pl.multiple_of(i * ROWS, ROWS))
        return carry

    lax.fori_loop(0, total // ROWS, step, 0)


def each_piece(pieces, body, group=4):
    if group == pieces:
        for m in range(pieces):
            body(m)
        return

    def step(i, carry):
        for g in range(group):
            body(i * group + g)
        return carry

    lax.fori_loop(0, pieces // group, step, 0)


def dot(a, b):
    return lax.dot_general(a, b, (((1,), (0,)), ((), ())), preferred_element_type=f32)


def places(tokens, span):
    beside = max(1, tokens // span)

    def place(index, start):
        row = start + (index // beside) * tokens
        column = (index % beside) * span
        return row, slice(column, column + span)

    tall = -(-2 // beside) * tokens
    return place, tall


def copies(*pairs):
    started = [pltpu.make_async_copy(*pair) for pair in pairs]
    for copy in started:
        copy.start()
    return started


def finish(*started):
    for copy in started:
        copy.wait()


def row_copies(source, target, sems):
    count = sems.shape[0]
    group = source.shape[0] // count
    rows = [pl.ds(g * group, group) for g in range(count)]
    return copies(*[(source.at[r], target.at[r], sems.at[g]) for g, r in enumerate(rows)])


def prep_kernel(
    pieces,
    joint,
    own_ref,
    input_hbm,
    grad_hbm,
    gate_hbm,
    taps_hbm,
    doc_ref,
    lang_ref,
    out_hbm,
    input_ref,
    grad_ref,
    gate_ref,
    made_ref,
    in_sem,
    taps_sem,
    out_sem,
):
    tokens, channels = grad_ref.shape
    groups = in_sem.shape[1]
    span = channels // pieces
    share = span // joint
    taps = share // joint
    place, tall = places(tokens, share)
    in_row, in_lanes = place(0, taps)
    grad_row, grad_lanes = place(1, taps)
    owners = [(d, i) for d in range(joint) for i in range(pieces)]

    def send(part, start, size):
        rows = pl.ds(start, size)
        return copies((made_ref.at[:, rows, :], out_hbm.at[:, rows, :], out_sem.at[part]))

    input_in = row_copies(input_hbm, input_ref, in_sem.at[2])
    grad_in = row_copies(grad_hbm, grad_ref, in_sem.at[0])
    gate_in = row_copies(gate_hbm, gate_ref, in_sem.at[1])
    taps_in = []
    for d in range(joint):
        start = pl.multiple_of(d * share + own_ref[0] * taps, ROWS)
        taps_in += copies(
            (
                taps_hbm.at[:, pl.ds(start, taps), :],
                made_ref.at[pl.ds(d * pieces, pieces), pl.ds(0, taps), :],
                taps_sem.at[d],
            )
        )
    tile = lax.broadcasted_iota(jnp.int32, (ROWS, tokens), 0)
    ids = jnp.where(tile == 0, doc_ref[...], lang_ref[...]).astype(f32).astype(bf16)
    for o in range(len(owners)):
        made_ref[o, taps + tall :, :] = ids
    group = tokens // groups
    sent = []
    for g in range(groups):
        finish(input_in[g])
        rows = slice(g * group, (g + 1) * group)
        at = slice(in_row + g * group, in_row + (g + 1) * group)
        for o, (d, i) in enumerate(owners):
            part = slice(i * span + d * share, i * span + (d + 1) * share)
            made_ref[o, at, in_lanes] = input_ref[rows, part]
    finish(*taps_in)
    sent += send(0, 0, taps if grad_row == in_row else grad_row)
    for g in range(groups):
        finish(grad_in[g], gate_in[g])
        rows = slice(g * group, (g + 1) * group)
        at = slice(grad_row + g * group, grad_row + (g + 1) * group)
        made = (grad_ref[rows, :].astype(f32) * gate_ref[rows, :].astype(f32)).astype(bf16)
        for o, (d, i) in enumerate(owners):
            part = slice(i * span + d * share, i * span + (d + 1) * share)
            made_ref[o, at, grad_lanes] = made[:, part]
        if g == groups // 2 - 1:
            sent += send(1, grad_row, (g + 1) * group)
    start = grad_row + tokens // 2
    sent += send(2, start, taps + tall + ROWS - start)
    finish(*sent)


def token_scale(message_ref, scale_ref, dro_ref, ids, pieces, mean_len, doc_ref, lang_ref):
    for j in range(message_ref.shape[0]):
        rows = message_ref[j, ids:, :].astype(f32)
        doc_ref[j : j + 1, :] = rows[0:1]
        lang_ref[j : j + 1, :] = rows[1:2]
    for start in range(0, message_ref.shape[0], pieces):
        own = slice(start, start + pieces)
        docs, langs = doc_ref[own, :], lang_ref[own, :]
        doc_len = jnp.zeros_like(docs)
        for d in range(NDOCS):
            hot = (docs == float(d)).astype(f32)
            doc_len = doc_len + hot * jnp.sum(hot, axis=(0, 1), keepdims=True)
        weight = jnp.zeros_like(langs)
        for g in range(dro_ref.shape[0]):
            weight = jnp.where(langs == float(g), dro_ref[g], weight)
        scale_ref[:, own] = (weight * (2.0 * mean_len) / (doc_len + mean_len)).T


def conv_kernel(
    mean_len,
    joint,
    message_ref,
    dro_ref,
    skip_ref,
    table_ref,
    out_ref,
    cross_ref,
    scale_ref,
    both_ref,
    taps_mid_ref,
    mid_ref,
    back_ref,
    doc_ref,
    lang_ref,
):
    pieces = message_ref.shape[0] // joint
    tokens = message_ref.shape[2]
    share = skip_ref.shape[1] // 2
    taps = share // joint
    place, tall = places(tokens, share)
    width = 2 * tokens
    slab = pieces * ROWS
    pair = 2 * share

    def ahead(m):
        return table_ref[m * width : (m + 1) * width, :]

    def behind(m):
        return ahead(pieces + m)

    def blocks(start, rows, count):
        parts = [slice(start + b * rows, start + (b + 1) * rows) for b in range(count)]
        return jnp.concatenate([table_ref[part, :] for part in parts], axis=1)

    start = 2 * pieces * width
    outer_blocks = slab // width
    outer_table = blocks(start, 2 * slab, outer_blocks)
    inverse_table = blocks(start + 2 * slab * outer_blocks, slab, 2 * outer_blocks)
    token_scale(message_ref, scale_ref, dro_ref, taps + tall, pieces, mean_len, doc_ref, lang_ref)

    for d in range(joint):
        for row in range(0, taps, ROWS):
            held = [message_ref[d * pieces + j, row : row + ROWS, :] for j in range(pieces)]
            out = dot(outer_table, jnp.concatenate(held, axis=0)).astype(bf16)
            for m in range(pieces):
                at = 2 * m * ROWS
                for first in (d * taps + row, share + d * taps + row):
                    rows = slice(first, first + ROWS)
                    taps_mid_ref[m, rows, :tokens] = out[at : at + ROWS]
                    taps_mid_ref[m, rows, tokens:] = out[at + ROWS : at + 2 * ROWS]

    lane = lax.broadcasted_iota(jnp.int32, (ROWS, pair), 1)

    def load(o, row):
        (one, one_lanes), (two, two_lanes) = place(0, taps), place(1, taps)
        if one == two:
            return message_ref[o, pl.ds(one + row, ROWS), slice(one_lanes.start, two_lanes.stop)]
        return jnp.concatenate(
            [message_ref[o, pl.ds(first + row, ROWS), :] for first in (one, two)], axis=1
        )

    def outer(row):
        rows = pl.ds(row, ROWS)
        stack = []
        for j in range(pieces):
            line = []
            for d in range(joint):
                o = d * pieces + j
                factor = jnp.where(lane < share, 1.0, scale_ref[rows, o : o + 1])
                made = (load(o, row).astype(f32) * factor).astype(bf16)
                both_ref[o, rows, :] = made
                line.append(made)
            stack.append(jnp.concatenate(line, axis=1))
        out = dot(outer_table, jnp.concatenate(stack, axis=0)).astype(bf16)
        for m in range(pieces):
            at = 2 * m * ROWS
            mid_ref[m, rows, :] = out[at : at + ROWS]
            mid_ref[m, pl.ds(tokens + row, ROWS), :] = out[at + ROWS : at + 2 * ROWS]

    chunked(tokens, outer, True)
    sign = jnp.where(lax.broadcasted_iota(jnp.int32, (tokens, pair), 1) < share, 1.0, -1.0)

    def inner(m):
        filt = lax.dot_general(
            ahead(m), taps_mid_ref[m], (((1,), (1,)), ((), ())), preferred_element_type=f32
        )
        spec = dot(ahead(m), mid_ref[m])
        fre, fim = filt[:tokens], filt[tokens:] * sign
        cre, cim, prods = 0.0, 0.0, []
        for d in range(joint):
            part = slice(d * pair, (d + 1) * pair)
            re, im = spec[:tokens, part], spec[tokens:, part]
            xre, gre, xim, gim = re[:, :share], re[:, share:], im[:, :share], im[:, share:]
            cre, cim = cre + (xre * gre + xim * gim), cim + (xre * gim - xim * gre)
            prods.append(jnp.concatenate([fre * re - fim * im, fre * im + fim * re], axis=0))
        cross_ref[m, :tokens, :] = cre.astype(bf16)
        cross_ref[m, tokens:, :] = cim.astype(bf16)
        prods = jnp.concatenate([prod.astype(bf16) for prod in prods], axis=1)
        back_ref[m] = dot(behind(m), prods).astype(bf16)

    each_piece(pieces, inner, pieces)
    skip = skip_ref[...]

    def outer_back(row):
        rows = pl.ds(row, ROWS)
        stack = []
        for m in range(pieces):
            stack += [back_ref[m, rows, :], back_ref[m, pl.ds(tokens + row, ROWS), :]]
        out = dot(inverse_table, jnp.concatenate(stack, axis=0))
        (one, one_lanes), (two, two_lanes) = place(0, 0), place(1, 0)
        for j in range(pieces):
            for d in range(joint):
                o = d * pieces + j
                value = out[j * ROWS : (j + 1) * ROWS, d * pair : (d + 1) * pair]
                value = (value + skip * both_ref[o, rows, :].astype(f32)).astype(bf16)
                if one == two:
                    out_ref[o, rows, slice(one_lanes.start, two_lanes.stop)] = value
                else:
                    out_ref[o, rows, :] = value[:, :share]
                    out_ref[o, pl.ds(two + row, ROWS), :] = value[:, share:]

    chunked(tokens, outer_back, True)


def lags_kernel(own_ref, cross_ref, behind_ref, keep_ref, send_ref, back_ref, lag_ref):
    pieces, tall, span = cross_ref.shape
    tokens = tall // 2
    held = keep_ref.shape[1] // tokens
    members = pieces // held

    def inner(m):
        back_ref[m] = dot(behind_ref[m], cross_ref[m])

    each_piece(pieces, inner)

    def body(row):
        out = outer_inverse(
            [
                (back_ref[m, pl.ds(row, ROWS), :], back_ref[m, pl.ds(tokens + row, ROWS), :])
                for m in range(pieces)
            ]
        )
        for j in range(pieces):
            lag_ref[j, pl.ds(row, ROWS), :] = out[j]

    chunked(tokens, body)
    for j in range(held):
        part = slice(j * tokens, (j + 1) * tokens)
        keep_ref[:, part] = lag_ref[own_ref[0] * held + j].T
        for r in range(1, members):
            other = lax.rem(own_ref[0] + r, members)
            send_ref[r - 1, :, part] = lag_ref[other * held + j].T.astype(bf16)


def scaled_kernel(own_ref, grad_ref, scale_ref, out_ref):
    lane = lax.broadcasted_iota(jnp.int32, scale_ref.shape, 1)
    scale = jnp.where(lane == own_ref[0], scale_ref[...], jnp.zeros(scale_ref.shape, f32))
    out_ref[...] = grad_ref[...].astype(f32) * jnp.sum(scale, axis=1, keepdims=True)


def final_kernel(joint, scaled_ref, message_ref, gate_ref, input_ref):
    pieces = message_ref.shape[0] // joint
    tokens, channels = scaled_ref.shape
    span = channels // pieces
    share = span // joint
    place, _ = places(tokens, share)
    mixed_row, mixed_lanes = place(0, 0)
    back_row, back_lanes = place(1, 0)
    for i in range(pieces):
        owners = [d * pieces + i for d in range(joint)]
        mixed = [message_ref[o, mixed_row : mixed_row + tokens, mixed_lanes] for o in owners]
        back = [message_ref[o, back_row : back_row + tokens, back_lanes] for o in owners]
        part = slice(i * span, (i + 1) * span)
        mixed = jnp.concatenate(mixed, axis=1).astype(f32)
        gate_ref[:, part] = (scaled_ref[:, part] * mixed).astype(bf16)
        input_ref[:, part] = jnp.concatenate(back, axis=1)


def call(kernel, out, ins, scratch=(), outs=None, room=40 << 20, cost=(0, 0)):
    return pl.pallas_call(
        kernel,
        out_shape=out,
        in_specs=ins,
        out_specs=jax.tree.map(lambda _: VMEM, out) if outs is None else outs,
        scratch_shapes=scratch,
        compiler_params=pltpu.CompilerParams(vmem_limit_bytes=(64 << 20) - room),
        cost_estimate=pl.CostEstimate(flops=cost[0], bytes_accessed=cost[1], transcendentals=0),
    )


def local(grad_out, saved_input, gate_value, filter_taps, skip_gain, lang_ids, doc_ids, dro_weight):
    tokens = grad_out.shape[1]
    channels = grad_out.shape[2]
    pieces = lax.axis_size("ctx")
    members = lax.axis_size("dp")
    length = tokens * pieces
    span = channels // pieces
    mean_len = length / NDOCS
    tables, behind = all_tables(pieces, tokens)
    share = span // members
    joint = members if share * 2 % 128 == 0 and share // members % ROWS == 0 else 1
    if joint == 1:
        share = span
    taps = share // joint
    axes = ("dp", "ctx") if joint > 1 else "ctx"
    place = lax.axis_index("ctx")
    member = lax.axis_index("dp")
    first = place * span + (member * share if joint > 1 else 0)
    own = (place + member * pieces if joint > 1 else place).reshape(1)
    skip = lax.dynamic_slice_in_dim(skip_gain, first, share)
    skip = jnp.concatenate([skip, skip])[None, :]
    exchange = functools.partial(
        lax.all_to_all, axis_name=axes, split_axis=0, concat_axis=0, tiled=True
    )
    shape = jax.ShapeDtypeStruct
    dma = pltpu.SemaphoreType.DMA
    tall = places(tokens, share)[1]
    macs = pieces * (2 * tokens) ** 2 * span
    count = joint * pieces
    message = shape((count, taps + tall + ROWS, tokens), bf16)
    answer = shape((count, tall, tokens), bf16)
    groups = 4

    sent = call(
        functools.partial(prep_kernel, pieces, joint),
        message,
        [SMEM] + [HBM] * 4 + [VMEM] * 2,
        [
            pltpu.VMEM((tokens, channels), bf16),
            pltpu.VMEM((tokens, channels), bf16),
            pltpu.VMEM((tokens, channels), bf16),
            pltpu.VMEM(message.shape, bf16),
            dma((3, groups)),
            dma((joint,)),
            dma((3,)),
        ],
        outs=HBM,
        room=256 << 10,
        cost=(0, 4 << 20),
    )(
        (member if joint > 1 else jnp.zeros_like(member)).reshape(1),
        saved_input[0],
        grad_out[0],
        gate_value[0],
        filter_taps.reshape(pieces, span, tokens),
        doc_ids,
        lang_ids,
    )
    sent, cross, scale = call(
        functools.partial(conv_kernel, mean_len, joint),
        [answer, shape((pieces, 2 * tokens, share), bf16), shape((tokens, count), f32)],
        [VMEM, SMEM, VMEM, VMEM],
        [
            pltpu.VMEM((count, tokens, 2 * share), bf16),
            pltpu.VMEM((pieces, 2 * share, 2 * tokens), bf16),
            pltpu.VMEM((pieces, 2 * tokens, 2 * share * joint), bf16),
            pltpu.VMEM((pieces, 2 * tokens, 2 * share * joint), bf16),
            pltpu.VMEM((count, tokens), f32),
            pltpu.VMEM((count, tokens), f32),
        ],
        room=(40 << 20) if span % 128 == 0 else (20 << 20),
        cost=(10 * macs, 8 << 20),
    )(exchange(sent), dro_weight, skip, tables)
    got = exchange(sent)
    keep, send = call(
        lags_kernel,
        (
            shape((share, length // members), f32),
            shape((members - 1, share, length // members), bf16),
        ),
        [SMEM, VMEM, VMEM],
        [
            pltpu.VMEM((pieces, 2 * tokens, share), f32),
            pltpu.VMEM((pieces, tokens, share), f32),
        ],
        cost=(2 * macs, 6 << 20),
    )(member.reshape(1), cross, behind)
    rings = [[(d, (d + r) % members) for d in range(members)] for r in range(members)]
    came = [lax.ppermute(send[r - 1], "dp", rings[r]).astype(f32) for r in range(1, members)]
    if joint > 1:
        came = jnp.stack([keep] + came)
        d_filter = jnp.concatenate(
            [
                lax.dynamic_index_in_dim(came, (member - d) % members, 0, keepdims=False)
                for d in range(members)
            ]
        )
    else:
        d_filter = sum(came, keep)
    token_block = jax.ShapeDtypeStruct((tokens, channels), bf16)
    scaled = call(
        scaled_kernel,
        shape((tokens, channels), f32),
        [SMEM, VMEM, VMEM],
        cost=(0, 2 << 20),
    )(own, grad_out[0], scale)
    d_gate, d_input = call(
        functools.partial(final_kernel, joint),
        (token_block, token_block),
        [VMEM, VMEM],
        cost=(0, 4 << 20),
    )(scaled, got)
    return (d_input[None], d_gate[None], d_filter)


def solution(mesh):
    return jax.shard_map(
        local,
        mesh=mesh,
        in_specs=(
            P("dp", "ctx", None),
            P("dp", "ctx", None),
            P("dp", "ctx", None),
            P(None, "ctx"),
            P(),
            P("dp", "ctx"),
            P("dp", "ctx"),
            P(),
        ),
        out_specs=(P("dp", "ctx", None), P("dp", "ctx", None), P("ctx", "dp")),
        check_vma=False,
    )
```

```python
import functools
import math

import jax
import jax.numpy as jnp
import numpy as np
from jax import lax
from jax.experimental import pallas as pl
from jax.experimental.pallas import tpu as pltpu
from jax.sharding import PartitionSpec as P

NDOCS = 32
ROWS = 16
VMEM = pl.BlockSpec(memory_space=pltpu.VMEM)
HBM = pl.BlockSpec(memory_space=pltpu.HBM)
SMEM = pl.BlockSpec(memory_space=pltpu.SMEM)
f32 = jnp.float32
bf16 = jnp.bfloat16


def inner_tables(pieces, tokens):
    size = 2 * pieces * tokens
    m = np.arange(pieces)[:, None, None]
    k = np.arange(tokens)[None, :, None]
    q = np.arange(tokens)[None, None, :]
    turn = (q * (4 * m + 1 + 4 * pieces * k)) % (2 * size)
    angle = math.pi / size * turn
    cos, sin = np.cos(angle), np.sin(angle)
    ahead = np.concatenate(
        [np.concatenate([cos, sin], axis=2), np.concatenate([-sin, cos], axis=2)], axis=1
    )
    behind = np.swapaxes(ahead, 1, 2) * (2.0 / size)
    return ahead, behind


def outer_tables(pieces):
    m = np.arange(pieces)[:, None]
    j = np.arange(pieces)[None, :]
    angle = math.pi / (2 * pieces) * (j * (4 * m + 1) % (4 * pieces))
    both = np.stack([np.cos(angle), -np.sin(angle)], axis=1).reshape(2 * pieces, pieces)
    ahead = np.kron(both, np.eye(ROWS))
    return ahead, ahead.T


def side_by_side(table, width):
    return np.concatenate(np.split(table, table.shape[1] // width, axis=1), axis=0)


def all_tables(pieces, tokens):
    width = 2 * tokens
    ahead, behind = inner_tables(pieces, tokens)
    outer, inverse = outer_tables(pieces)
    parts = [
        ahead.reshape(-1, width),
        side_by_side(outer, width),
        side_by_side(inverse, width),
    ]
    return jnp.asarray(np.concatenate(parts, axis=0), bf16), jnp.asarray(behind, bf16)


def turned(value, turns):
    re, im = value
    turns = turns % 1.0
    if turns == 0.0:
        return value
    if turns == 0.25:
        return (-im, re)
    if turns == 0.5:
        return (-re, -im)
    if turns == 0.75:
        return (im, -re)
    cos, sin = math.cos(2.0 * math.pi * turns), math.sin(2.0 * math.pi * turns)
    if (turns * 8.0) % 1.0 == 0.0:
        root = math.sqrt(0.5)
        plus, minus = (re + im) * root, (re - im) * root
        if turns == 0.125:
            return (minus, plus)
        if turns == 0.375:
            return (-plus, minus)
        if turns == 0.625:
            return (-minus, -plus)
        return (plus, -minus)
    return (re * cos - im * sin, re * sin + im * cos)


def dft(values, sign):
    count = len(values)
    if count == 1:
        return values
    even, odd = dft(values[0::2], sign), dft(values[1::2], sign)
    first, second = [], []
    for k in range(count // 2):
        a, b = even[k], turned(odd[k], sign * k / count)
        first.append((a[0] + b[0], a[1] + b[1]))
        second.append((a[0] - b[0], a[1] - b[1]))
    return first + second


def outer_inverse(values):
    count = len(values)
    out = []
    for j, (re, im) in enumerate(dft(values, 1.0)):
        angle = math.pi * j / (2 * count)
        out.append(re if j == 0 else re * math.cos(angle) - im * math.sin(angle))
    return out


def chunked(total, body, unrolled=False):
    if unrolled:
        for i in range(total // ROWS):
            body(i * ROWS)
        return

    def step(i, carry):
        body(pl.multiple_of(i * ROWS, ROWS))
        return carry

    lax.fori_loop(0, total // ROWS, step, 0)


def each_piece(pieces, body, group=4):
    if group == pieces:
        for m in range(pieces):
            body(m)
        return

    def step(i, carry):
        for g in range(group):
            body(i * group + g)
        return carry

    lax.fori_loop(0, pieces // group, step, 0)


def dot(a, b):
    return lax.dot_general(a, b, (((1,), (0,)), ((), ())), preferred_element_type=f32)


def places(tokens, span):
    beside = max(1, tokens // span)

    def place(index, start):
        row = start + (index // beside) * tokens
        column = (index % beside) * span
        return row, slice(column, column + span)

    tall = -(-2 // beside) * tokens
    return place, tall


def copies(*pairs):
    started = [pltpu.make_async_copy(*pair) for pair in pairs]
    for copy in started:
        copy.start()
    return started


def finish(*started):
    for copy in started:
        copy.wait()


def row_copies(source, target, sems):
    count = sems.shape[0]
    group = source.shape[0] // count
    rows = [pl.ds(g * group, group) for g in range(count)]
    return copies(*[(source.at[r], target.at[r], sems.at[g]) for g, r in enumerate(rows)])


def prep_kernel(
    pieces,
    joint,
    own_ref,
    input_hbm,
    grad_hbm,
    gate_hbm,
    taps_hbm,
    doc_ref,
    lang_ref,
    out_hbm,
    input_ref,
    grad_ref,
    gate_ref,
    made_ref,
    in_sem,
    taps_sem,
    out_sem,
):
    tokens, channels = grad_ref.shape
    groups = in_sem.shape[1]
    span = channels // pieces
    share = span // joint
    taps = share // joint
    place, tall = places(tokens, share)
    in_row, in_lanes = place(0, taps)
    grad_row, grad_lanes = place(1, taps)
    owners = [(i, d) for i in range(pieces) for d in range(joint)]

    def send(part, start, size):
        rows = pl.ds(start, size)
        return copies((made_ref.at[:, :, rows, :], out_hbm.at[:, :, rows, :], out_sem.at[part]))

    input_in = row_copies(input_hbm, input_ref, in_sem.at[2])
    grad_in = row_copies(grad_hbm, grad_ref, in_sem.at[0])
    gate_in = row_copies(gate_hbm, gate_ref, in_sem.at[1])
    taps_in = []
    for d in range(joint):
        start = pl.multiple_of(d * share + own_ref[0] * taps, ROWS)
        taps_in += copies(
            (
                taps_hbm.at[:, pl.ds(start, taps), :],
                made_ref.at[:, d, pl.ds(0, taps), :],
                taps_sem.at[d],
            )
        )
    tile = lax.broadcasted_iota(jnp.int32, (ROWS, tokens), 0)
    ids = jnp.where(tile == 0, doc_ref[...], lang_ref[...]).astype(f32).astype(bf16)
    for i, d in owners:
        made_ref[i, d, taps + tall :, :] = ids
    group = tokens // groups
    sent = []
    for g in range(groups):
        finish(input_in[g])
        rows = slice(g * group, (g + 1) * group)
        at = slice(in_row + g * group, in_row + (g + 1) * group)
        for i, d in owners:
            part = slice(i * span + d * share, i * span + (d + 1) * share)
            made_ref[i, d, at, in_lanes] = input_ref[rows, part]
    finish(*taps_in)
    sent += send(0, 0, taps if grad_row == in_row else grad_row)
    for g in range(groups):
        finish(grad_in[g], gate_in[g])
        rows = slice(g * group, (g + 1) * group)
        at = slice(grad_row + g * group, grad_row + (g + 1) * group)
        made = (grad_ref[rows, :].astype(f32) * gate_ref[rows, :].astype(f32)).astype(bf16)
        for i, d in owners:
            part = slice(i * span + d * share, i * span + (d + 1) * share)
            made_ref[i, d, at, grad_lanes] = made[:, part]
        if g == groups // 2 - 1:
            sent += send(1, grad_row, (g + 1) * group)
    start = grad_row + tokens // 2
    sent += send(2, start, taps + tall + ROWS - start)
    finish(*sent)


def token_scale(message_ref, scale_ref, dro_ref, ids, pieces, mean_len, doc_ref, lang_ref):
    joint = message_ref.shape[0] // pieces
    for o in range(message_ref.shape[0]):
        rows = message_ref[o, ids:, :].astype(f32)
        at = (o % joint) * pieces + o // joint
        doc_ref[at : at + 1, :] = rows[0:1]
        lang_ref[at : at + 1, :] = rows[1:2]
    for start in range(0, message_ref.shape[0], pieces):
        own = slice(start, start + pieces)
        docs, langs = doc_ref[own, :], lang_ref[own, :]
        doc_len = jnp.zeros_like(docs)
        for d in range(NDOCS):
            hot = (docs == float(d)).astype(f32)
            doc_len = doc_len + hot * jnp.sum(hot, axis=(0, 1), keepdims=True)
        weight = jnp.zeros_like(langs)
        for g in range(dro_ref.shape[0]):
            weight = jnp.where(langs == float(g), dro_ref[g], weight)
        scale_ref[:, own] = (weight * (2.0 * mean_len) / (doc_len + mean_len)).T


def conv_kernel(
    mean_len,
    joint,
    message_ref,
    dro_ref,
    skip_ref,
    table_ref,
    behind_ref,
    out_ref,
    cross_ref,
    scale_ref,
    both_ref,
    taps_mid_ref,
    mid_ref,
    back_ref,
    doc_ref,
    lang_ref,
):
    pieces = message_ref.shape[0] // joint
    tokens = message_ref.shape[2]
    share = skip_ref.shape[1] // 2
    taps = share // joint
    place, tall = places(tokens, share)
    width = 2 * tokens
    slab = pieces * ROWS
    pair = 2 * share

    def ahead(m):
        return table_ref[m * width : (m + 1) * width, :]

    def blocks(start, rows, count):
        parts = [slice(start + b * rows, start + (b + 1) * rows) for b in range(count)]
        return jnp.concatenate([table_ref[part, :] for part in parts], axis=1)

    start = pieces * width
    outer_blocks = slab // width
    outer_table = blocks(start, 2 * slab, outer_blocks)
    inverse_table = blocks(start + 2 * slab * outer_blocks, slab, 2 * outer_blocks)
    token_scale(message_ref, scale_ref, dro_ref, taps + tall, pieces, mean_len, doc_ref, lang_ref)

    for d in range(joint):
        for row in range(0, taps, ROWS):
            held = [message_ref[j * joint + d, row : row + ROWS, :] for j in range(pieces)]
            out = dot(outer_table, jnp.concatenate(held, axis=0)).astype(bf16)
            for m in range(pieces):
                at = 2 * m * ROWS
                for first in (d * taps + row, share + d * taps + row):
                    rows = slice(first, first + ROWS)
                    taps_mid_ref[m, rows, :tokens] = out[at : at + ROWS]
                    taps_mid_ref[m, rows, tokens:] = out[at + ROWS : at + 2 * ROWS]

    lane = lax.broadcasted_iota(jnp.int32, (ROWS, pair), 1)

    def load(o, row):
        (one, one_lanes), (two, two_lanes) = place(0, taps), place(1, taps)
        if one == two:
            return message_ref[o, pl.ds(one + row, ROWS), slice(one_lanes.start, two_lanes.stop)]
        return jnp.concatenate(
            [message_ref[o, pl.ds(first + row, ROWS), :] for first in (one, two)], axis=1
        )

    def outer(row):
        rows = pl.ds(row, ROWS)
        stack = []
        for j in range(pieces):
            line = []
            for d in range(joint):
                o = j * joint + d
                at = d * pieces + j
                factor = jnp.where(lane < share, 1.0, scale_ref[rows, at : at + 1])
                made = (load(o, row).astype(f32) * factor).astype(bf16)
                both_ref[o, rows, :] = made
                line.append(made)
            stack.append(jnp.concatenate(line, axis=1))
        out = dot(outer_table, jnp.concatenate(stack, axis=0)).astype(bf16)
        for m in range(pieces):
            at = 2 * m * ROWS
            mid_ref[m, rows, :] = out[at : at + ROWS]
            mid_ref[m, pl.ds(tokens + row, ROWS), :] = out[at + ROWS : at + 2 * ROWS]

    chunked(tokens, outer, True)
    sign = jnp.where(lax.broadcasted_iota(jnp.int32, (tokens, pair), 1) < share, 1.0, -1.0)

    def inner(m):
        filt = lax.dot_general(
            ahead(m), taps_mid_ref[m], (((1,), (1,)), ((), ())), preferred_element_type=f32
        )
        spec = dot(ahead(m), mid_ref[m])
        fre, fim = filt[:tokens], filt[tokens:] * sign
        cre, cim, prods = 0.0, 0.0, []
        for d in range(joint):
            part = slice(d * pair, (d + 1) * pair)
            re, im = spec[:tokens, part], spec[tokens:, part]
            xre, gre, xim, gim = re[:, :share], re[:, share:], im[:, :share], im[:, share:]
            cre, cim = cre + (xre * gre + xim * gim), cim + (xre * gim - xim * gre)
            prods.append(jnp.concatenate([fre * re - fim * im, fre * im + fim * re], axis=0))
        cross_ref[m, :tokens, :] = cre.astype(bf16)
        cross_ref[m, tokens:, :] = cim.astype(bf16)
        prods = jnp.concatenate([prod.astype(bf16) for prod in prods], axis=1)
        back_ref[m] = dot(behind_ref[m], prods).astype(bf16)

    each_piece(pieces, inner, pieces)
    skip = skip_ref[...]

    def outer_back(row):
        rows = pl.ds(row, ROWS)
        stack = []
        for m in range(pieces):
            stack += [back_ref[m, rows, :], back_ref[m, pl.ds(tokens + row, ROWS), :]]
        out = dot(inverse_table, jnp.concatenate(stack, axis=0))
        (one, one_lanes), (two, two_lanes) = place(0, 0), place(1, 0)
        for j in range(pieces):
            for d in range(joint):
                o = j * joint + d
                value = out[j * ROWS : (j + 1) * ROWS, d * pair : (d + 1) * pair]
                value = (value + skip * both_ref[o, rows, :].astype(f32)).astype(bf16)
                if one == two:
                    out_ref[o, rows, slice(one_lanes.start, two_lanes.stop)] = value
                else:
                    out_ref[o, rows, :] = value[:, :share]
                    out_ref[o, pl.ds(two + row, ROWS), :] = value[:, share:]

    chunked(tokens, outer_back, True)


def lags_kernel(own_ref, cross_ref, behind_ref, keep_ref, send_ref, back_ref, lag_ref):
    pieces, tall, span = cross_ref.shape
    tokens = tall // 2
    held = keep_ref.shape[1] // tokens
    members = pieces // held

    def inner(m):
        back_ref[m] = dot(behind_ref[m], cross_ref[m])

    each_piece(pieces, inner)

    def body(row):
        out = outer_inverse(
            [
                (back_ref[m, pl.ds(row, ROWS), :], back_ref[m, pl.ds(tokens + row, ROWS), :])
                for m in range(pieces)
            ]
        )
        for j in range(pieces):
            lag_ref[j, pl.ds(row, ROWS), :] = out[j]

    chunked(tokens, body)
    for j in range(held):
        part = slice(j * tokens, (j + 1) * tokens)
        keep_ref[:, part] = lag_ref[own_ref[0] * held + j].T
        for r in range(1, members):
            other = lax.rem(own_ref[0] + r, members)
            send_ref[r - 1, :, part] = lag_ref[other * held + j].T.astype(bf16)


def scaled_kernel(own_ref, grad_ref, scale_ref, out_ref):
    lane = lax.broadcasted_iota(jnp.int32, scale_ref.shape, 1)
    scale = jnp.where(lane == own_ref[0], scale_ref[...], jnp.zeros(scale_ref.shape, f32))
    out_ref[...] = grad_ref[...].astype(f32) * jnp.sum(scale, axis=1, keepdims=True)


def final_kernel(joint, scaled_ref, message_ref, gate_ref, input_ref):
    pieces = message_ref.shape[0] // joint
    tokens, channels = scaled_ref.shape
    span = channels // pieces
    share = span // joint
    place, _ = places(tokens, share)
    mixed_row, mixed_lanes = place(0, 0)
    back_row, back_lanes = place(1, 0)
    for i in range(pieces):
        owners = [i * joint + d for d in range(joint)]
        mixed = [message_ref[o, mixed_row : mixed_row + tokens, mixed_lanes] for o in owners]
        back = [message_ref[o, back_row : back_row + tokens, back_lanes] for o in owners]
        part = slice(i * span, (i + 1) * span)
        mixed = jnp.concatenate(mixed, axis=1).astype(f32)
        gate_ref[:, part] = (scaled_ref[:, part] * mixed).astype(bf16)
        input_ref[:, part] = jnp.concatenate(back, axis=1)


def call(kernel, out, ins, scratch=(), outs=None, room=40 << 20, cost=(0, 0)):
    return pl.pallas_call(
        kernel,
        out_shape=out,
        in_specs=ins,
        out_specs=jax.tree.map(lambda _: VMEM, out) if outs is None else outs,
        scratch_shapes=scratch,
        compiler_params=pltpu.CompilerParams(vmem_limit_bytes=(64 << 20) - room),
        cost_estimate=pl.CostEstimate(flops=cost[0], bytes_accessed=cost[1], transcendentals=0),
    )


def local(grad_out, saved_input, gate_value, filter_taps, skip_gain, lang_ids, doc_ids, dro_weight):
    tokens = grad_out.shape[1]
    channels = grad_out.shape[2]
    pieces = lax.axis_size("ctx")
    members = lax.axis_size("dp")
    length = tokens * pieces
    span = channels // pieces
    mean_len = length / NDOCS
    tables, behind = all_tables(pieces, tokens)
    share = span // members
    joint = members if share * 2 % 128 == 0 and share // members % ROWS == 0 else 1
    if joint == 1:
        share = span
    taps = share // joint
    axes = ("ctx", "dp") if joint > 1 else "ctx"
    place = lax.axis_index("ctx")
    member = lax.axis_index("dp")
    first = place * span + (member * share if joint > 1 else 0)
    own = (place + member * pieces if joint > 1 else place).reshape(1)
    skip = lax.dynamic_slice_in_dim(skip_gain, first, share)
    skip = jnp.concatenate([skip, skip])[None, :]
    exchange = functools.partial(
        lax.all_to_all, axis_name=axes, split_axis=0, concat_axis=0, tiled=True
    )
    shape = jax.ShapeDtypeStruct
    dma = pltpu.SemaphoreType.DMA
    tall = places(tokens, share)[1]
    macs = pieces * (2 * tokens) ** 2 * span
    count = joint * pieces
    message = shape((pieces, joint, taps + tall + ROWS, tokens), bf16)
    answer = shape((count, tall, tokens), bf16)
    groups = 4

    sent = call(
        functools.partial(prep_kernel, pieces, joint),
        message,
        [SMEM] + [HBM] * 4 + [VMEM] * 2,
        [
            pltpu.VMEM((tokens, channels), bf16),
            pltpu.VMEM((tokens, channels), bf16),
            pltpu.VMEM((tokens, channels), bf16),
            pltpu.VMEM(message.shape, bf16),
            dma((3, groups)),
            dma((joint,)),
            dma((3,)),
        ],
        outs=HBM,
        room=256 << 10,
        cost=(0, 4 << 20),
    )(
        (member if joint > 1 else jnp.zeros_like(member)).reshape(1),
        saved_input[0],
        grad_out[0],
        gate_value[0],
        filter_taps.reshape(pieces, span, tokens),
        doc_ids,
        lang_ids,
    )
    sent, cross, scale = call(
        functools.partial(conv_kernel, mean_len, joint),
        [answer, shape((pieces, 2 * tokens, share), bf16), shape((tokens, count), f32)],
        [VMEM, SMEM, VMEM, VMEM, VMEM],
        [
            pltpu.VMEM((count, tokens, 2 * share), bf16),
            pltpu.VMEM((pieces, 2 * share, 2 * tokens), bf16),
            pltpu.VMEM((pieces, 2 * tokens, 2 * share * joint), bf16),
            pltpu.VMEM((pieces, 2 * tokens, 2 * share * joint), bf16),
            pltpu.VMEM((count, tokens), f32),
            pltpu.VMEM((count, tokens), f32),
        ],
        room=(40 << 20) if span % 128 == 0 else (20 << 20),
        cost=(10 * macs, 8 << 20),
    )(exchange(sent.reshape(count, -1, tokens)), dro_weight, skip, tables, behind)
    got = exchange(sent)
    keep, send = call(
        lags_kernel,
        (
            shape((share, length // members), f32),
            shape((members - 1, share, length // members), bf16),
        ),
        [SMEM, VMEM, VMEM],
        [
            pltpu.VMEM((pieces, 2 * tokens, share), f32),
            pltpu.VMEM((pieces, tokens, share), f32),
        ],
        cost=(2 * macs, 6 << 20),
    )(member.reshape(1), cross, behind)
    rings = [[(d, (d + r) % members) for d in range(members)] for r in range(members)]
    came = [lax.ppermute(send[r - 1], "dp", rings[r]).astype(f32) for r in range(1, members)]
    if joint > 1:
        came = jnp.stack([keep] + came)
        d_filter = jnp.concatenate(
            [
                lax.dynamic_index_in_dim(came, (member - d) % members, 0, keepdims=False)
                for d in range(members)
            ]
        )
    else:
        d_filter = sum(came, keep)
    token_block = jax.ShapeDtypeStruct((tokens, channels), bf16)
    scaled = call(
        scaled_kernel,
        shape((tokens, channels), f32),
        [SMEM, VMEM, VMEM],
        cost=(0, 2 << 20),
    )(own, grad_out[0], scale)
    d_gate, d_input = call(
        functools.partial(final_kernel, joint),
        (token_block, token_block),
        [VMEM, VMEM],
        cost=(0, 4 << 20),
    )(scaled, got)
    return (d_input[None], d_gate[None], d_filter)


def solution(mesh):
    return jax.shard_map(
        local,
        mesh=mesh,
        in_specs=(
            P("dp", "ctx", None),
            P("dp", "ctx", None),
            P("dp", "ctx", None),
            P(None, "ctx"),
            P(),
            P("dp", "ctx"),
            P("dp", "ctx"),
            P(),
        ),
        out_specs=(P("dp", "ctx", None), P("dp", "ctx", None), P("ctx", "dp")),
        check_vma=False,
    )
```

```python
import functools
import math

import jax
import jax.numpy as jnp
import numpy as np
from jax import lax
from jax.experimental import pallas as pl
from jax.experimental.pallas import tpu as pltpu
from jax.sharding import PartitionSpec as P

NDOCS = 32
ROWS = 16
VMEM = pl.BlockSpec(memory_space=pltpu.VMEM)
HBM = pl.BlockSpec(memory_space=pltpu.HBM)
SMEM = pl.BlockSpec(memory_space=pltpu.SMEM)
f32 = jnp.float32
bf16 = jnp.bfloat16


def inner_tables(pieces, tokens):
    size = 2 * pieces * tokens
    m = np.arange(pieces)[:, None, None]
    k = np.arange(tokens)[None, :, None]
    q = np.arange(tokens)[None, None, :]
    turn = (q * (4 * m + 1 + 4 * pieces * k)) % (2 * size)
    angle = math.pi / size * turn
    cos, sin = np.cos(angle), np.sin(angle)
    ahead = np.concatenate(
        [np.concatenate([cos, sin], axis=2), np.concatenate([-sin, cos], axis=2)], axis=1
    )
    behind = np.swapaxes(ahead, 1, 2) * (2.0 / size)
    return ahead, behind


def outer_tables(pieces):
    m = np.arange(pieces)[:, None]
    j = np.arange(pieces)[None, :]
    angle = math.pi / (2 * pieces) * (j * (4 * m + 1) % (4 * pieces))
    both = np.stack([np.cos(angle), -np.sin(angle)], axis=1).reshape(2 * pieces, pieces)
    ahead = np.kron(both, np.eye(ROWS))
    return ahead, ahead.T


def side_by_side(table, width):
    return np.concatenate(np.split(table, table.shape[1] // width, axis=1), axis=0)


def all_tables(pieces, tokens):
    width = 2 * tokens
    ahead, behind = inner_tables(pieces, tokens)
    outer, inverse = outer_tables(pieces)
    parts = [
        ahead.reshape(-1, width),
        side_by_side(outer, width),
        side_by_side(inverse, width),
    ]
    return jnp.asarray(np.concatenate(parts, axis=0), bf16), jnp.asarray(behind, bf16)


def turned(value, turns):
    re, im = value
    turns = turns % 1.0
    if turns == 0.0:
        return value
    if turns == 0.25:
        return (-im, re)
    if turns == 0.5:
        return (-re, -im)
    if turns == 0.75:
        return (im, -re)
    cos, sin = math.cos(2.0 * math.pi * turns), math.sin(2.0 * math.pi * turns)
    if (turns * 8.0) % 1.0 == 0.0:
        root = math.sqrt(0.5)
        plus, minus = (re + im) * root, (re - im) * root
        if turns == 0.125:
            return (minus, plus)
        if turns == 0.375:
            return (-plus, minus)
        if turns == 0.625:
            return (-minus, -plus)
        return (plus, -minus)
    return (re * cos - im * sin, re * sin + im * cos)


def dft(values, sign):
    count = len(values)
    if count == 1:
        return values
    even, odd = dft(values[0::2], sign), dft(values[1::2], sign)
    first, second = [], []
    for k in range(count // 2):
        a, b = even[k], turned(odd[k], sign * k / count)
        first.append((a[0] + b[0], a[1] + b[1]))
        second.append((a[0] - b[0], a[1] - b[1]))
    return first + second


def outer_inverse(values):
    count = len(values)
    out = []
    for j, (re, im) in enumerate(dft(values, 1.0)):
        angle = math.pi * j / (2 * count)
        out.append(re if j == 0 else re * math.cos(angle) - im * math.sin(angle))
    return out


def chunked(total, body, unrolled=False):
    if unrolled:
        for i in range(total // ROWS):
            body(i * ROWS)
        return

    def step(i, carry):
        body(pl.multiple_of(i * ROWS, ROWS))
        return carry

    lax.fori_loop(0, total // ROWS, step, 0)


def each_piece(pieces, body, group=4):
    if group == pieces:
        for m in range(pieces):
            body(m)
        return

    def step(i, carry):
        for g in range(group):
            body(i * group + g)
        return carry

    lax.fori_loop(0, pieces // group, step, 0)


def dot(a, b):
    return lax.dot_general(a, b, (((1,), (0,)), ((), ())), preferred_element_type=f32)


def places(tokens, span):
    beside = max(1, tokens // span)

    def place(index, start):
        row = start + (index // beside) * tokens
        column = (index % beside) * span
        return row, slice(column, column + span)

    tall = -(-2 // beside) * tokens
    return place, tall


def copies(*pairs):
    started = [pltpu.make_async_copy(*pair) for pair in pairs]
    for copy in started:
        copy.start()
    return started


def finish(*started):
    for copy in started:
        copy.wait()


def row_copies(source, target, sems):
    count = sems.shape[0]
    group = source.shape[0] // count
    rows = [pl.ds(g * group, group) for g in range(count)]
    return copies(*[(source.at[r], target.at[r], sems.at[g]) for g, r in enumerate(rows)])


def prep_kernel(
    pieces,
    joint,
    own_ref,
    input_hbm,
    grad_hbm,
    gate_hbm,
    taps_hbm,
    doc_ref,
    lang_ref,
    out_hbm,
    input_ref,
    grad_ref,
    gate_ref,
    made_ref,
    in_sem,
    taps_sem,
    out_sem,
):
    tokens, channels = grad_ref.shape
    groups = in_sem.shape[1]
    span = channels // pieces
    share = span // joint
    taps = share // joint
    place, tall = places(tokens, share)
    in_row, in_lanes = place(0, taps)
    grad_row, grad_lanes = place(1, taps)
    owners = [(i, d) for i in range(pieces) for d in range(joint)]

    def send(part, start, size):
        rows = pl.ds(start, size)
        return copies((made_ref.at[:, :, rows, :], out_hbm.at[:, :, rows, :], out_sem.at[part]))

    input_in = row_copies(input_hbm, input_ref, in_sem.at[2])
    grad_in = row_copies(grad_hbm, grad_ref, in_sem.at[0])
    gate_in = row_copies(gate_hbm, gate_ref, in_sem.at[1])
    taps_in = []
    for d in range(joint):
        start = pl.multiple_of(d * share + own_ref[0] * taps, ROWS)
        taps_in += copies(
            (
                taps_hbm.at[:, pl.ds(start, taps), :],
                made_ref.at[:, d, pl.ds(0, taps), :],
                taps_sem.at[d],
            )
        )
    tile = lax.broadcasted_iota(jnp.int32, (ROWS, tokens), 0)
    ids = jnp.where(tile == 0, doc_ref[...], lang_ref[...]).astype(f32).astype(bf16)
    for i, d in owners:
        made_ref[i, d, taps + tall :, :] = ids
    group = tokens // groups
    sent = []
    for g in range(groups):
        finish(input_in[g])
        rows = slice(g * group, (g + 1) * group)
        at = slice(in_row + g * group, in_row + (g + 1) * group)
        for i, d in owners:
            part = slice(i * span + d * share, i * span + (d + 1) * share)
            made_ref[i, d, at, in_lanes] = input_ref[rows, part]
    finish(*taps_in)
    sent += send(0, 0, taps if grad_row == in_row else grad_row)
    for g in range(groups):
        finish(grad_in[g], gate_in[g])
        rows = slice(g * group, (g + 1) * group)
        at = slice(grad_row + g * group, grad_row + (g + 1) * group)
        made = (grad_ref[rows, :].astype(f32) * gate_ref[rows, :].astype(f32)).astype(bf16)
        for i, d in owners:
            part = slice(i * span + d * share, i * span + (d + 1) * share)
            made_ref[i, d, at, grad_lanes] = made[:, part]
        if g == groups // 2 - 1:
            sent += send(1, grad_row, (g + 1) * group)
    start = grad_row + tokens // 2
    sent += send(2, start, taps + tall + ROWS - start)
    finish(*sent)


def token_scale(message_ref, scale_ref, dro_ref, ids, pieces, mean_len, doc_ref, lang_ref):
    joint = message_ref.shape[0] // pieces
    for o in range(message_ref.shape[0]):
        rows = message_ref[o, ids:, :].astype(f32)
        at = (o % joint) * pieces + o // joint
        doc_ref[at : at + 1, :] = rows[0:1]
        lang_ref[at : at + 1, :] = rows[1:2]
    for start in range(0, message_ref.shape[0], pieces):
        own = slice(start, start + pieces)
        docs, langs = doc_ref[own, :], lang_ref[own, :]
        doc_len = jnp.zeros_like(docs)
        for d in range(NDOCS):
            hot = (docs == float(d)).astype(f32)
            doc_len = doc_len + hot * jnp.sum(hot, axis=(0, 1), keepdims=True)
        weight = jnp.zeros_like(langs)
        for g in range(dro_ref.shape[0]):
            weight = jnp.where(langs == float(g), dro_ref[g], weight)
        scale_ref[:, own] = (weight * (2.0 * mean_len) / (doc_len + mean_len)).T


def conv_kernel(
    mean_len,
    joint,
    message_ref,
    dro_ref,
    skip_ref,
    table_ref,
    behind_ref,
    out_ref,
    cross_ref,
    scale_ref,
    both_ref,
    taps_mid_ref,
    mid_ref,
    back_ref,
    doc_ref,
    lang_ref,
):
    pieces = message_ref.shape[0] // joint
    tokens = message_ref.shape[2]
    share = skip_ref.shape[1] // 2
    taps = share // joint
    place, tall = places(tokens, share)
    width = 2 * tokens
    slab = pieces * ROWS
    pair = 2 * share

    def ahead(m):
        return table_ref[m * width : (m + 1) * width, :]

    def blocks(start, rows, count):
        parts = [slice(start + b * rows, start + (b + 1) * rows) for b in range(count)]
        return jnp.concatenate([table_ref[part, :] for part in parts], axis=1)

    start = pieces * width
    outer_blocks = slab // width
    outer_table = blocks(start, 2 * slab, outer_blocks)
    inverse_table = blocks(start + 2 * slab * outer_blocks, slab, 2 * outer_blocks)
    token_scale(message_ref, scale_ref, dro_ref, taps + tall, pieces, mean_len, doc_ref, lang_ref)

    for d in range(joint):
        for row in range(0, taps, ROWS):
            held = [message_ref[j * joint + d, row : row + ROWS, :] for j in range(pieces)]
            out = dot(outer_table, jnp.concatenate(held, axis=0)).astype(bf16)
            for m in range(pieces):
                at = 2 * m * ROWS
                for first in (d * taps + row, share + d * taps + row):
                    rows = slice(first, first + ROWS)
                    taps_mid_ref[m, rows, :tokens] = out[at : at + ROWS]
                    taps_mid_ref[m, rows, tokens:] = out[at + ROWS : at + 2 * ROWS]

    lane = lax.broadcasted_iota(jnp.int32, (ROWS, pair), 1)

    def load(o, row):
        (one, one_lanes), (two, two_lanes) = place(0, taps), place(1, taps)
        if one == two:
            return message_ref[o, pl.ds(one + row, ROWS), slice(one_lanes.start, two_lanes.stop)]
        return jnp.concatenate(
            [message_ref[o, pl.ds(first + row, ROWS), :] for first in (one, two)], axis=1
        )

    def outer(row):
        rows = pl.ds(row, ROWS)
        stack = []
        for j in range(pieces):
            line = []
            for d in range(joint):
                o = j * joint + d
                at = d * pieces + j
                factor = jnp.where(lane < share, 1.0, scale_ref[rows, at : at + 1])
                made = (load(o, row).astype(f32) * factor).astype(bf16)
                both_ref[o, rows, :] = made
                line.append(made)
            stack.append(jnp.concatenate(line, axis=1))
        out = dot(outer_table, jnp.concatenate(stack, axis=0)).astype(bf16)
        for m in range(pieces):
            at = 2 * m * ROWS
            mid_ref[m, rows, :] = out[at : at + ROWS]
            mid_ref[m, pl.ds(tokens + row, ROWS), :] = out[at + ROWS : at + 2 * ROWS]

    chunked(tokens, outer, True)
    sign = jnp.where(lax.broadcasted_iota(jnp.int32, (tokens, pair), 1) < share, 1.0, -1.0)

    def inner(m):
        filt = lax.dot_general(
            ahead(m), taps_mid_ref[m], (((1,), (1,)), ((), ())), preferred_element_type=f32
        )
        spec = dot(ahead(m), mid_ref[m])
        fre, fim = filt[:tokens], filt[tokens:] * sign
        cre, cim, prods = 0.0, 0.0, []
        for d in range(joint):
            part = slice(d * pair, (d + 1) * pair)
            re, im = spec[:tokens, part], spec[tokens:, part]
            xre, gre, xim, gim = re[:, :share], re[:, share:], im[:, :share], im[:, share:]
            cre, cim = cre + (xre * gre + xim * gim), cim + (xre * gim - xim * gre)
            prods.append(jnp.concatenate([fre * re - fim * im, fre * im + fim * re], axis=0))
        cross_ref[m, :tokens, :] = cre.astype(bf16)
        cross_ref[m, tokens:, :] = cim.astype(bf16)
        prods = jnp.concatenate([prod.astype(bf16) for prod in prods], axis=1)
        back_ref[m] = dot(behind_ref[m], prods).astype(bf16)

    each_piece(pieces, inner, pieces)
    skip = skip_ref[...]

    def outer_back(row):
        rows = pl.ds(row, ROWS)
        stack = []
        for m in range(pieces):
            stack += [back_ref[m, rows, :], back_ref[m, pl.ds(tokens + row, ROWS), :]]
        out = dot(inverse_table, jnp.concatenate(stack, axis=0))
        (one, one_lanes), (two, two_lanes) = place(0, 0), place(1, 0)
        for j in range(pieces):
            for d in range(joint):
                o = j * joint + d
                value = out[j * ROWS : (j + 1) * ROWS, d * pair : (d + 1) * pair]
                value = (value + skip * both_ref[o, rows, :].astype(f32)).astype(bf16)
                if one == two:
                    out_ref[o, rows, slice(one_lanes.start, two_lanes.stop)] = value
                else:
                    out_ref[o, rows, :] = value[:, :share]
                    out_ref[o, pl.ds(two + row, ROWS), :] = value[:, share:]

    chunked(tokens, outer_back, True)


def lags_kernel(own_ref, cross_ref, behind_ref, keep_ref, send_ref, back_ref, lag_ref):
    pieces, tall, span = cross_ref.shape
    tokens = tall // 2
    held = keep_ref.shape[1] // tokens
    members = pieces // held

    def inner(m):
        back_ref[m] = dot(behind_ref[m], cross_ref[m])

    each_piece(pieces, inner)

    def body(row):
        out = outer_inverse(
            [
                (back_ref[m, pl.ds(row, ROWS), :], back_ref[m, pl.ds(tokens + row, ROWS), :])
                for m in range(pieces)
            ]
        )
        for j in range(pieces):
            lag_ref[j, pl.ds(row, ROWS), :] = out[j]

    chunked(tokens, body)
    for j in range(held):
        part = slice(j * tokens, (j + 1) * tokens)
        keep_ref[:, part] = lag_ref[own_ref[0] * held + j].T
        for r in range(1, members):
            other = lax.rem(own_ref[0] + r, members)
            send_ref[r - 1, :, part] = lag_ref[other * held + j].T.astype(bf16)


def scaled_kernel(own_ref, grad_ref, scale_ref, out_ref):
    lane = lax.broadcasted_iota(jnp.int32, scale_ref.shape, 1)
    scale = jnp.where(lane == own_ref[0], scale_ref[...], jnp.zeros(scale_ref.shape, f32))
    out_ref[...] = grad_ref[...].astype(f32) * jnp.sum(scale, axis=1, keepdims=True)


def final_kernel(joint, scaled_ref, message_ref, gate_ref, input_ref):
    pieces = message_ref.shape[0] // joint
    tokens, channels = scaled_ref.shape
    span = channels // pieces
    share = span // joint
    place, _ = places(tokens, share)
    mixed_row, mixed_lanes = place(0, 0)
    back_row, back_lanes = place(1, 0)
    for i in range(pieces):
        owners = [i * joint + d for d in range(joint)]
        mixed = [message_ref[o, mixed_row : mixed_row + tokens, mixed_lanes] for o in owners]
        back = [message_ref[o, back_row : back_row + tokens, back_lanes] for o in owners]
        part = slice(i * span, (i + 1) * span)
        mixed = jnp.concatenate(mixed, axis=1).astype(f32)
        gate_ref[:, part] = (scaled_ref[:, part] * mixed).astype(bf16)
        input_ref[:, part] = jnp.concatenate(back, axis=1)


def call(kernel, out, ins, scratch=(), outs=None, room=40 << 20, cost=(0, 0)):
    return pl.pallas_call(
        kernel,
        out_shape=out,
        in_specs=ins,
        out_specs=jax.tree.map(lambda _: VMEM, out) if outs is None else outs,
        scratch_shapes=scratch,
        compiler_params=pltpu.CompilerParams(vmem_limit_bytes=(64 << 20) - room),
        cost_estimate=pl.CostEstimate(flops=cost[0], bytes_accessed=cost[1], transcendentals=0),
    )


def local(grad_out, saved_input, gate_value, filter_taps, skip_gain, lang_ids, doc_ids, dro_weight):
    tokens = grad_out.shape[1]
    channels = grad_out.shape[2]
    pieces = lax.axis_size("ctx")
    members = lax.axis_size("dp")
    length = tokens * pieces
    span = channels // pieces
    mean_len = length / NDOCS
    tables, behind = all_tables(pieces, tokens)
    share = span // members
    joint = members if share * 2 % 128 == 0 and share // members % ROWS == 0 else 1
    if joint == 1:
        share = span
    taps = share // joint
    axes = ("ctx", "dp") if joint > 1 else "ctx"
    place = lax.axis_index("ctx")
    member = lax.axis_index("dp")
    first = place * span + (member * share if joint > 1 else 0)
    own = (place + member * pieces if joint > 1 else place).reshape(1)
    skip = lax.dynamic_slice_in_dim(skip_gain, first, share)
    skip = jnp.concatenate([skip, skip])[None, :]
    exchange = functools.partial(
        lax.all_to_all, axis_name=axes, split_axis=0, concat_axis=0, tiled=True
    )
    shape = jax.ShapeDtypeStruct
    dma = pltpu.SemaphoreType.DMA
    tall = places(tokens, share)[1]
    macs = pieces * (2 * tokens) ** 2 * span
    count = joint * pieces
    message = shape((pieces, joint, taps + tall + ROWS, tokens), bf16)
    answer = shape((count, tall, tokens), bf16)
    groups = 4

    sent = call(
        functools.partial(prep_kernel, pieces, joint),
        message,
        [SMEM] + [HBM] * 4 + [VMEM] * 2,
        [
            pltpu.VMEM((tokens, channels), bf16),
            pltpu.VMEM((tokens, channels), bf16),
            pltpu.VMEM((tokens, channels), bf16),
            pltpu.VMEM(message.shape, bf16),
            dma((3, groups)),
            dma((joint,)),
            dma((3,)),
        ],
        outs=HBM,
        room=256 << 10,
        cost=(0, 4 << 20),
    )(
        (member if joint > 1 else jnp.zeros_like(member)).reshape(1),
        saved_input[0],
        grad_out[0],
        gate_value[0],
        filter_taps.reshape(pieces, span, tokens),
        doc_ids,
        lang_ids,
    )
    sent, cross, scale = call(
        functools.partial(conv_kernel, mean_len, joint),
        [answer, shape((pieces, 2 * tokens, share), bf16), shape((tokens, count), f32)],
        [VMEM, SMEM, VMEM, VMEM, VMEM],
        [
            pltpu.VMEM((count, tokens, 2 * share), bf16),
            pltpu.VMEM((pieces, 2 * share, 2 * tokens), bf16),
            pltpu.VMEM((pieces, 2 * tokens, 2 * share * joint), bf16),
            pltpu.VMEM((pieces, 2 * tokens, 2 * share * joint), bf16),
            pltpu.VMEM((count, tokens), f32),
            pltpu.VMEM((count, tokens), f32),
        ],
        room=(14 << 20) if span % 128 == 0 else (20 << 20),
        cost=(10 * macs, 8 << 20),
    )(exchange(sent.reshape(count, -1, tokens)), dro_weight, skip, tables, behind)
    got = exchange(sent)
    keep, send = call(
        lags_kernel,
        (
            shape((share, length // members), f32),
            shape((members - 1, share, length // members), bf16),
        ),
        [SMEM, VMEM, VMEM],
        [
            pltpu.VMEM((pieces, 2 * tokens, share), f32),
            pltpu.VMEM((pieces, tokens, share), f32),
        ],
        cost=(2 * macs, 6 << 20),
    )(member.reshape(1), cross, behind)
    rings = [[(d, (d + r) % members) for d in range(members)] for r in range(members)]
    came = [lax.ppermute(send[r - 1], "dp", rings[r]).astype(f32) for r in range(1, members)]
    if joint > 1:
        came = jnp.stack([keep] + came)
        d_filter = jnp.concatenate(
            [
                lax.dynamic_index_in_dim(came, (member - d) % members, 0, keepdims=False)
                for d in range(members)
            ]
        )
    else:
        d_filter = sum(came, keep)
    token_block = jax.ShapeDtypeStruct((tokens, channels), bf16)
    scaled = call(
        scaled_kernel,
        shape((tokens, channels), f32),
        [SMEM, VMEM, VMEM],
        cost=(0, 2 << 20),
    )(own, grad_out[0], scale)
    d_gate, d_input = call(
        functools.partial(final_kernel, joint),
        (token_block, token_block),
        [VMEM, VMEM],
        cost=(0, 4 << 20),
    )(scaled, got)
    return (d_input[None], d_gate[None], d_filter)


def solution(mesh):
    return jax.shard_map(
        local,
        mesh=mesh,
        in_specs=(
            P("dp", "ctx", None),
            P("dp", "ctx", None),
            P("dp", "ctx", None),
            P(None, "ctx"),
            P(),
            P("dp", "ctx"),
            P("dp", "ctx"),
            P(),
        ),
        out_specs=(P("dp", "ctx", None), P("dp", "ctx", None), P("ctx", "dp")),
        check_vma=False,
    )
```

```python
import functools
import math

import jax
import jax.numpy as jnp
import numpy as np
from jax import lax
from jax.experimental import pallas as pl
from jax.experimental.pallas import tpu as pltpu
from jax.sharding import PartitionSpec as P

NDOCS = 32
ROWS = 16
VMEM = pl.BlockSpec(memory_space=pltpu.VMEM)
HBM = pl.BlockSpec(memory_space=pltpu.HBM)
SMEM = pl.BlockSpec(memory_space=pltpu.SMEM)
f32 = jnp.float32
bf16 = jnp.bfloat16


def inner_tables(pieces, tokens):
    size = 2 * pieces * tokens
    m = np.arange(pieces)[:, None, None]
    k = np.arange(tokens)[None, :, None]
    q = np.arange(tokens)[None, None, :]
    turn = (q * (4 * m + 1 + 4 * pieces * k)) % (2 * size)
    angle = math.pi / size * turn
    cos, sin = np.cos(angle), np.sin(angle)
    ahead = np.concatenate(
        [np.concatenate([cos, sin], axis=2), np.concatenate([-sin, cos], axis=2)], axis=1
    )
    behind = np.swapaxes(ahead, 1, 2) * (2.0 / size)
    return ahead, behind


def outer_tables(pieces):
    m = np.arange(pieces)[:, None]
    j = np.arange(pieces)[None, :]
    angle = math.pi / (2 * pieces) * (j * (4 * m + 1) % (4 * pieces))
    both = np.stack([np.cos(angle), -np.sin(angle)], axis=1).reshape(2 * pieces, pieces)
    ahead = np.kron(both, np.eye(ROWS))
    return ahead, ahead.T


def side_by_side(table, width):
    return np.concatenate(np.split(table, table.shape[1] // width, axis=1), axis=0)


def all_tables(pieces, tokens):
    width = 2 * tokens
    ahead, behind = inner_tables(pieces, tokens)
    outer, inverse = outer_tables(pieces)
    parts = [
        ahead.reshape(-1, width),
        side_by_side(outer, width),
        side_by_side(inverse, width),
    ]
    return jnp.asarray(np.concatenate(parts, axis=0), bf16), jnp.asarray(behind, bf16)


def turned(value, turns):
    re, im = value
    turns = turns % 1.0
    if turns == 0.0:
        return value
    if turns == 0.25:
        return (-im, re)
    if turns == 0.5:
        return (-re, -im)
    if turns == 0.75:
        return (im, -re)
    cos, sin = math.cos(2.0 * math.pi * turns), math.sin(2.0 * math.pi * turns)
    if (turns * 8.0) % 1.0 == 0.0:
        root = math.sqrt(0.5)
        plus, minus = (re + im) * root, (re - im) * root
        if turns == 0.125:
            return (minus, plus)
        if turns == 0.375:
            return (-plus, minus)
        if turns == 0.625:
            return (-minus, -plus)
        return (plus, -minus)
    return (re * cos - im * sin, re * sin + im * cos)


def dft(values, sign):
    count = len(values)
    if count == 1:
        return values
    even, odd = dft(values[0::2], sign), dft(values[1::2], sign)
    first, second = [], []
    for k in range(count // 2):
        a, b = even[k], turned(odd[k], sign * k / count)
        first.append((a[0] + b[0], a[1] + b[1]))
        second.append((a[0] - b[0], a[1] - b[1]))
    return first + second


def outer_inverse(values):
    count = len(values)
    out = []
    for j, (re, im) in enumerate(dft(values, 1.0)):
        angle = math.pi * j / (2 * count)
        out.append(re if j == 0 else re * math.cos(angle) - im * math.sin(angle))
    return out


def chunked(total, body, unrolled=False):
    if unrolled:
        for i in range(total // ROWS):
            body(i * ROWS)
        return

    def step(i, carry):
        body(pl.multiple_of(i * ROWS, ROWS))
        return carry

    lax.fori_loop(0, total // ROWS, step, 0)


def each_piece(pieces, body, group=4):
    if group == pieces:
        for m in range(pieces):
            body(m)
        return

    def step(i, carry):
        for g in range(group):
            body(i * group + g)
        return carry

    lax.fori_loop(0, pieces // group, step, 0)


def dot(a, b):
    return lax.dot_general(a, b, (((1,), (0,)), ((), ())), preferred_element_type=f32)


def places(tokens, span):
    beside = max(1, tokens // span)

    def place(index, start):
        row = start + (index // beside) * tokens
        column = (index % beside) * span
        return row, slice(column, column + span)

    tall = -(-2 // beside) * tokens
    return place, tall


def copies(*pairs):
    started = [pltpu.make_async_copy(*pair) for pair in pairs]
    for copy in started:
        copy.start()
    return started


def finish(*started):
    for copy in started:
        copy.wait()


def row_copies(source, target, sems):
    count = sems.shape[0]
    group = source.shape[0] // count
    rows = [pl.ds(g * group, group) for g in range(count)]
    return copies(*[(source.at[r], target.at[r], sems.at[g]) for g, r in enumerate(rows)])


def prep_kernel(
    pieces,
    joint,
    own_ref,
    input_hbm,
    grad_hbm,
    gate_hbm,
    taps_hbm,
    doc_ref,
    lang_ref,
    out_hbm,
    input_ref,
    grad_ref,
    gate_ref,
    made_ref,
    in_sem,
    taps_sem,
    out_sem,
):
    tokens, channels = grad_ref.shape
    groups = in_sem.shape[1]
    span = channels // pieces
    share = span // joint
    taps = share // joint
    place, tall = places(tokens, share)
    in_row, in_lanes = place(0, taps)
    grad_row, grad_lanes = place(1, taps)
    owners = [(i, d) for i in range(pieces) for d in range(joint)]

    def send(part, start, size):
        rows = pl.ds(start, size)
        return copies((made_ref.at[:, :, rows, :], out_hbm.at[:, :, rows, :], out_sem.at[part]))

    input_in = row_copies(input_hbm, input_ref, in_sem.at[2])
    grad_in = row_copies(grad_hbm, grad_ref, in_sem.at[0])
    gate_in = row_copies(gate_hbm, gate_ref, in_sem.at[1])
    taps_in = []
    for d in range(joint):
        start = pl.multiple_of(d * share + own_ref[0] * taps, ROWS)
        taps_in += copies(
            (
                taps_hbm.at[:, pl.ds(start, taps), :],
                made_ref.at[:, d, pl.ds(0, taps), :],
                taps_sem.at[d],
            )
        )
    tile = lax.broadcasted_iota(jnp.int32, (ROWS, tokens), 0)
    ids = jnp.where(tile == 0, doc_ref[...], lang_ref[...]).astype(f32).astype(bf16)
    for i, d in owners:
        made_ref[i, d, taps + tall :, :] = ids
    group = tokens // groups
    sent = []
    for g in range(groups):
        finish(input_in[g])
        rows = slice(g * group, (g + 1) * group)
        at = slice(in_row + g * group, in_row + (g + 1) * group)
        for i, d in owners:
            part = slice(i * span + d * share, i * span + (d + 1) * share)
            made_ref[i, d, at, in_lanes] = input_ref[rows, part]
    finish(*taps_in)
    sent += send(0, 0, taps if grad_row == in_row else grad_row)
    for g in range(groups):
        finish(grad_in[g], gate_in[g])
        rows = slice(g * group, (g + 1) * group)
        at = slice(grad_row + g * group, grad_row + (g + 1) * group)
        made = (grad_ref[rows, :].astype(f32) * gate_ref[rows, :].astype(f32)).astype(bf16)
        for i, d in owners:
            part = slice(i * span + d * share, i * span + (d + 1) * share)
            made_ref[i, d, at, grad_lanes] = made[:, part]
        if g == groups // 2 - 1:
            sent += send(1, grad_row, (g + 1) * group)
    start = grad_row + tokens // 2
    sent += send(2, start, taps + tall + ROWS - start)
    finish(*sent)


def token_scale(message_ref, scale_ref, dro_ref, ids, pieces, mean_len, doc_ref, lang_ref):
    joint = message_ref.shape[0] // pieces
    for o in range(message_ref.shape[0]):
        rows = message_ref[o, ids:, :].astype(f32)
        at = (o % joint) * pieces + o // joint
        doc_ref[at : at + 1, :] = rows[0:1]
        lang_ref[at : at + 1, :] = rows[1:2]
    for start in range(0, message_ref.shape[0], pieces):
        own = slice(start, start + pieces)
        docs, langs = doc_ref[own, :], lang_ref[own, :]
        doc_len = jnp.zeros_like(docs)
        for d in range(NDOCS):
            hot = (docs == float(d)).astype(f32)
            doc_len = doc_len + hot * jnp.sum(hot, axis=(0, 1), keepdims=True)
        weight = jnp.zeros_like(langs)
        for g in range(dro_ref.shape[0]):
            weight = jnp.where(langs == float(g), dro_ref[g], weight)
        scale_ref[:, own] = (weight * (2.0 * mean_len) / (doc_len + mean_len)).T


def conv_kernel(
    mean_len,
    joint,
    message_ref,
    dro_ref,
    skip_ref,
    table_ref,
    behind_ref,
    out_ref,
    cross_ref,
    scale_ref,
    both_ref,
    taps_mid_ref,
    mid_ref,
    back_ref,
    doc_ref,
    lang_ref,
):
    pieces = message_ref.shape[0] // joint
    tokens = message_ref.shape[2]
    share = skip_ref.shape[1] // 2
    taps = share // joint
    place, tall = places(tokens, share)
    width = 2 * tokens
    slab = pieces * ROWS
    pair = 2 * share

    def ahead(m):
        return table_ref[m * width : (m + 1) * width, :]

    def blocks(start, rows, count):
        parts = [slice(start + b * rows, start + (b + 1) * rows) for b in range(count)]
        return jnp.concatenate([table_ref[part, :] for part in parts], axis=1)

    start = pieces * width
    outer_blocks = slab // width
    outer_table = blocks(start, 2 * slab, outer_blocks)
    inverse_table = blocks(start + 2 * slab * outer_blocks, slab, 2 * outer_blocks)
    token_scale(message_ref, scale_ref, dro_ref, taps + tall, pieces, mean_len, doc_ref, lang_ref)

    for d in range(joint):
        for row in range(0, taps, ROWS):
            held = [message_ref[j * joint + d, row : row + ROWS, :] for j in range(pieces)]
            out = dot(outer_table, jnp.concatenate(held, axis=0)).astype(bf16)
            for m in range(pieces):
                at = 2 * m * ROWS
                for first in (d * taps + row, share + d * taps + row):
                    rows = slice(first, first + ROWS)
                    taps_mid_ref[m, rows, :tokens] = out[at : at + ROWS]
                    taps_mid_ref[m, rows, tokens:] = out[at + ROWS : at + 2 * ROWS]

    lane = lax.broadcasted_iota(jnp.int32, (ROWS, pair), 1)

    def load(o, row):
        (one, one_lanes), (two, two_lanes) = place(0, taps), place(1, taps)
        if one == two:
            return message_ref[o, pl.ds(one + row, ROWS), slice(one_lanes.start, two_lanes.stop)]
        return jnp.concatenate(
            [message_ref[o, pl.ds(first + row, ROWS), :] for first in (one, two)], axis=1
        )

    def outer(row):
        rows = pl.ds(row, ROWS)
        stack = []
        for j in range(pieces):
            line = []
            for d in range(joint):
                o = j * joint + d
                at = d * pieces + j
                factor = jnp.where(lane < share, 1.0, scale_ref[rows, at : at + 1])
                made = (load(o, row).astype(f32) * factor).astype(bf16)
                both_ref[o, rows, :] = made
                line.append(made)
            stack.append(jnp.concatenate(line, axis=1))
        out = dot(outer_table, jnp.concatenate(stack, axis=0)).astype(bf16)
        for m in range(pieces):
            at = 2 * m * ROWS
            mid_ref[m, rows, :] = out[at : at + ROWS]
            mid_ref[m, pl.ds(tokens + row, ROWS), :] = out[at + ROWS : at + 2 * ROWS]

    chunked(tokens, outer, True)
    sign = jnp.where(lax.broadcasted_iota(jnp.int32, (tokens, pair), 1) < share, 1.0, -1.0)

    def inner(m):
        filt = lax.dot_general(
            ahead(m), taps_mid_ref[m], (((1,), (1,)), ((), ())), preferred_element_type=f32
        )
        spec = dot(ahead(m), mid_ref[m])
        fre, fim = filt[:tokens], filt[tokens:] * sign
        cre, cim, prods = 0.0, 0.0, []
        for d in range(joint):
            part = slice(d * pair, (d + 1) * pair)
            re, im = spec[:tokens, part], spec[tokens:, part]
            xre, gre, xim, gim = re[:, :share], re[:, share:], im[:, :share], im[:, share:]
            cre, cim = cre + (xre * gre + xim * gim), cim + (xre * gim - xim * gre)
            prods.append(jnp.concatenate([fre * re - fim * im, fre * im + fim * re], axis=0))
        cross_ref[m, :tokens, :] = cre.astype(bf16)
        cross_ref[m, tokens:, :] = cim.astype(bf16)
        prods = jnp.concatenate([prod.astype(bf16) for prod in prods], axis=1)
        back_ref[m] = dot(behind_ref[m], prods).astype(bf16)

    each_piece(pieces, inner, pieces)
    skip = skip_ref[...]

    def outer_back(row):
        rows = pl.ds(row, ROWS)
        stack = []
        for m in range(pieces):
            stack += [back_ref[m, rows, :], back_ref[m, pl.ds(tokens + row, ROWS), :]]
        out = dot(inverse_table, jnp.concatenate(stack, axis=0))
        (one, one_lanes), (two, two_lanes) = place(0, 0), place(1, 0)
        for j in range(pieces):
            for d in range(joint):
                o = j * joint + d
                value = out[j * ROWS : (j + 1) * ROWS, d * pair : (d + 1) * pair]
                value = (value + skip * both_ref[o, rows, :].astype(f32)).astype(bf16)
                if one == two:
                    out_ref[o, rows, slice(one_lanes.start, two_lanes.stop)] = value
                else:
                    out_ref[o, rows, :] = value[:, :share]
                    out_ref[o, pl.ds(two + row, ROWS), :] = value[:, share:]

    chunked(tokens, outer_back, True)


def lags_kernel(own_ref, cross_ref, behind_ref, keep_ref, send_ref, back_ref, lag_ref):
    pieces, tall, span = cross_ref.shape
    tokens = tall // 2
    held = keep_ref.shape[1] // tokens
    members = pieces // held

    def inner(m):
        back_ref[m] = dot(behind_ref[m], cross_ref[m])

    each_piece(pieces, inner)

    def body(row):
        out = outer_inverse(
            [
                (back_ref[m, pl.ds(row, ROWS), :], back_ref[m, pl.ds(tokens + row, ROWS), :])
                for m in range(pieces)
            ]
        )
        for j in range(pieces):
            lag_ref[j, pl.ds(row, ROWS), :] = out[j]

    chunked(tokens, body)
    for j in range(held):
        part = slice(j * tokens, (j + 1) * tokens)
        keep_ref[:, part] = lag_ref[own_ref[0] * held + j].T
        for r in range(1, members):
            other = lax.rem(own_ref[0] + r, members)
            send_ref[r - 1, :, part] = lag_ref[other * held + j].T.astype(bf16)


def scaled_kernel(own_ref, grad_ref, scale_ref, out_ref):
    lane = lax.broadcasted_iota(jnp.int32, scale_ref.shape, 1)
    scale = jnp.where(lane == own_ref[0], scale_ref[...], jnp.zeros(scale_ref.shape, f32))
    out_ref[...] = grad_ref[...].astype(f32) * jnp.sum(scale, axis=1, keepdims=True)


def final_kernel(joint, scaled_ref, message_ref, gate_ref, input_ref):
    pieces = message_ref.shape[0] // joint
    tokens, channels = scaled_ref.shape
    span = channels // pieces
    share = span // joint
    place, _ = places(tokens, share)
    mixed_row, mixed_lanes = place(0, 0)
    back_row, back_lanes = place(1, 0)
    for i in range(pieces):
        owners = [i * joint + d for d in range(joint)]
        mixed = [message_ref[o, mixed_row : mixed_row + tokens, mixed_lanes] for o in owners]
        back = [message_ref[o, back_row : back_row + tokens, back_lanes] for o in owners]
        part = slice(i * span, (i + 1) * span)
        mixed = jnp.concatenate(mixed, axis=1).astype(f32)
        gate_ref[:, part] = (scaled_ref[:, part] * mixed).astype(bf16)
        input_ref[:, part] = jnp.concatenate(back, axis=1)


def call(kernel, out, ins, scratch=(), outs=None, room=40 << 20, cost=(0, 0)):
    return pl.pallas_call(
        kernel,
        out_shape=out,
        in_specs=ins,
        out_specs=jax.tree.map(lambda _: VMEM, out) if outs is None else outs,
        scratch_shapes=scratch,
        compiler_params=pltpu.CompilerParams(vmem_limit_bytes=(64 << 20) - room),
        cost_estimate=pl.CostEstimate(flops=cost[0], bytes_accessed=cost[1], transcendentals=0),
    )


def local(grad_out, saved_input, gate_value, filter_taps, skip_gain, lang_ids, doc_ids, dro_weight):
    tokens = grad_out.shape[1]
    channels = grad_out.shape[2]
    pieces = lax.axis_size("ctx")
    members = lax.axis_size("dp")
    length = tokens * pieces
    span = channels // pieces
    mean_len = length / NDOCS
    tables, behind = all_tables(pieces, tokens)
    share = span // members
    joint = members if share * 2 % 128 == 0 and share // members % ROWS == 0 else 1
    if joint == 1:
        share = span
    taps = share // joint
    axes = ("ctx", "dp") if joint > 1 else "ctx"
    place = lax.axis_index("ctx")
    member = lax.axis_index("dp")
    first = place * span + (member * share if joint > 1 else 0)
    own = (place + member * pieces if joint > 1 else place).reshape(1)
    skip = lax.dynamic_slice_in_dim(skip_gain, first, share)
    skip = jnp.concatenate([skip, skip])[None, :]
    exchange = functools.partial(
        lax.all_to_all, axis_name=axes, split_axis=0, concat_axis=0, tiled=True
    )
    shape = jax.ShapeDtypeStruct
    dma = pltpu.SemaphoreType.DMA
    tall = places(tokens, share)[1]
    macs = pieces * (2 * tokens) ** 2 * span
    count = joint * pieces
    message = shape((pieces, joint, taps + tall + ROWS, tokens), bf16)
    answer = shape((count, tall, tokens), bf16)
    groups = 4

    sent = call(
        functools.partial(prep_kernel, pieces, joint),
        message,
        [SMEM] + [HBM] * 4 + [VMEM] * 2,
        [
            pltpu.VMEM((tokens, channels), bf16),
            pltpu.VMEM((tokens, channels), bf16),
            pltpu.VMEM((tokens, channels), bf16),
            pltpu.VMEM(message.shape, bf16),
            dma((3, groups)),
            dma((joint,)),
            dma((3,)),
        ],
        outs=HBM,
        room=256 << 10,
        cost=(0, 4 << 20),
    )(
        (member if joint > 1 else jnp.zeros_like(member)).reshape(1),
        saved_input[0],
        grad_out[0],
        gate_value[0],
        filter_taps.reshape(pieces, span, tokens),
        doc_ids,
        lang_ids,
    )
    sent, cross, scale = call(
        functools.partial(conv_kernel, mean_len, joint),
        [answer, shape((pieces, 2 * tokens, share), bf16), shape((tokens, count), f32)],
        [VMEM, SMEM, VMEM, VMEM, VMEM],
        [
            pltpu.VMEM((count, tokens, 2 * share), bf16),
            pltpu.VMEM((pieces, 2 * share, 2 * tokens), bf16),
            pltpu.VMEM((pieces, 2 * tokens, 2 * share * joint), bf16),
            pltpu.VMEM((pieces, 2 * tokens, 2 * share * joint), bf16),
            pltpu.VMEM((count, tokens), f32),
            pltpu.VMEM((count, tokens), f32),
        ],
        room=(10 << 20) if span % 128 == 0 else (20 << 20),
        cost=(10 * macs, 8 << 20),
    )(exchange(sent.reshape(count, -1, tokens)), dro_weight, skip, tables, behind)
    got = exchange(sent)
    keep, send = call(
        lags_kernel,
        (
            shape((share, length // members), f32),
            shape((members - 1, share, length // members), bf16),
        ),
        [SMEM, VMEM, VMEM],
        [
            pltpu.VMEM((pieces, 2 * tokens, share), f32),
            pltpu.VMEM((pieces, tokens, share), f32),
        ],
        cost=(2 * macs, 6 << 20),
    )(member.reshape(1), cross, behind)
    rings = [[(d, (d + r) % members) for d in range(members)] for r in range(members)]
    came = [lax.ppermute(send[r - 1], "dp", rings[r]).astype(f32) for r in range(1, members)]
    if joint > 1:
        came = jnp.stack([keep] + came)
        d_filter = jnp.concatenate(
            [
                lax.dynamic_index_in_dim(came, (member - d) % members, 0, keepdims=False)
                for d in range(members)
            ]
        )
    else:
        d_filter = sum(came, keep)
    token_block = jax.ShapeDtypeStruct((tokens, channels), bf16)
    scaled = call(
        scaled_kernel,
        shape((tokens, channels), f32),
        [SMEM, VMEM, VMEM],
        cost=(0, 2 << 20),
    )(own, grad_out[0], scale)
    d_gate, d_input = call(
        functools.partial(final_kernel, joint),
        (token_block, token_block),
        [VMEM, VMEM],
        cost=(0, 4 << 20),
    )(scaled, got)
    return (d_input[None], d_gate[None], d_filter)


def solution(mesh):
    return jax.shard_map(
        local,
        mesh=mesh,
        in_specs=(
            P("dp", "ctx", None),
            P("dp", "ctx", None),
            P("dp", "ctx", None),
            P(None, "ctx"),
            P(),
            P("dp", "ctx"),
            P("dp", "ctx"),
            P(),
        ),
        out_specs=(P("dp", "ctx", None), P("dp", "ctx", None), P("ctx", "dp")),
        check_vma=False,
    )
```
